32 devices in a mesh: groups: 2 (over y), ctx: 4 (over z), exp: 4 (over x, core).
Axes of the slice: x: 2, y: 2, z: 4, core: 2. Of those that a mesh axis runs over, the one named last changes fastest.
Arguments:
- resid: bfloat16 [1024, 2048], P(('groups', 'ctx', 'exp')), parts along dimension 0, may hold values from -36 to 36
- query: bfloat16 [1024, 4096], P(('groups', 'ctx'), 'exp'), parts along dimension 0, may hold values from -144 to 144
- key: bfloat16 [1024, 512], P(('groups', 'ctx'), 'exp'), parts along dimension 0, may hold values from -6 to 6
- value: bfloat16 [1024, 512], P(('groups', 'ctx'), 'exp'), parts along dimension 0, may hold values from -6 to 6
- out_proj: bfloat16 [4096, 2048], P('exp', 'ctx'), may hold values from -0.5 to 0.5
- norm_gain: float32 [2048], replicated, may hold values from 0.25 to 1.75
- w_gate: bfloat16 [16, 2048, 384], P(('ctx', 'exp')), may hold values from -0.125 to 0.125
- w_up: bfloat16 [16, 2048, 384], P(('ctx', 'exp')), may hold values from -0.125 to 0.125
- w_down: bfloat16 [16, 384, 2048], P(('ctx', 'exp')), may hold values from -0.3125 to 0.3125
- routes: int32 [1024, 8], P(('groups', 'ctx', 'exp')), parts along dimension 0, may hold values from 0 to 15, all different within a row; in each aligned block of 32 rows (0 to 31, 32 to 63, ...) at most 32 rows name the same one
- gate_weights: float32 [1024, 8], P(('groups', 'ctx', 'exp')), parts along dimension 0, may hold values from 0.05 to 0.25
- grad_out: bfloat16 [1024, 2048], P(('groups', 'ctx', 'exp')), parts along dimension 0, may hold values from -6 to 6
Outputs:
- layer_out: bfloat16 [1024, 2048], P(('groups', 'ctx', 'exp')), parts along dimension 0
- grad_resid: bfloat16 [1024, 2048], P(('groups', 'ctx', 'exp')), parts along dimension 0
- grad_query: bfloat16 [1024, 4096], P(('groups', 'ctx'), 'exp'), parts along dimension 0
- key_gradient: bfloat16 [1024, 512], P(('groups', 'ctx'), 'exp'), parts along dimension 0
- value_gradient: bfloat16 [1024, 512], P(('groups', 'ctx'), 'exp'), parts along dimension 0
- grad_out_proj: bfloat16 [8192, 2048], P(('groups', 'exp'), 'ctx'), parts along dimension 0
- grad_gain: float32 [4096], P('groups'), parts along dimension 0
- grad_w_gate: bfloat16 [32, 2048, 384], P(('groups', 'ctx', 'exp')), parts along dimension 0
- grad_w_up: bfloat16 [32, 2048, 384], P(('groups', 'ctx', 'exp')), parts along dimension 0
- grad_w_down: bfloat16 [32, 384, 2048], P(('groups', 'ctx', 'exp')), parts along dimension 0
The draws below stay inside these ranges and needn't reach their ends.
There are 2 independent parts, one for each index of `groups`. The reference program is written for one: setup_inputs(seed, part) draws one part's arguments, and reference() takes and returns one part's arrays. A program takes and returns all parts, laid end to end along the dimension named above; an argument that names none is the same for every part. Nothing has to cross between parts.
Inputs may be any that keep to these rules, and one draw needn't show every extreme that they name: `routes`: each token names 8 different experts. Among the 32 tokens of one device no expert is named more than 32 times, a bound that some block reaches.
All inputs are finite; a program needn't handle non-finite values.
Results may differ from the reference program's by a relative error of at most 0.018.
Values may be sent and summed in bfloat16 or wider, within the bound.
No kernel may reach another device: no remote copies, remote signals or barrier semaphores. Data moves between devices by JAX's collectives and lax.ppermute only.
A program may use at most 128 MiB of HBM per device.

```python
import math
import jax
import jax.numpy as jnp
import numpy as np
from jax import lax

D = 2048
QUERY_HEADS = 32
KEY_VALUE_HEADS = 4
HEAD_SIZE = 128
TOPK = 8
FW = 384
SEQ_DEV = 128
TOK_DEV = 32
SEQUENCE_LENGTH = 512
EXPERTS = 16
CAP = 32


def shared_keys(key):
    unscaled_keys = jax.random.normal(key, (SEQUENCE_LENGTH, KEY_VALUE_HEADS * HEAD_SIZE), jnp.float32)
    return jnp.clip(unscaled_keys, -6.0, 6.0)


def drawn_queries(key):
    raw_vals = jnp.clip(jax.random.normal(key, (SEQUENCE_LENGTH, QUERY_HEADS * HEAD_SIZE), jnp.float32), -6.0, 6.0)
    return raw_vals


def draw_key(key, part):
    return shared_keys(key).astype(jnp.bfloat16)


def draw_query(key, part):
    key = jax.random.fold_in(key, 7)
    return drawn_queries(key).astype(jnp.bfloat16)


def draw_resid(key, part):
    key = jax.random.fold_in(key, 3)
    key_core, key_rows, key_cols = jax.random.split(key, 3)
    core_vals = jnp.clip(jax.random.normal(key_core, (SEQUENCE_LENGTH, D), jnp.float32), -4.0, 4.0)
    row_scale = jnp.exp(jax.random.uniform(key_rows, (SEQUENCE_LENGTH, 1), jnp.float32, math.log(0.3), math.log(3.0)))
    col_scale = jnp.exp(jax.random.uniform(key_cols, (1, D), jnp.float32, math.log(0.3), math.log(3.0)))
    return (core_vals * row_scale * col_scale).astype(jnp.bfloat16)


def level_of(stream_key, dims, pieces, smallest, top_value):
    level, own = 1.0, jax.random.fold_in(stream_key, 6)
    for dim, shards_of in pieces:
        steps = jnp.exp(jax.random.uniform(jax.random.fold_in(own, dim), (shards_of,), jnp.float32, smallest / len(pieces), top_value / len(pieces)))
        level = level * jnp.repeat(steps, dims[dim] // shards_of).reshape([-1 if axis == dim else 1 for axis in range(len(dims))])
    return level


def shared_out(rng, own, number, rows, amount, top, bound, skew):
    order = jax.random.permutation(rng, amount)
    crowded, ordinary = load_shares(amount, rows * top, bound, skew, True), load_shares(amount, rows * top, bound, skew, False)
    places = jnp.arange(amount)

    def named(tallies, turn):
        used = int((tallies > 0).sum())
        fixed = max(1, used // 4)
        moved = fixed + (places - fixed + turn * (used - fixed)) % max(1, amount - fixed)
        return jnp.zeros((amount,), jnp.int32).at[order[jnp.where(places < fixed, places, moved)]].set(jnp.asarray(tallies, jnp.int32))

    tallies = jnp.where(number % 4 == 0, named(crowded, number // 4), named(ordinary, number - number // 4 - 1))
    mixed = jax.random.permutation(jax.random.fold_in(own, 3), amount)
    source_of, taker = mixed[0:amount // 2 * 2:2], mixed[1:amount // 2 * 2:2]
    margin = jnp.minimum(tallies[source_of] - 1, bound - tallies[taker]) // 2
    margin = jnp.where((source_of == order[0]) | (taker == order[0]) | (tallies[taker] == 0), 0, jnp.maximum(margin, 0))
    moved = jax.random.randint(jax.random.fold_in(own, 4), (amount // 2,), 0, 1 << 20) % (margin + 1)
    tallies = tallies.at[source_of].add(-moved).at[taker].add(moved)
    members = jnp.searchsorted(jnp.cumsum(tallies), jnp.arange(rows * top), side="right").astype(jnp.int32)
    table = members.reshape(top, rows).T
    table = table[jax.random.permutation(jax.random.fold_in(own, 1), rows)]
    turn = jax.random.randint(jax.random.fold_in(own, 2), (rows, 1), 0, top)
    return jnp.take_along_axis(table, (jnp.arange(top)[None, :] + turn) % top, axis=1)


def load_shares(count, total, most, skew, full):
    portions = [(1 << 20) // math.isqrt(standing ** skew) + 1 for standing in range(1, count + 1)]
    largest = most if full else min(most, max(-(-total // count), total * portions[0] // sum(portions)))
    least = 1 if total - largest >= count - 1 else 0
    counts, spare = [largest] + [least] * (count - 1), total - largest - least * (count - 1)
    while spare > 0:
        candidates = [i for i in range(1, count) if counts[i] < largest] or [i for i in range(1, count) if counts[i] < most]
        pool, left = sum([portions[i] for i in candidates]), spare
        for i in candidates:
            more = min(most - counts[i], max(1, left * portions[i] // pool), spare)
            counts[i] = counts[i] + more
            spare = spare - more
    return np.array(counts)


def gaussian(rng, extent, spread, most, pieces=(), kind=jnp.bfloat16):
    array = jax.random.normal(rng, extent, jnp.float32) * spread
    if len(pieces) > 0:
        array = level_of(rng, extent, pieces, -0.22, 0.18) * array
    return jnp.clip(array, min=-most, max=most).astype(kind)


def setup_inputs(seed: int = 0, part: int = 0) -> dict:
    streams_of = jax.random.split(jax.random.key(seed), 13)
    part_splits = jax.random.split(jax.random.fold_in(streams_of[12], part), 13)
    resid = draw_resid(jax.random.fold_in(jax.random.fold_in(streams_of[12], part), 71), part)
    query = draw_query(jax.random.fold_in(jax.random.fold_in(streams_of[12], part), 71), part)
    key = draw_key(jax.random.fold_in(jax.random.fold_in(streams_of[12], part), 71), part)
    value = gaussian(part_splits[3], (SEQUENCE_LENGTH, KEY_VALUE_HEADS * HEAD_SIZE), 1.0, 6.0, ((0, 4), (1, 4)))
    out_proj = gaussian(streams_of[4], (QUERY_HEADS * HEAD_SIZE, D), HEAD_SIZE ** -0.5, 0.5, ((0, 4), (1, 4)))
    norm_gain = jnp.clip(1.0 + 0.15 * jax.random.normal(streams_of[5], (D,), jnp.float32), 0.25, 1.75)
    w_gate = gaussian(streams_of[6], (EXPERTS, D, FW), D ** -0.5, 0.125, ((0, 16),))
    w_up = gaussian(streams_of[7], (EXPERTS, D, FW), D ** -0.5, 0.125, ((0, 16),))
    w_down = gaussian(streams_of[8], (EXPERTS, FW, D), FW ** -0.5, 0.3125, ((0, 16),))
    routes_keys = jax.random.split(jax.random.fold_in(part_splits[9], 1), SEQUENCE_LENGTH // TOK_DEV)
    routes_turns = jax.random.permutation(jax.random.fold_in(part_splits[9], 3), SEQUENCE_LENGTH // TOK_DEV)
    routes = jax.vmap(lambda own, number: shared_out(jax.random.fold_in(part_splits[9], 2), own, number, TOK_DEV, EXPERTS, TOPK, CAP, 2))(routes_keys, routes_turns).reshape((SEQUENCE_LENGTH, TOPK))
    gate_weights = jnp.clip(0.05 + 0.2 * jax.random.uniform(part_splits[10], (SEQUENCE_LENGTH, TOPK), jnp.float32) ** level_of(part_splits[10], (SEQUENCE_LENGTH, TOPK), ((0, 16),), -0.2, 0.2), 0.05, 0.25)
    grad_out = gaussian(part_splits[11], (SEQUENCE_LENGTH, D), 1.0, 6.0, ((0, 16),))
    return dict(resid=resid, query=query, key=key, value=value, out_proj=out_proj, norm_gain=norm_gain, w_gate=w_gate, w_up=w_up, w_down=w_down, routes=routes, gate_weights=gate_weights, grad_out=grad_out)


EPS = 1e-06
NEG = -1e+30

def round_half(values):
    return lax.optimization_barrier(values.astype(jnp.bfloat16)).astype(jnp.float32)

def masked_scores(query_blk, keys_float, row_start):
    scores = jnp.einsum('bngd,snd->bngs', query_blk, keys_float) * HEAD_SIZE ** (-0.5)
    query_pos = row_start + jnp.arange(SEQ_DEV, dtype=jnp.int32)
    key_pos = jnp.arange(SEQUENCE_LENGTH, dtype=jnp.int32)
    visible = key_pos[None, :] <= query_pos[:, None]
    return (visible[:, None, None, :], scores)

def reference(resid, query, key, value, out_proj, norm_gain, w_gate, w_up, w_down, routes, gate_weights, grad_out):
    group_width = QUERY_HEADS // KEY_VALUE_HEADS
    score_scale = HEAD_SIZE ** (-0.5)
    query_quad = query.reshape(SEQUENCE_LENGTH, KEY_VALUE_HEADS, group_width, HEAD_SIZE)
    keys_float = key.reshape(SEQUENCE_LENGTH, KEY_VALUE_HEADS, HEAD_SIZE).astype(jnp.float32)
    values_float = value.reshape(SEQUENCE_LENGTH, KEY_VALUE_HEADS, HEAD_SIZE).astype(jnp.float32)
    block_ids = jnp.arange(SEQUENCE_LENGTH // SEQ_DEV, dtype=jnp.int32)

    def forward_block(block_id):
        row_start = block_id * SEQ_DEV
        query_blk = lax.dynamic_slice_in_dim(query_quad, row_start, SEQ_DEV, 0).astype(jnp.float32)
        visible, scores = masked_scores(query_blk, keys_float, row_start)
        scores = jnp.where(visible, scores, NEG)
        peak_val = lax.optimization_barrier(jnp.max(scores, -1))
        weights = jnp.exp(scores - peak_val[..., None])
        total_val = lax.optimization_barrier(jnp.sum(weights, -1))
        mixed_rows = jnp.einsum('bngs,snd->bngd', round_half(weights), values_float)
        attn_block = (mixed_rows / total_val[..., None]).astype(jnp.bfloat16)
        return (attn_block, peak_val + jnp.log(total_val))
    attention_quad, log_sum_total = lax.map(forward_block, block_ids)
    attention_quad = attention_quad.reshape(SEQUENCE_LENGTH, KEY_VALUE_HEADS, group_width, HEAD_SIZE)
    log_sum_total = log_sum_total.reshape(SEQUENCE_LENGTH, KEY_VALUE_HEADS, group_width)
    attn_mix = attention_quad.reshape(SEQUENCE_LENGTH, QUERY_HEADS * HEAD_SIZE)
    hidden = (resid.astype(jnp.float32) + jnp.dot(attn_mix, out_proj, preferred_element_type=jnp.float32)).astype(jnp.bfloat16)
    hidden_f = hidden.astype(jnp.float32)
    inv_rms = lax.rsqrt(lax.optimization_barrier(jnp.mean(hidden_f * hidden_f, -1, keepdims=True)) + EPS)
    unit_rows = hidden_f * inv_rms
    normed = (unit_rows * norm_gain).astype(jnp.bfloat16)
    device_count = SEQUENCE_LENGTH // TOK_DEV
    flat_routes = routes.reshape(device_count, TOK_DEV * TOPK)
    member = (flat_routes[:, :, None] == jnp.arange(EXPERTS, dtype=jnp.int32)[None, None, :]).astype(jnp.int32)
    slot_pos = lax.optimization_barrier(jnp.sum(jnp.cumsum(member, 1) * member, 2)) - 1
    column = jnp.arange(device_count, dtype=jnp.int32)[:, None] * CAP + slot_pos
    token_ids = jnp.arange(device_count, dtype=jnp.int32)[:, None] * TOK_DEV + jnp.arange(TOK_DEV * TOPK, dtype=jnp.int32)[None, :] // TOPK
    table = jnp.full((EXPERTS, device_count * CAP), SEQUENCE_LENGTH, jnp.int32).at[flat_routes, column].set(token_ids)
    gate_table = jnp.zeros((EXPERTS, device_count * CAP), jnp.float32).at[flat_routes, column].set(gate_weights.reshape(device_count, TOK_DEV * TOPK))
    normed_pad = jnp.concatenate([normed, jnp.zeros((1, D), jnp.bfloat16)], 0)
    grad_pad = jnp.concatenate([grad_out, jnp.zeros((1, D), jnp.bfloat16)], 0)

    def expert_block(loop_carry, expert):
        moe_acc, normed_acc = loop_carry
        index_row = table[expert]
        gate_row = gate_table[expert]
        rows_in = normed_pad[index_row]
        pre_gate = jnp.dot(rows_in, w_gate[expert], preferred_element_type=jnp.float32)
        pre_up = jnp.dot(rows_in, w_up[expert], preferred_element_type=jnp.float32)
        sig_gate = jax.nn.sigmoid(pre_gate)
        act_rows = (pre_gate * sig_gate * pre_up).astype(jnp.bfloat16)
        out_rows = jnp.dot(act_rows, w_down[expert], preferred_element_type=jnp.float32).astype(jnp.bfloat16)
        moe_acc = moe_acc.at[index_row].add(out_rows.astype(jnp.float32) * gate_row[:, None])
        grad_rows = (grad_pad[index_row].astype(jnp.float32) * gate_row[:, None]).astype(jnp.bfloat16)
        act_grad = jnp.dot(grad_rows, w_down[expert].T, preferred_element_type=jnp.float32)
        down_grad = jnp.dot(act_rows.T, grad_rows, preferred_element_type=jnp.float32).astype(jnp.bfloat16)
        up_grad = (act_grad * pre_gate * sig_gate).astype(jnp.bfloat16)
        gate_grad = (act_grad * pre_up * sig_gate * (1.0 + pre_gate * (1.0 - sig_gate))).astype(jnp.bfloat16)
        gate_wgrad = jnp.dot(rows_in.T, gate_grad, preferred_element_type=jnp.float32).astype(jnp.bfloat16)
        up_wgrad = jnp.dot(rows_in.T, up_grad, preferred_element_type=jnp.float32).astype(jnp.bfloat16)
        row_grad = (jnp.dot(gate_grad, w_gate[expert].T, preferred_element_type=jnp.float32) + jnp.dot(up_grad, w_up[expert].T, preferred_element_type=jnp.float32)).astype(jnp.bfloat16)
        normed_acc = normed_acc.at[index_row].add(row_grad.astype(jnp.float32))
        return ((moe_acc, normed_acc), (gate_wgrad, up_wgrad, down_grad))
    start_acc = (jnp.zeros((SEQUENCE_LENGTH + 1, D), jnp.float32), jnp.zeros((SEQUENCE_LENGTH + 1, D), jnp.float32))
    (moe_acc, normed_acc), (grad_w_gate, grad_w_up, grad_w_down) = lax.scan(expert_block, start_acc, jnp.arange(EXPERTS, dtype=jnp.int32))
    layer_out = (hidden_f + moe_acc[:SEQUENCE_LENGTH]).astype(jnp.bfloat16)
    normed_grad = normed_acc[:SEQUENCE_LENGTH]
    grad_gain = lax.optimization_barrier(jnp.sum(normed_grad * unit_rows, 0))
    scaled_grad = norm_gain * normed_grad
    hidden_grad = inv_rms * (scaled_grad - unit_rows * lax.optimization_barrier(jnp.mean(scaled_grad * unit_rows, -1, keepdims=True)))
    grad_resid = (grad_out.astype(jnp.float32) + hidden_grad).astype(jnp.bfloat16)
    attn_blocks = attn_mix.reshape(SEQUENCE_LENGTH // SEQ_DEV, SEQ_DEV, QUERY_HEADS * HEAD_SIZE)
    resid_blocks = grad_resid.reshape(SEQUENCE_LENGTH // SEQ_DEV, SEQ_DEV, D)

    def proj_block(proj_acc, pair_rows):
        part_sum = jnp.dot(pair_rows[0].T, pair_rows[1], preferred_element_type=jnp.float32)
        return (proj_acc + round_half(part_sum), 0)
    proj_acc, unused = lax.scan(proj_block, jnp.zeros((QUERY_HEADS * HEAD_SIZE, D), jnp.float32), (attn_blocks, resid_blocks))
    grad_out_proj = proj_acc.astype(jnp.bfloat16)
    mixture_gradient = jnp.dot(grad_resid, out_proj.T, preferred_element_type=jnp.float32).astype(jnp.bfloat16)
    mixture_quad = mixture_gradient.reshape(SEQUENCE_LENGTH, KEY_VALUE_HEADS, group_width, HEAD_SIZE)

    def backward_block(loop_carry, block_id):
        key_running_total, value_running_total = loop_carry
        row_start = block_id * SEQ_DEV
        query_blk = lax.dynamic_slice_in_dim(query_quad, row_start, SEQ_DEV, 0).astype(jnp.float32)
        mix_blk = lax.dynamic_slice_in_dim(mixture_quad, row_start, SEQ_DEV, 0).astype(jnp.float32)
        attn_blk = lax.dynamic_slice_in_dim(attention_quad, row_start, SEQ_DEV, 0).astype(jnp.float32)
        lse_blk = lax.dynamic_slice_in_dim(log_sum_total, row_start, SEQ_DEV, 0)
        visible, scores = masked_scores(query_blk, keys_float, row_start)
        prob_full = jnp.where(visible, jnp.exp(scores - lse_blk[..., None]), 0.0)
        prob_grad = jnp.einsum('bngd,snd->bngs', mix_blk, values_float)
        delta_sum = lax.optimization_barrier(jnp.sum(mix_blk * attn_blk, -1))
        score_grad = prob_full * (prob_grad - delta_sum[..., None])
        score_half = round_half(score_grad)
        query_grad = (jnp.einsum('bngs,snd->bngd', score_half, keys_float) * score_scale).astype(jnp.bfloat16)
        key_part = jnp.einsum('bngs,bngd->snd', score_half, query_blk) * score_scale
        value_part = jnp.einsum('bngs,bngd->snd', round_half(prob_full), mix_blk)
        return ((key_running_total + round_half(key_part), value_running_total + round_half(value_part)), query_grad)
    key_value_begin = (jnp.zeros((SEQUENCE_LENGTH, KEY_VALUE_HEADS, HEAD_SIZE), jnp.float32), jnp.zeros((SEQUENCE_LENGTH, KEY_VALUE_HEADS, HEAD_SIZE), jnp.float32))
    (key_running_total, value_running_total), grad_query = lax.scan(backward_block, key_value_begin, block_ids)
    grad_query = grad_query.reshape(SEQUENCE_LENGTH, QUERY_HEADS * HEAD_SIZE)
    key_gradient = key_running_total.reshape(SEQUENCE_LENGTH, KEY_VALUE_HEADS * HEAD_SIZE).astype(jnp.bfloat16)
    value_gradient = value_running_total.reshape(SEQUENCE_LENGTH, KEY_VALUE_HEADS * HEAD_SIZE).astype(jnp.bfloat16)
    return (layer_out, grad_resid, grad_query, key_gradient, value_gradient, grad_out_proj, grad_gain, grad_w_gate, grad_w_up, grad_w_down)
```

```python
import jax
import jax.numpy as jnp
from jax import lax
from jax.experimental import pallas as pl
from jax.experimental.pallas import tpu as pltpu
from jax.sharding import PartitionSpec as P

HEAD_SIZE = 128


EPS = 1e-06
NEG = -1e30


def attend_block(soft_state, queries, key_rows, val_rows, row_begin, query_pos, score_scale):
    peak_run, total_run, accum_rows = soft_state
    scores = (
        jnp.einsum("bngd,knd->bngk", queries, key_rows, preferred_element_type=jnp.float32)
        * score_scale
    )
    key_pos = row_begin + jnp.arange(key_rows.shape[0], dtype=jnp.int32)
    visible = key_pos[None, :] <= query_pos[:, None]
    scores = jnp.where(visible[:, None, None, :], scores, NEG)
    peak_new = jnp.maximum(peak_run, jnp.max(scores, -1))
    rescale = jnp.exp(peak_run - peak_new)
    weights = jnp.exp(scores - peak_new[..., None])
    total_new = total_run * rescale + jnp.sum(weights, -1)
    mixed_rows = jnp.einsum(
        "bngk,knd->bngd", weights.astype(jnp.bfloat16), val_rows, preferred_element_type=jnp.float32
    )
    return (peak_new, total_new, accum_rows * rescale[..., None] + mixed_rows)


def expert_trade(buffer):
    return lax.all_to_all(buffer, ("ctx", "exp"), split_axis=0, concat_axis=0, tiled=True)


def local_routed(
    resid,
    query,
    key,
    value,
    out_proj,
    norm_gain,
    w_gate,
    w_up,
    w_down,
    routes,
    gate_weights,
    grad_out,
):
    ctx_count = lax.axis_size("ctx")
    exp_count = lax.axis_size("exp")
    ctx_index = lax.axis_index("ctx")
    seq_rows = query.shape[0]
    kv_heads = key.shape[1] // HEAD_SIZE
    group_width = query.shape[1] // HEAD_SIZE // kv_heads
    seq_total = seq_rows * ctx_count
    score_scale = HEAD_SIZE ** (-0.5)
    query_start = ctx_index * seq_rows
    query_pos = query_start + jnp.arange(seq_rows, dtype=jnp.int32)
    queries = query.reshape(seq_rows, kv_heads, group_width, HEAD_SIZE)
    state_shape = (seq_rows, kv_heads, group_width)
    start_state = (
        jnp.full(state_shape, NEG, jnp.float32),
        jnp.zeros(state_shape, jnp.float32),
        jnp.zeros(state_shape + (HEAD_SIZE,), jnp.float32),
    )
    block_len = min(512, seq_total)
    keys_flat, values_flat = (
        lax.all_gather(key, "ctx", axis=0, tiled=True),
        lax.all_gather(value, "ctx", axis=0, tiled=True),
    )
    keys_all = keys_flat.reshape(seq_total, kv_heads, HEAD_SIZE)
    values_all = values_flat.reshape(seq_total, kv_heads, HEAD_SIZE)
    block_count = (query_start + seq_rows + block_len - 1) // block_len

    def forward_turn(loop_turn, soft_state):
        row_begin = loop_turn * block_len
        key_rows = lax.dynamic_slice_in_dim(keys_all, row_begin, block_len, 0)
        val_rows = lax.dynamic_slice_in_dim(values_all, row_begin, block_len, 0)
        return attend_block(
            soft_state, queries, key_rows, val_rows, row_begin, query_pos, score_scale
        )

    soft_state = lax.fori_loop(0, block_count, forward_turn, start_state)
    peak_val, total_val, accum_rows = soft_state
    attention_quad = (accum_rows / total_val[..., None]).astype(jnp.bfloat16)
    attn_mix = attention_quad.reshape(seq_rows, kv_heads * group_width * HEAD_SIZE)
    log_sum_total = peak_val + jnp.log(total_val)
    proj_full = lax.all_gather(out_proj, "ctx", axis=1, tiled=True)
    tok_rows = resid.shape[0]
    proj_sum = lax.psum_scatter(
        jnp.dot(attn_mix, proj_full, preferred_element_type=jnp.float32).astype(jnp.bfloat16),
        "exp",
        scatter_dimension=0,
        tiled=True,
    ).astype(jnp.float32)
    hidden = (resid.astype(jnp.float32) + proj_sum).astype(jnp.bfloat16)
    hidden_f = hidden.astype(jnp.float32)
    inv_rms = lax.rsqrt(jnp.mean(hidden_f * hidden_f, -1, keepdims=True) + EPS)
    unit_rows = hidden_f * inv_rms
    normed = (unit_rows * norm_gain).astype(jnp.bfloat16)
    top_count = routes.shape[1]
    model_width = normed.shape[1]
    experts_local = w_gate.shape[0]
    device_count = ctx_count * exp_count
    expert_total = experts_local * device_count
    capacity = 2 * tok_rows * top_count // expert_total
    flat_routes = routes.reshape(-1)
    member = (flat_routes[:, None] == jnp.arange(expert_total, dtype=jnp.int32)[None, :]).astype(
        jnp.int32
    )
    slot_pos = jnp.sum(jnp.cumsum(member, 0) * member, 1) - 1
    dest_row = flat_routes * capacity + slot_pos
    pair_weights = gate_weights.reshape(-1)

    def place_rows(rows_out):
        return (
            jnp.zeros((expert_total * capacity, model_width), jnp.bfloat16)
            .at[dest_row]
            .set(rows_out)
        )

    def to_experts(buffer):
        return (
            buffer.reshape(device_count, experts_local, capacity, model_width)
            .transpose(1, 0, 2, 3)
            .reshape(experts_local, device_count * capacity, model_width)
        )

    def from_experts(rows_back):
        return (
            rows_back.reshape(experts_local, device_count, capacity, model_width)
            .transpose(1, 0, 2, 3)
            .reshape(device_count * experts_local * capacity, model_width)
        )

    rows_in = to_experts(expert_trade(place_rows(jnp.repeat(normed, top_count, 0))))
    pre_gate = jnp.einsum("erd,edf->erf", rows_in, w_gate, preferred_element_type=jnp.float32)
    pre_up = jnp.einsum("erd,edf->erf", rows_in, w_up, preferred_element_type=jnp.float32)
    sig_gate = jax.nn.sigmoid(pre_gate)
    act_rows = (pre_gate * sig_gate * pre_up).astype(jnp.bfloat16)
    out_rows = jnp.einsum(
        "erf,efd->erd", act_rows, w_down, preferred_element_type=jnp.float32
    ).astype(jnp.bfloat16)
    back_rows = expert_trade(from_experts(out_rows))
    returned = back_rows[dest_row].astype(jnp.float32)
    moe_sum = jnp.sum(
        (returned * pair_weights[:, None]).reshape(tok_rows, top_count, model_width), 1
    )
    layer_out = (hidden_f + moe_sum).astype(jnp.bfloat16)
    grad_f = grad_out.astype(jnp.float32)
    pair_grad = (jnp.repeat(grad_f, top_count, 0) * pair_weights[:, None]).astype(jnp.bfloat16)
    grad_in = to_experts(expert_trade(place_rows(pair_grad)))
    act_grad = jnp.einsum("erd,efd->erf", grad_in, w_down, preferred_element_type=jnp.float32)
    grad_w_down = jnp.einsum(
        "erf,erd->efd", act_rows, grad_in, preferred_element_type=jnp.float32
    ).astype(jnp.bfloat16)
    up_grad = (act_grad * pre_gate * sig_gate).astype(jnp.bfloat16)
    gate_grad = (act_grad * pre_up * sig_gate * (1.0 + pre_gate * (1.0 - sig_gate))).astype(
        jnp.bfloat16
    )
    grad_w_gate = jnp.einsum(
        "erd,erf->edf", rows_in, gate_grad, preferred_element_type=jnp.float32
    ).astype(jnp.bfloat16)
    grad_w_up = jnp.einsum(
        "erd,erf->edf", rows_in, up_grad, preferred_element_type=jnp.float32
    ).astype(jnp.bfloat16)
    row_grad = (
        jnp.einsum("erf,edf->erd", gate_grad, w_gate, preferred_element_type=jnp.float32)
        + jnp.einsum("erf,edf->erd", up_grad, w_up, preferred_element_type=jnp.float32)
    ).astype(jnp.bfloat16)
    back_grad = expert_trade(from_experts(row_grad))
    normed_grad = jnp.sum(
        back_grad[dest_row].astype(jnp.float32).reshape(tok_rows, top_count, model_width), 1
    )
    gain_part = jnp.sum(normed_grad * unit_rows, 0)
    grad_gain = lax.psum(gain_part, ("ctx", "exp"))
    scaled_grad = norm_gain * normed_grad
    hidden_grad = inv_rms * (
        scaled_grad - unit_rows * jnp.mean(scaled_grad * unit_rows, -1, keepdims=True)
    )
    grad_resid = (grad_f + hidden_grad).astype(jnp.bfloat16)
    block_grad = lax.all_gather(grad_resid, "exp", axis=0, tiled=True)
    mixture_gradient = jnp.einsum(
        "td,hd->th", block_grad, proj_full, preferred_element_type=jnp.float32
    ).astype(jnp.bfloat16)
    proj_part = jnp.einsum("th,td->hd", attn_mix, block_grad, preferred_element_type=jnp.float32)
    grad_out_proj = lax.psum_scatter(
        proj_part.astype(jnp.bfloat16), "ctx", scatter_dimension=1, tiled=True
    )
    mixture_quad = mixture_gradient.reshape(seq_rows, kv_heads, group_width, HEAD_SIZE)
    delta_sum = jnp.sum(mixture_quad.astype(jnp.float32) * attention_quad.astype(jnp.float32), -1)
    back_count = (query_start + seq_rows + block_len - 1) // block_len

    def backward_turn(loop_turn, loop_carry):
        query_grad, pair_store = loop_carry
        row_begin = loop_turn * block_len
        key_rows = lax.dynamic_slice_in_dim(keys_all, row_begin, block_len, 0)
        val_rows = lax.dynamic_slice_in_dim(values_all, row_begin, block_len, 0)
        scores = (
            jnp.einsum("bngd,knd->bngk", queries, key_rows, preferred_element_type=jnp.float32)
            * score_scale
        )
        key_pos = row_begin + jnp.arange(block_len, dtype=jnp.int32)
        visible = key_pos[None, :] <= query_pos[:, None]
        prob_full = jnp.where(
            visible[:, None, None, :], jnp.exp(scores - log_sum_total[..., None]), 0.0
        )
        prob_grad = jnp.einsum(
            "bngd,knd->bngk", mixture_quad, val_rows, preferred_element_type=jnp.float32
        )
        score_grad = prob_full * (prob_grad - delta_sum[..., None])
        prob_half = prob_full.astype(jnp.bfloat16)
        score_half = score_grad.astype(jnp.bfloat16)
        query_grad = (
            query_grad
            + jnp.einsum("bngk,knd->bngd", score_half, key_rows, preferred_element_type=jnp.float32)
            * score_scale
        )
        key_grad = (
            jnp.einsum("bngk,bngd->knd", score_half, queries, preferred_element_type=jnp.float32)
            * score_scale
        )
        value_grad = jnp.einsum(
            "bngk,bngd->knd", prob_half, mixture_quad, preferred_element_type=jnp.float32
        )
        pair_store = lax.dynamic_update_slice_in_dim(
            pair_store, jnp.stack([key_grad, value_grad], 2), row_begin, 0
        )
        return (query_grad, pair_store)

    start_back = (
        jnp.zeros(state_shape + (HEAD_SIZE,), jnp.float32),
        jnp.zeros((seq_total, kv_heads, 2, HEAD_SIZE), jnp.float32),
    )
    query_grad, pair_store = lax.fori_loop(0, back_count, backward_turn, start_back)
    grad_query = query_grad.reshape(seq_rows, kv_heads * group_width * HEAD_SIZE).astype(
        jnp.bfloat16
    )
    pair_sum = lax.psum_scatter(
        pair_store.reshape(seq_total, kv_heads * 2 * HEAD_SIZE).astype(jnp.bfloat16),
        "ctx",
        scatter_dimension=0,
        tiled=True,
    ).astype(jnp.float32)
    pair_sum = pair_sum.reshape(seq_rows, kv_heads, 2, HEAD_SIZE)
    key_gradient = pair_sum[:, :, 0].reshape(seq_rows, kv_heads * HEAD_SIZE).astype(jnp.bfloat16)
    value_gradient = pair_sum[:, :, 1].reshape(seq_rows, kv_heads * HEAD_SIZE).astype(jnp.bfloat16)
    return (
        layer_out,
        grad_resid,
        grad_query,
        key_gradient,
        value_gradient,
        grad_out_proj,
        grad_gain,
        grad_w_gate,
        grad_w_up,
        grad_w_down,
    )

F32 = jnp.float32
BF16 = jnp.bfloat16


def shifted(x, shift, count):
    return lax.ppermute(x, "ctx", [(i, (i + shift) % count) for i in range(count)])


def swapped(x, bit, count):
    return lax.ppermute(x, "exp", [(i, i ^ bit) for i in range(count)])


def exp_bits(exp_count):
    return [1 << b for b in reversed(range(exp_count.bit_length() - 1))]


def pick(x, index, axis):
    return lax.dynamic_index_in_dim(x, index, axis, keepdims=False)


def ctx_order(blocks, ctx_index):
    count = len(blocks)
    return jnp.stack(blocks)[(ctx_index - jnp.arange(count, dtype=jnp.int32)) % count]


def exp_order(blocks, exp_index):
    count = len(blocks)
    return jnp.stack(blocks)[exp_index ^ jnp.arange(count, dtype=jnp.int32)]


def gather_ctx(x, count):
    return [x] + [shifted(x, d, count) for d in range(1, count)]


def gather_exp(x, count):
    parts = {0: x}
    for bit in exp_bits(count):
        for r in list(parts):
            parts[r ^ bit] = swapped(parts[r], bit, count)
    return [parts[r] for r in range(count)]


def scatter_exp(x, exp_index, count):
    for bit in reversed(exp_bits(count)):
        halves = x.reshape((x.shape[0] // 2, 2) + x.shape[1:])
        mine = (exp_index // bit) % 2
        got = swapped(pick(halves, 1 - mine, 1), bit, count)
        x = (pick(halves, mine, 1).astype(F32) + got.astype(F32)).astype(BF16)
    return x[0]


def scatter_ctx(x, ctx_index, count):
    total = pick(x, ctx_index, 0).astype(F32)
    for d in range(1, count):
        total = total + shifted(pick(x, (ctx_index + d) % count, 0), d, count).astype(F32)
    return total


def nt(a, b):
    return lax.dot_general(a, b, (((1,), (1,)), ((), ())), preferred_element_type=F32)


def tn(a, b):
    return lax.dot_general(a, b, (((0,), (0,)), ((), ())), preferred_element_type=F32)


def nn(a, b):
    return lax.dot_general(a, b, (((1,), (0,)), ((), ())), preferred_element_type=F32)


def soft_rows(query, keys, block):
    rows = query.shape[0]
    scores = nt(query, keys) * HEAD_SIZE ** (-0.5)
    query_pos = block * rows + lax.broadcasted_iota(jnp.int32, scores.shape, 0)
    key_pos = lax.broadcasted_iota(jnp.int32, scores.shape, 1)
    scores = jnp.where(key_pos <= query_pos, scores, NEG)
    weights = jnp.exp(scores - jnp.max(scores, -1, keepdims=True))
    return weights, jnp.sum(weights, -1, keepdims=True)


def forward_kernel(query_ref, key_ref, value_ref, mix_ref):
    block = pl.program_id(0)
    for head in range(query_ref.shape[1] // HEAD_SIZE):
        cols = slice(head * HEAD_SIZE, (head + 1) * HEAD_SIZE)
        weights, total = soft_rows(query_ref[:, cols], key_ref[...], block)
        mixed = nn(weights.astype(BF16), value_ref[...])
        mix_ref[:, cols] = (mixed / total).astype(BF16)


def attention_forward(query_all, key_all, value_all, rows):
    total, width = query_all.shape
    return pl.pallas_call(
        forward_kernel,
        grid=(total // rows,),
        in_specs=[
            pl.BlockSpec((rows, width), lambda i: (i, 0)),
            pl.BlockSpec(key_all.shape, lambda i: (0, 0)),
            pl.BlockSpec(value_all.shape, lambda i: (0, 0)),
        ],
        out_specs=pl.BlockSpec((rows, width), lambda i: (i, 0)),
        out_shape=jax.ShapeDtypeStruct((total, width), BF16),
        compiler_params=pltpu.CompilerParams(vmem_limit_bytes=32 << 20),
        name="attention_forward",
    )(query_all, key_all, value_all)


def backward_kernel(block_ref, query_ref, key_ref, value_ref, mix_ref, grad_ref, dq_ref, pair_ref):
    block = block_ref[0]
    keys, values = key_ref[...], value_ref[...]
    scale = HEAD_SIZE ** (-0.5)
    key_sum = value_sum = 0.0
    for head in range(query_ref.shape[1] // HEAD_SIZE):
        cols = slice(head * HEAD_SIZE, (head + 1) * HEAD_SIZE)
        query, mix, grad = query_ref[:, cols], mix_ref[:, cols], grad_ref[:, cols]
        weights, total = soft_rows(query, keys, block)
        prob = weights / total
        delta = jnp.sum(grad.astype(F32) * mix.astype(F32), -1, keepdims=True)
        score_half = (prob * (nt(grad, values) - delta)).astype(BF16)
        dq_ref[:, cols] = (nn(score_half, keys) * scale).astype(BF16)
        key_sum = key_sum + tn(score_half, query)
        value_sum = value_sum + tn(prob.astype(BF16), grad)
    pair_ref[:, :HEAD_SIZE] = (key_sum * scale).astype(BF16)
    pair_ref[:, HEAD_SIZE:] = value_sum.astype(BF16)


def attention_backward(block, query, key_all, value_all, mix, grad):
    vmem = pl.BlockSpec(memory_space=pltpu.VMEM)
    return pl.pallas_call(
        backward_kernel,
        in_specs=[pl.BlockSpec(memory_space=pltpu.SMEM)] + [vmem] * 5,
        out_specs=[vmem, vmem],
        out_shape=[
            jax.ShapeDtypeStruct(query.shape, BF16),
            jax.ShapeDtypeStruct((key_all.shape[0], 2 * HEAD_SIZE), BF16),
        ],
        compiler_params=pltpu.CompilerParams(vmem_limit_bytes=32 << 20),
        name="attention_backward",
    )(block.reshape(1), query, key_all, value_all, mix, grad)


def local_dense(
    resid,
    query,
    key,
    value,
    out_proj,
    norm_gain,
    w_gate,
    w_up,
    w_down,
    routes,
    gate_weights,
    grad_out,
):
    n, m = lax.axis_size("ctx"), lax.axis_size("exp")
    c, e = lax.axis_index("ctx"), lax.axis_index("exp")
    rows, head_cols = query.shape
    tok, width = resid.shape
    cols = out_proj.shape[1]
    expert_total = n * m
    total = n * m * tok

    pair = jnp.concatenate([key, value], 1)
    pair_all = ctx_order(gather_ctx(pair, n), c).reshape(n * rows, 2 * HEAD_SIZE)
    key_all, value_all = pair_all[:, :HEAD_SIZE], pair_all[:, HEAD_SIZE:]
    query_all = ctx_order(gather_ctx(query, n), c).reshape(n * rows, head_cols)
    resid_cut = resid.reshape(tok, n, cols)
    resid_all = ctx_order(
        [pick(resid_cut, c, 1)]
        + [shifted(pick(resid_cut, (c + d) % n, 1), d, n) for d in range(1, n)],
        c,
    )
    gate_dense = jnp.sum(
        jnp.where(
            routes[:, :, None] == jnp.arange(expert_total, dtype=jnp.int32)[None, None, :],
            gate_weights[:, :, None],
            0.0,
        ),
        1,
    )
    gate_all = lax.all_gather(gate_dense, ("ctx", "exp"), axis=0, tiled=True)
    gate_col = lax.dynamic_slice_in_dim(gate_all, c * m + e, 1, 1)

    def gather_rows(x):
        got = ctx_order(gather_ctx(x, n), c)
        got = exp_order(gather_exp(got, m), e)
        return got.transpose(1, 0, 2, 3).reshape(total, width)

    grad_all = gather_rows(grad_out)
    proj_full = lax.all_gather(out_proj, "ctx", axis=1, tiled=True)

    mix_all = attention_forward(query_all, key_all, value_all, rows)
    part = nn(mix_all, out_proj).astype(BF16).reshape(n, m, tok, cols)
    block_sum = scatter_exp(part.transpose(1, 0, 2, 3), e, m)
    hidden_block = (block_sum.astype(F32) + resid_all.astype(F32)).astype(BF16)

    got = jnp.stack(exp_order(gather_exp(ctx_order(gather_ctx(hidden_block, n), c), m), e))
    hidden_all = got.transpose(2, 0, 3, 1, 4).reshape(total, width)
    hidden_f = hidden_all.astype(F32)
    rms_all = lax.rsqrt(jnp.mean(hidden_f * hidden_f, -1, keepdims=True) + EPS)
    normed_all = (hidden_f * rms_all * norm_gain).astype(BF16)

    gate_in, up_in, down_in = w_gate[0], w_up[0], w_down[0]
    routed = gate_col > 0.0
    grad_rows = (grad_all.astype(F32) * gate_col).astype(BF16)
    act_grad = nt(grad_rows, down_in)
    pre_gate = nn(normed_all, gate_in)
    pre_up = nn(normed_all, up_in)
    sig = jax.nn.sigmoid(pre_gate)
    act_rows = (pre_gate * sig * pre_up).astype(BF16)
    up_grad = (act_grad * pre_gate * sig).astype(BF16)
    gate_grad = (act_grad * pre_up * sig * (1.0 + pre_gate * (1.0 - sig))).astype(BF16)
    row_grad = (nt(gate_grad, gate_in) + nt(up_grad, up_in)).astype(BF16)
    out_rows = nn(act_rows, down_in).astype(BF16)
    weighted = (out_rows.astype(F32) * gate_col).astype(BF16)

    def scatter_rows(x):
        blocks = x.reshape(n, m, tok, width).transpose(1, 0, 2, 3)
        return scatter_ctx(scatter_exp(blocks, e, m), c, n)

    normed_grad = scatter_rows(row_grad)
    moe_sum = scatter_rows(weighted)
    grad_w_down = tn(act_rows, grad_rows).astype(BF16)[None]
    grad_w_gate = tn(normed_all, gate_grad).astype(BF16)[None]
    grad_w_up = tn(normed_all, up_grad).astype(BF16)[None]

    start = (c * m + e) * tok
    hidden = lax.dynamic_slice_in_dim(hidden_all, start, tok, 0).astype(F32)
    inv_rms = lax.dynamic_slice_in_dim(rms_all, start, tok, 0)
    layer_out = (hidden + moe_sum).astype(BF16)
    unit_rows = hidden * inv_rms
    scaled = norm_gain * normed_grad
    hidden_grad = inv_rms * (scaled - unit_rows * jnp.mean(scaled * unit_rows, -1, keepdims=True))
    grad_resid = (grad_out.astype(F32) + hidden_grad).astype(BF16)
    grad_gain = jnp.sum(normed_grad * unit_rows, 0).reshape(-1, 128)
    for bit in exp_bits(m):
        grad_gain = grad_gain + swapped(grad_gain, bit, m)
    grad_gain = sum(gather_ctx(grad_gain, n)[1:], grad_gain).reshape(width)

    block_grad = exp_order(gather_exp(grad_resid, m), e).reshape(rows, width)
    mix_grad = nt(block_grad, proj_full).astype(BF16)
    mix = lax.dynamic_slice_in_dim(mix_all, c * rows, rows, 0)
    grad_query, pair_part = attention_backward(c, query, key_all, value_all, mix, mix_grad)
    pair_sum = scatter_ctx(pair_part.reshape(n, rows, 2 * HEAD_SIZE), c, n).astype(BF16)

    grad_cut = grad_resid.reshape(tok, n, cols)
    cut = ctx_order(
        [pick(grad_cut, c, 1)]
        + [shifted(pick(grad_cut, (c + d) % n, 1), d, n) for d in range(1, n)],
        c,
    )
    cut = exp_order(gather_exp(cut, m), e).transpose(1, 0, 2, 3).reshape(total, cols)
    grad_out_proj = tn(mix_all, cut).astype(BF16)
    return (
        layer_out,
        grad_resid,
        grad_query,
        pair_sum[:, :HEAD_SIZE],
        pair_sum[:, HEAD_SIZE:],
        grad_out_proj,
        grad_gain,
        grad_w_gate,
        grad_w_up,
        grad_w_down,
    )


def local(*args):
    resid, key, w_gate, routes = args[0], args[2], args[6], args[9]
    ctx_count, exp_count = lax.axis_size("ctx"), lax.axis_size("exp")
    expert_total = w_gate.shape[0] * ctx_count * exp_count
    dense = (
        2 * routes.shape[1] >= expert_total
        and w_gate.shape[0] == 1
        and key.shape[1] == HEAD_SIZE
        and exp_count & (exp_count - 1) == 0
    )
    return (local_dense if dense else local_routed)(*args)


def solution(mesh):
    in_specs = (
        P(("groups", "ctx", "exp"), None),
        P(("groups", "ctx"), "exp"),
        P(("groups", "ctx"), "exp"),
        P(("groups", "ctx"), "exp"),
        P("exp", "ctx"),
        P(),
        P(("ctx", "exp"), None, None),
        P(("ctx", "exp"), None, None),
        P(("ctx", "exp"), None, None),
        P(("groups", "ctx", "exp"), None),
        P(("groups", "ctx", "exp"), None),
        P(("groups", "ctx", "exp"), None),
    )
    out_specs = (
        P(("groups", "ctx", "exp"), None),
        P(("groups", "ctx", "exp"), None),
        P(("groups", "ctx"), "exp"),
        P(("groups", "ctx"), "exp"),
        P(("groups", "ctx"), "exp"),
        P(("groups", "exp"), "ctx"),
        P("groups"),
        P(("groups", "ctx", "exp"), None, None),
        P(("groups", "ctx", "exp"), None, None),
        P(("groups", "ctx", "exp"), None, None),
    )
    return jax.shard_map(local, mesh=mesh, in_specs=in_specs, out_specs=out_specs, check_vma=False)
```

```python
import jax
import jax.numpy as jnp
from jax import lax
from jax.experimental import pallas as pl
from jax.experimental.pallas import tpu as pltpu
from jax.sharding import PartitionSpec as P

HEAD_SIZE = 128


EPS = 1e-06
NEG = -1e30


def attend_block(soft_state, queries, key_rows, val_rows, row_begin, query_pos, score_scale):
    peak_run, total_run, accum_rows = soft_state
    scores = (
        jnp.einsum("bngd,knd->bngk", queries, key_rows, preferred_element_type=jnp.float32)
        * score_scale
    )
    key_pos = row_begin + jnp.arange(key_rows.shape[0], dtype=jnp.int32)
    visible = key_pos[None, :] <= query_pos[:, None]
    scores = jnp.where(visible[:, None, None, :], scores, NEG)
    peak_new = jnp.maximum(peak_run, jnp.max(scores, -1))
    rescale = jnp.exp(peak_run - peak_new)
    weights = jnp.exp(scores - peak_new[..., None])
    total_new = total_run * rescale + jnp.sum(weights, -1)
    mixed_rows = jnp.einsum(
        "bngk,knd->bngd", weights.astype(jnp.bfloat16), val_rows, preferred_element_type=jnp.float32
    )
    return (peak_new, total_new, accum_rows * rescale[..., None] + mixed_rows)


def expert_trade(buffer):
    return lax.all_to_all(buffer, ("ctx", "exp"), split_axis=0, concat_axis=0, tiled=True)


def local_routed(
    resid,
    query,
    key,
    value,
    out_proj,
    norm_gain,
    w_gate,
    w_up,
    w_down,
    routes,
    gate_weights,
    grad_out,
):
    ctx_count = lax.axis_size("ctx")
    exp_count = lax.axis_size("exp")
    ctx_index = lax.axis_index("ctx")
    seq_rows = query.shape[0]
    kv_heads = key.shape[1] // HEAD_SIZE
    group_width = query.shape[1] // HEAD_SIZE // kv_heads
    seq_total = seq_rows * ctx_count
    score_scale = HEAD_SIZE ** (-0.5)
    query_start = ctx_index * seq_rows
    query_pos = query_start + jnp.arange(seq_rows, dtype=jnp.int32)
    queries = query.reshape(seq_rows, kv_heads, group_width, HEAD_SIZE)
    state_shape = (seq_rows, kv_heads, group_width)
    start_state = (
        jnp.full(state_shape, NEG, jnp.float32),
        jnp.zeros(state_shape, jnp.float32),
        jnp.zeros(state_shape + (HEAD_SIZE,), jnp.float32),
    )
    block_len = min(512, seq_total)
    keys_flat, values_flat = (
        lax.all_gather(key, "ctx", axis=0, tiled=True),
        lax.all_gather(value, "ctx", axis=0, tiled=True),
    )
    keys_all = keys_flat.reshape(seq_total, kv_heads, HEAD_SIZE)
    values_all = values_flat.reshape(seq_total, kv_heads, HEAD_SIZE)
    block_count = (query_start + seq_rows + block_len - 1) // block_len

    def forward_turn(loop_turn, soft_state):
        row_begin = loop_turn * block_len
        key_rows = lax.dynamic_slice_in_dim(keys_all, row_begin, block_len, 0)
        val_rows = lax.dynamic_slice_in_dim(values_all, row_begin, block_len, 0)
        return attend_block(
            soft_state, queries, key_rows, val_rows, row_begin, query_pos, score_scale
        )

    soft_state = lax.fori_loop(0, block_count, forward_turn, start_state)
    peak_val, total_val, accum_rows = soft_state
    attention_quad = (accum_rows / total_val[..., None]).astype(jnp.bfloat16)
    attn_mix = attention_quad.reshape(seq_rows, kv_heads * group_width * HEAD_SIZE)
    log_sum_total = peak_val + jnp.log(total_val)
    proj_full = lax.all_gather(out_proj, "ctx", axis=1, tiled=True)
    tok_rows = resid.shape[0]
    proj_sum = lax.psum_scatter(
        jnp.dot(attn_mix, proj_full, preferred_element_type=jnp.float32).astype(jnp.bfloat16),
        "exp",
        scatter_dimension=0,
        tiled=True,
    ).astype(jnp.float32)
    hidden = (resid.astype(jnp.float32) + proj_sum).astype(jnp.bfloat16)
    hidden_f = hidden.astype(jnp.float32)
    inv_rms = lax.rsqrt(jnp.mean(hidden_f * hidden_f, -1, keepdims=True) + EPS)
    unit_rows = hidden_f * inv_rms
    normed = (unit_rows * norm_gain).astype(jnp.bfloat16)
    top_count = routes.shape[1]
    model_width = normed.shape[1]
    experts_local = w_gate.shape[0]
    device_count = ctx_count * exp_count
    expert_total = experts_local * device_count
    capacity = 2 * tok_rows * top_count // expert_total
    flat_routes = routes.reshape(-1)
    member = (flat_routes[:, None] == jnp.arange(expert_total, dtype=jnp.int32)[None, :]).astype(
        jnp.int32
    )
    slot_pos = jnp.sum(jnp.cumsum(member, 0) * member, 1) - 1
    dest_row = flat_routes * capacity + slot_pos
    pair_weights = gate_weights.reshape(-1)

    def place_rows(rows_out):
        return (
            jnp.zeros((expert_total * capacity, model_width), jnp.bfloat16)
            .at[dest_row]
            .set(rows_out)
        )

    def to_experts(buffer):
        return (
            buffer.reshape(device_count, experts_local, capacity, model_width)
            .transpose(1, 0, 2, 3)
            .reshape(experts_local, device_count * capacity, model_width)
        )

    def from_experts(rows_back):
        return (
            rows_back.reshape(experts_local, device_count, capacity, model_width)
            .transpose(1, 0, 2, 3)
            .reshape(device_count * experts_local * capacity, model_width)
        )

    rows_in = to_experts(expert_trade(place_rows(jnp.repeat(normed, top_count, 0))))
    pre_gate = jnp.einsum("erd,edf->erf", rows_in, w_gate, preferred_element_type=jnp.float32)
    pre_up = jnp.einsum("erd,edf->erf", rows_in, w_up, preferred_element_type=jnp.float32)
    sig_gate = jax.nn.sigmoid(pre_gate)
    act_rows = (pre_gate * sig_gate * pre_up).astype(jnp.bfloat16)
    out_rows = jnp.einsum(
        "erf,efd->erd", act_rows, w_down, preferred_element_type=jnp.float32
    ).astype(jnp.bfloat16)
    back_rows = expert_trade(from_experts(out_rows))
    returned = back_rows[dest_row].astype(jnp.float32)
    moe_sum = jnp.sum(
        (returned * pair_weights[:, None]).reshape(tok_rows, top_count, model_width), 1
    )
    layer_out = (hidden_f + moe_sum).astype(jnp.bfloat16)
    grad_f = grad_out.astype(jnp.float32)
    pair_grad = (jnp.repeat(grad_f, top_count, 0) * pair_weights[:, None]).astype(jnp.bfloat16)
    grad_in = to_experts(expert_trade(place_rows(pair_grad)))
    act_grad = jnp.einsum("erd,efd->erf", grad_in, w_down, preferred_element_type=jnp.float32)
    grad_w_down = jnp.einsum(
        "erf,erd->efd", act_rows, grad_in, preferred_element_type=jnp.float32
    ).astype(jnp.bfloat16)
    up_grad = (act_grad * pre_gate * sig_gate).astype(jnp.bfloat16)
    gate_grad = (act_grad * pre_up * sig_gate * (1.0 + pre_gate * (1.0 - sig_gate))).astype(
        jnp.bfloat16
    )
    grad_w_gate = jnp.einsum(
        "erd,erf->edf", rows_in, gate_grad, preferred_element_type=jnp.float32
    ).astype(jnp.bfloat16)
    grad_w_up = jnp.einsum(
        "erd,erf->edf", rows_in, up_grad, preferred_element_type=jnp.float32
    ).astype(jnp.bfloat16)
    row_grad = (
        jnp.einsum("erf,edf->erd", gate_grad, w_gate, preferred_element_type=jnp.float32)
        + jnp.einsum("erf,edf->erd", up_grad, w_up, preferred_element_type=jnp.float32)
    ).astype(jnp.bfloat16)
    back_grad = expert_trade(from_experts(row_grad))
    normed_grad = jnp.sum(
        back_grad[dest_row].astype(jnp.float32).reshape(tok_rows, top_count, model_width), 1
    )
    gain_part = jnp.sum(normed_grad * unit_rows, 0)
    grad_gain = lax.psum(gain_part, ("ctx", "exp"))
    scaled_grad = norm_gain * normed_grad
    hidden_grad = inv_rms * (
        scaled_grad - unit_rows * jnp.mean(scaled_grad * unit_rows, -1, keepdims=True)
    )
    grad_resid = (grad_f + hidden_grad).astype(jnp.bfloat16)
    block_grad = lax.all_gather(grad_resid, "exp", axis=0, tiled=True)
    mixture_gradient = jnp.einsum(
        "td,hd->th", block_grad, proj_full, preferred_element_type=jnp.float32
    ).astype(jnp.bfloat16)
    proj_part = jnp.einsum("th,td->hd", attn_mix, block_grad, preferred_element_type=jnp.float32)
    grad_out_proj = lax.psum_scatter(
        proj_part.astype(jnp.bfloat16), "ctx", scatter_dimension=1, tiled=True
    )
    mixture_quad = mixture_gradient.reshape(seq_rows, kv_heads, group_width, HEAD_SIZE)
    delta_sum = jnp.sum(mixture_quad.astype(jnp.float32) * attention_quad.astype(jnp.float32), -1)
    back_count = (query_start + seq_rows + block_len - 1) // block_len

    def backward_turn(loop_turn, loop_carry):
        query_grad, pair_store = loop_carry
        row_begin = loop_turn * block_len
        key_rows = lax.dynamic_slice_in_dim(keys_all, row_begin, block_len, 0)
        val_rows = lax.dynamic_slice_in_dim(values_all, row_begin, block_len, 0)
        scores = (
            jnp.einsum("bngd,knd->bngk", queries, key_rows, preferred_element_type=jnp.float32)
            * score_scale
        )
        key_pos = row_begin + jnp.arange(block_len, dtype=jnp.int32)
        visible = key_pos[None, :] <= query_pos[:, None]
        prob_full = jnp.where(
            visible[:, None, None, :], jnp.exp(scores - log_sum_total[..., None]), 0.0
        )
        prob_grad = jnp.einsum(
            "bngd,knd->bngk", mixture_quad, val_rows, preferred_element_type=jnp.float32
        )
        score_grad = prob_full * (prob_grad - delta_sum[..., None])
        prob_half = prob_full.astype(jnp.bfloat16)
        score_half = score_grad.astype(jnp.bfloat16)
        query_grad = (
            query_grad
            + jnp.einsum("bngk,knd->bngd", score_half, key_rows, preferred_element_type=jnp.float32)
            * score_scale
        )
        key_grad = (
            jnp.einsum("bngk,bngd->knd", score_half, queries, preferred_element_type=jnp.float32)
            * score_scale
        )
        value_grad = jnp.einsum(
            "bngk,bngd->knd", prob_half, mixture_quad, preferred_element_type=jnp.float32
        )
        pair_store = lax.dynamic_update_slice_in_dim(
            pair_store, jnp.stack([key_grad, value_grad], 2), row_begin, 0
        )
        return (query_grad, pair_store)

    start_back = (
        jnp.zeros(state_shape + (HEAD_SIZE,), jnp.float32),
        jnp.zeros((seq_total, kv_heads, 2, HEAD_SIZE), jnp.float32),
    )
    query_grad, pair_store = lax.fori_loop(0, back_count, backward_turn, start_back)
    grad_query = query_grad.reshape(seq_rows, kv_heads * group_width * HEAD_SIZE).astype(
        jnp.bfloat16
    )
    pair_sum = lax.psum_scatter(
        pair_store.reshape(seq_total, kv_heads * 2 * HEAD_SIZE).astype(jnp.bfloat16),
        "ctx",
        scatter_dimension=0,
        tiled=True,
    ).astype(jnp.float32)
    pair_sum = pair_sum.reshape(seq_rows, kv_heads, 2, HEAD_SIZE)
    key_gradient = pair_sum[:, :, 0].reshape(seq_rows, kv_heads * HEAD_SIZE).astype(jnp.bfloat16)
    value_gradient = pair_sum[:, :, 1].reshape(seq_rows, kv_heads * HEAD_SIZE).astype(jnp.bfloat16)
    return (
        layer_out,
        grad_resid,
        grad_query,
        key_gradient,
        value_gradient,
        grad_out_proj,
        grad_gain,
        grad_w_gate,
        grad_w_up,
        grad_w_down,
    )


F32 = jnp.float32
BF16 = jnp.bfloat16
LOG2E = 1.4426950408889634
SETS = (0, 2, 1, 3)


def shifted(x, shift, count):
    return lax.ppermute(x, "ctx", [(i, (i + shift) % count) for i in range(count)])


def swapped(x, bit):
    return lax.ppermute(x, "exp", [(i, i ^ bit) for i in range(4)])


def pick(x, index, axis):
    return lax.dynamic_index_in_dim(x, index, axis, keepdims=False)


def nt(a, b):
    return lax.dot_general(a, b, (((1,), (1,)), ((), ())), preferred_element_type=F32)


def tn(a, b):
    return lax.dot_general(a, b, (((0,), (0,)), ((), ())), preferred_element_type=F32)


def nn(a, b):
    return lax.dot_general(a, b, (((1,), (0,)), ((), ())), preferred_element_type=F32)


def wrap(value, count):
    return lax.rem(value + count, count)


def run_kernel(body, name, place, args, outs, scratch=(), flops=0, limit=40):
    vmem = pl.BlockSpec(memory_space=pltpu.VMEM)
    shapes = [jax.ShapeDtypeStruct(shape, dtype) for shape, dtype in outs]
    moved = sum(x.size * x.dtype.itemsize for x in list(args) + shapes)
    return pl.pallas_call(
        body,
        in_specs=[pl.BlockSpec(memory_space=pltpu.SMEM)] + [vmem] * len(args),
        out_specs=[vmem] * len(outs),
        out_shape=shapes,
        scratch_shapes=[pltpu.VMEM(shape, dtype) for shape, dtype in scratch],
        compiler_params=pltpu.CompilerParams(vmem_limit_bytes=limit << 20),
        cost_estimate=pl.CostEstimate(flops=flops, bytes_accessed=moved, transcendentals=0),
        name=name,
    )(place, *args)


def attend(place, query_parts, pair_parts, out_proj):
    n = len(query_parts)
    rows, width = query_parts[0].shape
    tok = rows // 4
    cols = out_proj.shape[1]
    heads = width // HEAD_SIZE
    factor = HEAD_SIZE ** (-0.5) * LOG2E

    def body(place_ref, *refs):
        q_refs, p_refs, proj_ref = refs[:n], refs[n : 2 * n], refs[2 * n]
        mix_ref, own_ref, keep_ref, send_ref, qs, ks, vs, ps = refs[2 * n + 1 :]
        c, e = place_ref[0], place_ref[1]
        for d in range(n):
            at = pl.multiple_of(wrap(c - d, n) * rows, rows)
            qs[pl.ds(at, rows), :] = q_refs[d][...]
            ks[pl.ds(at, rows), :] = p_refs[d][:, :HEAD_SIZE]
            vs[pl.ds(at, rows), :] = p_refs[d][:, HEAD_SIZE:]
        below = lax.broadcasted_iota(jnp.int32, (rows, rows), 1) <= lax.broadcasted_iota(
            jnp.int32, (rows, rows), 0
        )
        core, line = lax.rem(e, 2), lax.div(e, 2)
        for b in range(n):
            lo, hi = b * rows, (b + 1) * rows
            for head in range(heads):
                at = slice(head * HEAD_SIZE, (head + 1) * HEAD_SIZE)
                scores = nt(qs[lo:hi, at], ks[:hi, :])
                last = jnp.where(below, scores[:, lo:], NEG)
                scores = jnp.concatenate([scores[:, :lo], last], 1) if b else last
                peak = jnp.max(scores, -1, keepdims=True)
                weights = jnp.exp2((scores - peak) * factor)
                total = jnp.sum(weights, -1, keepdims=True)
                mix_ref[lo:hi, at] = (nn(weights.astype(BF16), vs[:hi, :]) / total).astype(BF16)
            ps[...] = nn(mix_ref[lo:hi, :], proj_ref[...]).astype(BF16)
            d = wrap(c - b, n)
            for turn in range(2):
                base = (line + turn - 2 * turn * line) * 2
                keep_ref[turn, d] = ps[pl.ds(pl.multiple_of((base + core) * tok, tok), tok), :]
                send_ref[turn, d] = ps[pl.ds(pl.multiple_of((base + 1 - core) * tok, tok), tok), :]
        own_ref[...] = mix_ref[pl.ds(pl.multiple_of(c * rows, rows), rows), :]

    return run_kernel(
        body,
        "attend",
        place,
        [*query_parts, *pair_parts, out_proj],
        [
            ((n * rows, width), BF16),
            ((rows, width), BF16),
            ((2, n, tok, cols), BF16),
            ((2, n, tok, cols), BF16),
        ],
        [
            ((n * rows, width), BF16),
            ((n * rows, HEAD_SIZE), BF16),
            ((n * rows, HEAD_SIZE), BF16),
            ((rows, cols), BF16),
        ],
        flops=4 * n * rows * n * rows * width,
    )


def hidden_rows(place, keep, received, crossed, resid_parts):
    n = len(resid_parts)

    def body(place_ref, keep_ref, received_ref, crossed_ref, *refs):
        for d in range(n):
            total = keep_ref[0, d].astype(F32) + received_ref[0, d].astype(F32)
            total = total + crossed_ref[d].astype(F32) + refs[d][...].astype(F32)
            refs[n][d] = total.astype(BF16)

    return run_kernel(
        body, "hidden_rows", place, [keep, received, crossed, *resid_parts], [(crossed.shape, BF16)]
    )[0]


def grad_rows_of(place, grad_sets, w_down, width):
    n, tok = grad_sets[0].shape[:2]
    total = 4 * n * tok
    experts = 4 * n

    def body(place_ref, *refs):
        down_ref, rows_ref, gate_ref, act_ref = refs[4:]
        expert = place_ref[0] * 4 + place_ref[1]
        lane = lax.broadcasted_iota(jnp.int32, (tok, 128), 1)
        wanted = (lane == expert) | (lane == expert + experts)
        for s in range(4):
            for d in range(n):
                at = s * n * tok + (-d) % n * tok
                gate = jnp.where(wanted, refs[s][d, :, width:].astype(F32), 0.0)
                gate = jnp.sum(gate, -1, keepdims=True)
                gate_ref[at : at + tok, :] = gate
                rows_ref[at : at + tok, :] = (refs[s][d, :, :width].astype(F32) * gate).astype(BF16)
        act_ref[...] = nt(rows_ref[...], down_ref[...])

    return run_kernel(
        body,
        "grad_rows",
        place,
        [*grad_sets, w_down],
        [((total, width), BF16), ((total, 1), F32), ((total, w_down.shape[0]), F32)],
        flops=2 * total * width * w_down.shape[0],
    )


def expert_rows(place, hidden_sets, act_grad, norm_gain, w_gate, w_up):
    n, tok, cols = hidden_sets[0][0].shape
    width, hidden_units = w_gate.shape
    group = n * tok
    total = 4 * group

    def body(place_ref, *refs):
        pieces = refs[: 4 * n]
        act_grad_ref, gain_ref, gate_ref, up_ref = refs[4 * n : 4 * n + 4]
        normed_ref, act_ref, gate_grad_ref, up_grad_ref, own_ref = refs[4 * n + 4 : 4 * n + 9]
        grads, hid = refs[4 * n + 9 : 4 * n + 13], refs[4 * n + 13]
        c = place_ref[0]
        for s in range(4):
            for d in range(n):
                at = pl.multiple_of(wrap(c - d, n) * cols, cols)
                for t in range(n):
                    row = s * group + (-(d + t)) % n * tok
                    hid[row : row + tok, pl.ds(at, cols)] = pieces[s * n + d][t]
            rows = slice(s * group, (s + 1) * group)
            value = hid[rows, :].astype(F32)
            inv_rms = lax.rsqrt(jnp.mean(value * value, -1, keepdims=True) + EPS)
            normed_ref[rows, :] = (value * inv_rms * gain_ref[...]).astype(BF16)
        own_ref[...] = hid[:tok, :]
        pre_gate = nn(normed_ref[...], gate_ref[...])
        pre_up = nn(normed_ref[...], up_ref[...])
        sig = jax.nn.sigmoid(pre_gate)
        act_ref[...] = (pre_gate * sig * pre_up).astype(BF16)
        act_grad_value = act_grad_ref[...]
        up_grad_ref[...] = (act_grad_value * pre_gate * sig).astype(BF16)
        gate_grad_ref[...] = (
            act_grad_value * pre_up * sig * (1.0 + pre_gate * (1.0 - sig))
        ).astype(BF16)
        for j in range(n):
            at = slice(j * cols, (j + 1) * cols)
            part = nt(gate_grad_ref[...], gate_ref[at, :]) + nt(up_grad_ref[...], up_ref[at, :])
            for s in range(4):
                block = part[s * group : (s + 1) * group].astype(BF16)
                grads[s][:, :, at] = block.reshape(n, tok, cols)

    units = ((total, hidden_units), BF16)
    return run_kernel(
        body,
        "expert_rows",
        place,
        [*sum(hidden_sets, []), act_grad, norm_gain.reshape(1, width), w_gate, w_up],
        [((total, width), BF16), units, units, units, ((tok, width), BF16)]
        + [((n, tok, width), BF16)] * 4,
        [((total, width), BF16)],
        flops=8 * total * width * hidden_units,
    )


def weighted_rows(place, act_rows, gate, w_down, n):
    total = act_rows.shape[0]
    width = w_down.shape[1]
    group, cols = total // 4, width // n

    def body(place_ref, act_ref, gate_ref, down_ref, *outs):
        for j in range(n):
            at = slice(j * cols, (j + 1) * cols)
            part = nn(act_ref[...], down_ref[:, at]).astype(BF16).astype(F32) * gate_ref[...]
            for s in range(4):
                block = part[s * group : (s + 1) * group].astype(BF16)
                outs[s][:, :, at] = block.reshape(n, group // n, cols)

    return run_kernel(
        body,
        "weighted_rows",
        place,
        [act_rows, gate, w_down],
        [((n, group // n, width), BF16)] * 4,
        flops=2 * total * width * w_down.shape[0],
    )


def sum_back(parts):
    n = parts[0].shape[0]
    order = sorted(range(n), key=lambda j: -min(j, n - j))
    far, near = swapped(parts[3], 1), swapped(parts[2], 1)

    def add(*xs):
        return sum([x.astype(F32) for x in xs[1:]], xs[0].astype(F32)).astype(BF16)

    crossed = {j: swapped(add(parts[1][j], far[j]), 2) for j in order}
    sums = {j: add(parts[0][j], near[j], crossed[j]) for j in order}
    received = {j: shifted(sums[j], j, n) for j in order if j}
    return [sums[0]] + [received[j] for j in range(1, n)]


def norm_backward(place, summed, hidden, grad_out, norm_gain, cols):
    n = len(summed)
    tok, width = hidden.shape

    def body(place_ref, *refs):
        hidden_ref, grad_ref, gain_ref = refs[n : n + 3]
        out_ref, part_ref, cuts = refs[n + 3], refs[n + 4], refs[n + 5 :]
        c = place_ref[0]
        normed_grad = sum([r[...].astype(F32) for r in refs[1:n]], refs[0][...].astype(F32))
        value = hidden_ref[...].astype(F32)
        inv_rms = lax.rsqrt(jnp.mean(value * value, -1, keepdims=True) + EPS)
        unit_rows = value * inv_rms
        part_ref[...] = jnp.sum(normed_grad * unit_rows, 0, keepdims=True)
        scaled = gain_ref[...] * normed_grad
        mean = jnp.mean(scaled * unit_rows, -1, keepdims=True)
        grad = grad_ref[...].astype(F32) + inv_rms * (scaled - unit_rows * mean)
        out_ref[...] = grad.astype(BF16)
        for d in range(n):
            cuts[d][...] = out_ref[:, pl.ds(pl.multiple_of(wrap(c + d, n) * cols, cols), cols)]

    return run_kernel(
        body,
        "norm_backward",
        place,
        [*summed, hidden, grad_out, norm_gain.reshape(1, width)],
        [((tok, width), BF16), ((1, width), F32)] + [((tok, cols), BF16)] * n,
    )


def layer_rows(place, summed, hidden):
    def body(place_ref, *refs):
        total = refs[-2][...].astype(F32)
        for r in refs[:-2]:
            total = total + r[...].astype(F32)
        refs[-1][...] = total.astype(BF16)

    return run_kernel(body, "layer_rows", place, [*summed, hidden], [(hidden.shape, BF16)])[0]


def attend_backward(place, grad_parts, out_proj, proj_near, proj_far, query, pair_parts, mix):
    n = len(pair_parts)
    rows, width = query.shape
    tok = rows // 4
    cols = out_proj.shape[1]
    heads = width // HEAD_SIZE
    half = width // 2
    scale = HEAD_SIZE ** (-0.5)

    def body(place_ref, *refs):
        g_refs, proj_ref = refs[:4], refs[4]
        near, far = refs[5 : 4 + n], refs[4 + n : 3 + 2 * n]
        query_ref = refs[3 + 2 * n]
        p_refs = refs[4 + 2 * n : 4 + 3 * n]
        mix_ref, dq_ref = refs[4 + 3 * n : 6 + 3 * n]
        outs = refs[6 + 3 * n : 6 + 4 * n]
        gs, acc, qs, ms, ks, vs, score_half, prob_half = refs[6 + 4 * n :]
        c, e, g = place_ref[0], place_ref[1], place_ref[2]
        core, line = lax.rem(e, 2), lax.div(e, 2)
        for r in range(4):
            low, high = r % 2, r // 2
            other = (line + high - 2 * high * line) * 2 + core + low - 2 * low * core
            gs[pl.ds(pl.multiple_of(other * tok, tok), tok), :] = g_refs[r][...]

        def columns(d):
            return gs[:, pl.ds(pl.multiple_of(wrap(c - d, n) * cols, cols), cols)]

        acc[...] = nt(columns(0), proj_ref[...])
        here = pl.ds(pl.multiple_of(g * half, half), half)
        there = pl.ds(pl.multiple_of((1 - g) * half, half), half)
        acc[:, here] += sum([nt(columns(d), near[d - 1][...]) for d in range(1, n)])
        acc[:, there] += sum([nt(columns(d), far[d - 1][...]) for d in range(1, n)])
        key_pos = lax.broadcasted_iota(jnp.int32, (rows, n * rows), 1)
        visible = (key_pos <= lax.broadcasted_iota(jnp.int32, (rows, n * rows), 0)) | (
            (key_pos >= rows) & (key_pos < (c + 1) * rows)
        )
        for d in range(n):
            ks[d * rows : (d + 1) * rows, :] = p_refs[d][:, :HEAD_SIZE]
            vs[d * rows : (d + 1) * rows, :] = p_refs[d][:, HEAD_SIZE:]
        for head in range(heads):
            at = slice(head * HEAD_SIZE, (head + 1) * HEAD_SIZE)
            rs = slice(head * rows, (head + 1) * rows)
            grad = acc[:, at].astype(BF16)
            qs[rs, :] = query_ref[:, at]
            ms[rs, :] = grad
            scores = jnp.where(visible, nt(query_ref[:, at], ks[...]), NEG)
            peak = jnp.max(scores, -1, keepdims=True)
            weights = jnp.exp2((scores - peak) * (scale * LOG2E))
            prob = weights * (1.0 / jnp.sum(weights, -1, keepdims=True))
            delta = jnp.sum(grad.astype(F32) * mix_ref[:, at].astype(F32), -1, keepdims=True)
            score_half[rs, :] = (prob * (nt(grad, vs[...]) - delta)).astype(BF16)
            prob_half[rs, :] = prob.astype(BF16)
            dq_ref[:, at] = (nn(score_half[rs, :], ks[...]) * scale).astype(BF16)
        key_sum = (tn(score_half[...], qs[...]) * scale).astype(BF16)
        value_sum = tn(prob_half[...], ms[...]).astype(BF16)
        for j in range(n):
            rs = slice((-j) % n * rows, ((-j) % n + 1) * rows)
            outs[j][:, :HEAD_SIZE] = key_sum[rs]
            outs[j][:, HEAD_SIZE:] = value_sum[rs]

    stacked = ((heads * rows, HEAD_SIZE), BF16)
    keys = ((n * rows, HEAD_SIZE), BF16)
    halves = ((heads * rows, n * rows), BF16)
    return run_kernel(
        body,
        "attend_backward",
        place,
        [*grad_parts, out_proj, *proj_near, *proj_far, query, *pair_parts, mix],
        [((rows, width), BF16)] + [((rows, 2 * HEAD_SIZE), BF16)] * n,
        [((rows, n * cols), BF16), ((rows, width), F32), stacked, stacked, keys, keys, halves, halves],
        flops=2 * rows * width * (n * cols + 5 * n * rows),
    )


def proj_grad(place, mix_all, cut_sets):
    n, tok, cols = cut_sets[0].shape
    width = mix_all.shape[1]

    def body(place_ref, mix_ref, *refs):
        out_ref, rows_ref = refs[4], refs[5]
        c, e = place_ref[0], place_ref[1]
        core, line = lax.rem(e, 2), lax.div(e, 2)
        for r in range(4):
            low, high = r % 2, r // 2
            other = (line + high - 2 * high * line) * 2 + core + low - 2 * low * core
            for d in range(n):
                at = pl.multiple_of((wrap(c - d, n) * 4 + other) * tok, tok)
                rows_ref[pl.ds(at, tok), :] = refs[r][d]
        out_ref[...] = tn(mix_ref[...], rows_ref[...]).astype(BF16)

    return run_kernel(
        body,
        "proj_grad",
        place,
        [mix_all, *cut_sets],
        [((width, cols), BF16)],
        [((4 * n * tok, cols), BF16)],
        flops=8 * n * tok * cols * width,
    )[0]


def local_dense(
    resid,
    query,
    key,
    value,
    out_proj,
    norm_gain,
    w_gate,
    w_up,
    w_down,
    routes,
    gate_weights,
    grad_out,
):
    n = lax.axis_size("ctx")
    c, e, g = lax.axis_index("ctx"), lax.axis_index("exp"), lax.axis_index("groups")
    place = jnp.stack([c, e, g]).astype(jnp.int32)
    tok, width = resid.shape
    cols = out_proj.shape[1]
    experts = 4 * n

    def to_all(x):
        return [x] + [shifted(x, d, n) for d in range(1, n)]

    pair_parts = to_all(jnp.concatenate([key, value], 1))
    query_parts = to_all(query)
    resid_cut = resid.reshape(tok, n, cols)
    resid_parts = [pick(resid_cut, c, 1)] + [
        shifted(pick(resid_cut, wrap(c + d, n), 1), d, n) for d in range(1, n)
    ]

    gates = jnp.sum(
        jnp.where(
            routes[:, :, None] == jnp.arange(experts, dtype=jnp.int32), gate_weights[:, :, None], 0.0
        ),
        1,
    )
    gate_high = lax.reduce_precision(gates, 8, 7)
    payload = jnp.concatenate(
        [
            grad_out,
            gate_high.astype(BF16),
            (gates - gate_high).astype(BF16),
            jnp.zeros((tok, 128 - 2 * experts), BF16),
        ],
        1,
    )
    payload, proj_half, *_ = lax.optimization_barrier(
        (payload, lax.dynamic_slice_in_dim(out_proj, g * (out_proj.shape[0] // 2), out_proj.shape[0] // 2, 0))
        + tuple(query_parts[1:])
    )
    grad_own = jnp.stack(to_all(payload))
    grad_line = swapped(grad_own, 2)
    grad_sets = [grad_own, grad_line, swapped(grad_own, 1), swapped(grad_line, 1)]

    proj_near = to_all(proj_half)[1:]
    proj_far = [lax.ppermute(x, "groups", [(0, 1), (1, 0)]) for x in proj_near]

    mix_all, mix, keep, send = attend(place, query_parts, pair_parts, out_proj)
    received = swapped(send, 1)
    crossed = swapped((keep[1].astype(F32) + received[1].astype(F32)).astype(BF16), 2)
    hidden_own = to_all(hidden_rows(place, keep, received, crossed, resid_parts))
    hidden_line = [swapped(x, 2) for x in hidden_own]
    hidden_sets = [hidden_own, hidden_line] + [
        [swapped(x, 1) for x in xs] for xs in (hidden_own, hidden_line)
    ]

    grad_rows, gate, act_grad = grad_rows_of(place, grad_sets, w_down[0], width)
    normed, act_rows, gate_grad, up_grad, hidden, *row_grads = expert_rows(
        place, hidden_sets, act_grad, norm_gain, w_gate[0], w_up[0]
    )
    summed = sum_back(row_grads)
    grad_resid, gain_part, *cuts = norm_backward(place, summed, hidden, grad_out, norm_gain, cols)

    near = swapped(grad_resid, 2)
    grad_parts = [grad_resid, swapped(grad_resid, 1), near, swapped(near, 1)]
    grad_query, *pairs = attend_backward(
        place, grad_parts, out_proj, proj_near, proj_far, query, pair_parts, mix
    )
    pair_sum = sum(
        [shifted(pairs[j], j, n).astype(F32) for j in range(1, n)], pairs[0].astype(F32)
    ).astype(BF16)

    cut_own = jnp.stack([cuts[0]] + [shifted(cuts[d], d, n) for d in range(1, n)])
    cut_line = swapped(cut_own, 2)
    cut_sets = [cut_own, swapped(cut_own, 1), cut_line, swapped(cut_line, 1)]
    grad_out_proj = proj_grad(place, mix_all, cut_sets)

    grad_gain = gain_part.reshape(-1, 128)
    for bit in (1, 2):
        grad_gain = grad_gain + swapped(grad_gain, bit)
    grad_gain = sum([shifted(grad_gain, d, n) for d in range(1, n)], grad_gain).reshape(width)

    layer_out = layer_rows(
        place, sum_back(weighted_rows(place, act_rows, gate, w_down[0], n)), hidden
    )
    return (
        layer_out,
        grad_resid,
        grad_query,
        pair_sum[:, :HEAD_SIZE],
        pair_sum[:, HEAD_SIZE:],
        grad_out_proj,
        grad_gain,
        tn(normed, gate_grad).astype(BF16)[None],
        tn(normed, up_grad).astype(BF16)[None],
        tn(act_rows, grad_rows).astype(BF16)[None],
    )


def local(*args):
    key, w_gate, routes = args[2], args[6], args[9]
    ctx_count, exp_count = lax.axis_size("ctx"), lax.axis_size("exp")
    expert_total = w_gate.shape[0] * ctx_count * exp_count
    dense = (
        2 * routes.shape[1] >= expert_total
        and w_gate.shape[0] == 1
        and key.shape[1] == HEAD_SIZE
        and exp_count == 4
        and lax.axis_size("groups") == 2
    )
    return (local_dense if dense else local_routed)(*args)


def solution(mesh):
    in_specs = (
        P(("groups", "ctx", "exp"), None),
        P(("groups", "ctx"), "exp"),
        P(("groups", "ctx"), "exp"),
        P(("groups", "ctx"), "exp"),
        P("exp", "ctx"),
        P(),
        P(("ctx", "exp"), None, None),
        P(("ctx", "exp"), None, None),
        P(("ctx", "exp"), None, None),
        P(("groups", "ctx", "exp"), None),
        P(("groups", "ctx", "exp"), None),
        P(("groups", "ctx", "exp"), None),
    )
    out_specs = (
        P(("groups", "ctx", "exp"), None),
        P(("groups", "ctx", "exp"), None),
        P(("groups", "ctx"), "exp"),
        P(("groups", "ctx"), "exp"),
        P(("groups", "ctx"), "exp"),
        P(("groups", "exp"), "ctx"),
        P("groups"),
        P(("groups", "ctx", "exp"), None, None),
        P(("groups", "ctx", "exp"), None, None),
        P(("groups", "ctx", "exp"), None, None),
    )
    return jax.shard_map(local, mesh=mesh, in_specs=in_specs, out_specs=out_specs, check_vma=False)
```

```python
import jax
import jax.numpy as jnp
from jax import lax
from jax.experimental import pallas as pl
from jax.experimental.pallas import tpu as pltpu
from jax.sharding import PartitionSpec as P

HEAD_SIZE = 128


EPS = 1e-06
NEG = -1e30


def attend_block(soft_state, queries, key_rows, val_rows, row_begin, query_pos, score_scale):
    peak_run, total_run, accum_rows = soft_state
    scores = (
        jnp.einsum("bngd,knd->bngk", queries, key_rows, preferred_element_type=jnp.float32)
        * score_scale
    )
    key_pos = row_begin + jnp.arange(key_rows.shape[0], dtype=jnp.int32)
    visible = key_pos[None, :] <= query_pos[:, None]
    scores = jnp.where(visible[:, None, None, :], scores, NEG)
    peak_new = jnp.maximum(peak_run, jnp.max(scores, -1))
    rescale = jnp.exp(peak_run - peak_new)
    weights = jnp.exp(scores - peak_new[..., None])
    total_new = total_run * rescale + jnp.sum(weights, -1)
    mixed_rows = jnp.einsum(
        "bngk,knd->bngd", weights.astype(jnp.bfloat16), val_rows, preferred_element_type=jnp.float32
    )
    return (peak_new, total_new, accum_rows * rescale[..., None] + mixed_rows)


def expert_trade(buffer):
    return lax.all_to_all(buffer, ("ctx", "exp"), split_axis=0, concat_axis=0, tiled=True)


def local_routed(
    resid,
    query,
    key,
    value,
    out_proj,
    norm_gain,
    w_gate,
    w_up,
    w_down,
    routes,
    gate_weights,
    grad_out,
):
    ctx_count = lax.axis_size("ctx")
    exp_count = lax.axis_size("exp")
    ctx_index = lax.axis_index("ctx")
    seq_rows = query.shape[0]
    kv_heads = key.shape[1] // HEAD_SIZE
    group_width = query.shape[1] // HEAD_SIZE // kv_heads
    seq_total = seq_rows * ctx_count
    score_scale = HEAD_SIZE ** (-0.5)
    query_start = ctx_index * seq_rows
    query_pos = query_start + jnp.arange(seq_rows, dtype=jnp.int32)
    queries = query.reshape(seq_rows, kv_heads, group_width, HEAD_SIZE)
    state_shape = (seq_rows, kv_heads, group_width)
    start_state = (
        jnp.full(state_shape, NEG, jnp.float32),
        jnp.zeros(state_shape, jnp.float32),
        jnp.zeros(state_shape + (HEAD_SIZE,), jnp.float32),
    )
    block_len = min(512, seq_total)
    keys_flat, values_flat = (
        lax.all_gather(key, "ctx", axis=0, tiled=True),
        lax.all_gather(value, "ctx", axis=0, tiled=True),
    )
    keys_all = keys_flat.reshape(seq_total, kv_heads, HEAD_SIZE)
    values_all = values_flat.reshape(seq_total, kv_heads, HEAD_SIZE)
    block_count = (query_start + seq_rows + block_len - 1) // block_len

    def forward_turn(loop_turn, soft_state):
        row_begin = loop_turn * block_len
        key_rows = lax.dynamic_slice_in_dim(keys_all, row_begin, block_len, 0)
        val_rows = lax.dynamic_slice_in_dim(values_all, row_begin, block_len, 0)
        return attend_block(
            soft_state, queries, key_rows, val_rows, row_begin, query_pos, score_scale
        )

    soft_state = lax.fori_loop(0, block_count, forward_turn, start_state)
    peak_val, total_val, accum_rows = soft_state
    attention_quad = (accum_rows / total_val[..., None]).astype(jnp.bfloat16)
    attn_mix = attention_quad.reshape(seq_rows, kv_heads * group_width * HEAD_SIZE)
    log_sum_total = peak_val + jnp.log(total_val)
    proj_full = lax.all_gather(out_proj, "ctx", axis=1, tiled=True)
    tok_rows = resid.shape[0]
    proj_sum = lax.psum_scatter(
        jnp.dot(attn_mix, proj_full, preferred_element_type=jnp.float32).astype(jnp.bfloat16),
        "exp",
        scatter_dimension=0,
        tiled=True,
    ).astype(jnp.float32)
    hidden = (resid.astype(jnp.float32) + proj_sum).astype(jnp.bfloat16)
    hidden_f = hidden.astype(jnp.float32)
    inv_rms = lax.rsqrt(jnp.mean(hidden_f * hidden_f, -1, keepdims=True) + EPS)
    unit_rows = hidden_f * inv_rms
    normed = (unit_rows * norm_gain).astype(jnp.bfloat16)
    top_count = routes.shape[1]
    model_width = normed.shape[1]
    experts_local = w_gate.shape[0]
    device_count = ctx_count * exp_count
    expert_total = experts_local * device_count
    capacity = 2 * tok_rows * top_count // expert_total
    flat_routes = routes.reshape(-1)
    member = (flat_routes[:, None] == jnp.arange(expert_total, dtype=jnp.int32)[None, :]).astype(
        jnp.int32
    )
    slot_pos = jnp.sum(jnp.cumsum(member, 0) * member, 1) - 1
    dest_row = flat_routes * capacity + slot_pos
    pair_weights = gate_weights.reshape(-1)

    def place_rows(rows_out):
        return (
            jnp.zeros((expert_total * capacity, model_width), jnp.bfloat16)
            .at[dest_row]
            .set(rows_out)
        )

    def to_experts(buffer):
        return (
            buffer.reshape(device_count, experts_local, capacity, model_width)
            .transpose(1, 0, 2, 3)
            .reshape(experts_local, device_count * capacity, model_width)
        )

    def from_experts(rows_back):
        return (
            rows_back.reshape(experts_local, device_count, capacity, model_width)
            .transpose(1, 0, 2, 3)
            .reshape(device_count * experts_local * capacity, model_width)
        )

    rows_in = to_experts(expert_trade(place_rows(jnp.repeat(normed, top_count, 0))))
    pre_gate = jnp.einsum("erd,edf->erf", rows_in, w_gate, preferred_element_type=jnp.float32)
    pre_up = jnp.einsum("erd,edf->erf", rows_in, w_up, preferred_element_type=jnp.float32)
    sig_gate = jax.nn.sigmoid(pre_gate)
    act_rows = (pre_gate * sig_gate * pre_up).astype(jnp.bfloat16)
    out_rows = jnp.einsum(
        "erf,efd->erd", act_rows, w_down, preferred_element_type=jnp.float32
    ).astype(jnp.bfloat16)
    back_rows = expert_trade(from_experts(out_rows))
    returned = back_rows[dest_row].astype(jnp.float32)
    moe_sum = jnp.sum(
        (returned * pair_weights[:, None]).reshape(tok_rows, top_count, model_width), 1
    )
    layer_out = (hidden_f + moe_sum).astype(jnp.bfloat16)
    grad_f = grad_out.astype(jnp.float32)
    pair_grad = (jnp.repeat(grad_f, top_count, 0) * pair_weights[:, None]).astype(jnp.bfloat16)
    grad_in = to_experts(expert_trade(place_rows(pair_grad)))
    act_grad = jnp.einsum("erd,efd->erf", grad_in, w_down, preferred_element_type=jnp.float32)
    grad_w_down = jnp.einsum(
        "erf,erd->efd", act_rows, grad_in, preferred_element_type=jnp.float32
    ).astype(jnp.bfloat16)
    up_grad = (act_grad * pre_gate * sig_gate).astype(jnp.bfloat16)
    gate_grad = (act_grad * pre_up * sig_gate * (1.0 + pre_gate * (1.0 - sig_gate))).astype(
        jnp.bfloat16
    )
    grad_w_gate = jnp.einsum(
        "erd,erf->edf", rows_in, gate_grad, preferred_element_type=jnp.float32
    ).astype(jnp.bfloat16)
    grad_w_up = jnp.einsum(
        "erd,erf->edf", rows_in, up_grad, preferred_element_type=jnp.float32
    ).astype(jnp.bfloat16)
    row_grad = (
        jnp.einsum("erf,edf->erd", gate_grad, w_gate, preferred_element_type=jnp.float32)
        + jnp.einsum("erf,edf->erd", up_grad, w_up, preferred_element_type=jnp.float32)
    ).astype(jnp.bfloat16)
    back_grad = expert_trade(from_experts(row_grad))
    normed_grad = jnp.sum(
        back_grad[dest_row].astype(jnp.float32).reshape(tok_rows, top_count, model_width), 1
    )
    gain_part = jnp.sum(normed_grad * unit_rows, 0)
    grad_gain = lax.psum(gain_part, ("ctx", "exp"))
    scaled_grad = norm_gain * normed_grad
    hidden_grad = inv_rms * (
        scaled_grad - unit_rows * jnp.mean(scaled_grad * unit_rows, -1, keepdims=True)
    )
    grad_resid = (grad_f + hidden_grad).astype(jnp.bfloat16)
    block_grad = lax.all_gather(grad_resid, "exp", axis=0, tiled=True)
    mixture_gradient = jnp.einsum(
        "td,hd->th", block_grad, proj_full, preferred_element_type=jnp.float32
    ).astype(jnp.bfloat16)
    proj_part = jnp.einsum("th,td->hd", attn_mix, block_grad, preferred_element_type=jnp.float32)
    grad_out_proj = lax.psum_scatter(
        proj_part.astype(jnp.bfloat16), "ctx", scatter_dimension=1, tiled=True
    )
    mixture_quad = mixture_gradient.reshape(seq_rows, kv_heads, group_width, HEAD_SIZE)
    delta_sum = jnp.sum(mixture_quad.astype(jnp.float32) * attention_quad.astype(jnp.float32), -1)
    back_count = (query_start + seq_rows + block_len - 1) // block_len

    def backward_turn(loop_turn, loop_carry):
        query_grad, pair_store = loop_carry
        row_begin = loop_turn * block_len
        key_rows = lax.dynamic_slice_in_dim(keys_all, row_begin, block_len, 0)
        val_rows = lax.dynamic_slice_in_dim(values_all, row_begin, block_len, 0)
        scores = (
            jnp.einsum("bngd,knd->bngk", queries, key_rows, preferred_element_type=jnp.float32)
            * score_scale
        )
        key_pos = row_begin + jnp.arange(block_len, dtype=jnp.int32)
        visible = key_pos[None, :] <= query_pos[:, None]
        prob_full = jnp.where(
            visible[:, None, None, :], jnp.exp(scores - log_sum_total[..., None]), 0.0
        )
        prob_grad = jnp.einsum(
            "bngd,knd->bngk", mixture_quad, val_rows, preferred_element_type=jnp.float32
        )
        score_grad = prob_full * (prob_grad - delta_sum[..., None])
        prob_half = prob_full.astype(jnp.bfloat16)
        score_half = score_grad.astype(jnp.bfloat16)
        query_grad = (
            query_grad
            + jnp.einsum("bngk,knd->bngd", score_half, key_rows, preferred_element_type=jnp.float32)
            * score_scale
        )
        key_grad = (
            jnp.einsum("bngk,bngd->knd", score_half, queries, preferred_element_type=jnp.float32)
            * score_scale
        )
        value_grad = jnp.einsum(
            "bngk,bngd->knd", prob_half, mixture_quad, preferred_element_type=jnp.float32
        )
        pair_store = lax.dynamic_update_slice_in_dim(
            pair_store, jnp.stack([key_grad, value_grad], 2), row_begin, 0
        )
        return (query_grad, pair_store)

    start_back = (
        jnp.zeros(state_shape + (HEAD_SIZE,), jnp.float32),
        jnp.zeros((seq_total, kv_heads, 2, HEAD_SIZE), jnp.float32),
    )
    query_grad, pair_store = lax.fori_loop(0, back_count, backward_turn, start_back)
    grad_query = query_grad.reshape(seq_rows, kv_heads * group_width * HEAD_SIZE).astype(
        jnp.bfloat16
    )
    pair_sum = lax.psum_scatter(
        pair_store.reshape(seq_total, kv_heads * 2 * HEAD_SIZE).astype(jnp.bfloat16),
        "ctx",
        scatter_dimension=0,
        tiled=True,
    ).astype(jnp.float32)
    pair_sum = pair_sum.reshape(seq_rows, kv_heads, 2, HEAD_SIZE)
    key_gradient = pair_sum[:, :, 0].reshape(seq_rows, kv_heads * HEAD_SIZE).astype(jnp.bfloat16)
    value_gradient = pair_sum[:, :, 1].reshape(seq_rows, kv_heads * HEAD_SIZE).astype(jnp.bfloat16)
    return (
        layer_out,
        grad_resid,
        grad_query,
        key_gradient,
        value_gradient,
        grad_out_proj,
        grad_gain,
        grad_w_gate,
        grad_w_up,
        grad_w_down,
    )


F32 = jnp.float32
BF16 = jnp.bfloat16
LOG2E = 1.4426950408889634
SETS = (0, 2, 1, 3)


def crossed(x, bits):
    return lax.ppermute(x, "ctx", [(i, i ^ bits) for i in range(4)])


def swapped(x, bits):
    return lax.ppermute(x, "exp", [(i, i ^ bits) for i in range(4)])


def after(x, *others):
    return lax.optimization_barrier((x, *others))[0]


def from_all(x):
    far, near = crossed(x, 2), crossed(x, 1)
    return [x, near, far, crossed(far, 1)]


def pick(x, index, axis):
    return lax.dynamic_index_in_dim(x, index, axis, keepdims=False)


def nt(a, b):
    return lax.dot_general(a, b, (((1,), (1,)), ((), ())), preferred_element_type=F32)


def tn(a, b):
    return lax.dot_general(a, b, (((0,), (0,)), ((), ())), preferred_element_type=F32)


def nn(a, b):
    return lax.dot_general(a, b, (((1,), (0,)), ((), ())), preferred_element_type=F32)


def run_kernel(body, name, place, args, outs, scratch=(), flops=0, limit=40):
    vmem = pl.BlockSpec(memory_space=pltpu.VMEM)
    shapes = [jax.ShapeDtypeStruct(shape, dtype) for shape, dtype in outs]
    moved = sum(x.size * x.dtype.itemsize for x in list(args) + shapes)
    return pl.pallas_call(
        body,
        in_specs=[pl.BlockSpec(memory_space=pltpu.SMEM)] + [vmem] * len(args),
        out_specs=[vmem] * len(outs),
        out_shape=shapes,
        scratch_shapes=[pltpu.VMEM(shape, dtype) for shape, dtype in scratch],
        compiler_params=pltpu.CompilerParams(vmem_limit_bytes=limit << 20),
        cost_estimate=pl.CostEstimate(flops=flops, bytes_accessed=moved, transcendentals=0),
        name=name,
    )(place, *args)


def visible_keys(rows, count, query_block, base):
    shape = (rows, count * rows)
    key_pos = lax.broadcasted_iota(jnp.int32, shape, 1)
    turn = sum([(key_pos >= i * rows).astype(jnp.int32) for i in range(1, count)])
    offset = key_pos - turn * rows
    diagonal = offset <= lax.broadcasted_iota(jnp.int32, shape, 0)
    block = turn ^ base
    return (block < query_block) | ((block == query_block) & diagonal)


def attend(place, turn, query, pairs, out_proj):
    n = len(pairs)
    rows, width = query.shape
    tok = rows // 4
    cols = out_proj.shape[1]
    heads = width // HEAD_SIZE
    factor = HEAD_SIZE ** (-0.5) * LOG2E

    def body(place_ref, query_ref, *refs):
        proj_ref, mix_ref, keep_ref, send_ref, ks, vs, ps = refs[n:]
        c, e = place_ref[0], place_ref[1]
        for r in range(n):
            ks[r * rows : (r + 1) * rows, :] = refs[r][:, :HEAD_SIZE]
            vs[r * rows : (r + 1) * rows, :] = refs[r][:, HEAD_SIZE:]
        visible = visible_keys(rows, n, c ^ turn, c)
        for head in range(heads):
            at = slice(head * HEAD_SIZE, (head + 1) * HEAD_SIZE)
            scores = jnp.where(visible, nt(query_ref[:, at], ks[...]), NEG)
            peak = jnp.max(scores, -1, keepdims=True)
            weights = jnp.exp2((scores - peak) * factor)
            total = jnp.sum(weights, -1, keepdims=True)
            mix_ref[:, at] = (nn(weights.astype(BF16), vs[...]) / total).astype(BF16)
        ps[...] = nn(mix_ref[...], proj_ref[...]).astype(BF16)
        for x in range(2):
            same, other = e ^ (2 * x), e ^ (2 * x + 1)
            keep_ref[x] = ps[pl.ds(pl.multiple_of(same * tok, tok), tok), :]
            send_ref[x] = ps[pl.ds(pl.multiple_of(other * tok, tok), tok), :]

    return run_kernel(
        body,
        "attend",
        place,
        [query, *pairs, out_proj],
        [((rows, width), BF16), ((2, tok, cols), BF16), ((2, tok, cols), BF16)],
        [((n * rows, HEAD_SIZE), BF16), ((n * rows, HEAD_SIZE), BF16), ((rows, cols), BF16)],
        flops=4 * rows * n * rows * width,
    )


def hidden_rows(place, keep, received, line, resid_parts):
    n = len(resid_parts)

    def body(place_ref, *refs):
        for d in range(n):
            total = refs[d][0].astype(F32) + refs[n + d][0].astype(F32)
            total = total + refs[2 * n + d][...].astype(F32) + refs[3 * n + d][...].astype(F32)
            refs[4 * n][d] = total.astype(BF16)

    return run_kernel(
        body,
        "hidden_rows",
        place,
        [*keep, *received, *line, *resid_parts],
        [((n, *line[0].shape), BF16)],
    )[0]


def grad_rows_of(place, grad_sets, w_down, width):
    n, tok = len(grad_sets[0]), grad_sets[0][0].shape[0]
    total = 4 * n * tok
    experts = 4 * n

    def body(place_ref, *refs):
        down_ref, rows_ref, gate_ref, act_ref = refs[4 * n :]
        expert = place_ref[0] * 4 + place_ref[1]
        lane = lax.broadcasted_iota(jnp.int32, (tok, 128), 1)
        wanted = (lane == expert) | (lane == expert + experts)
        for s in range(4 * n):
            at = slice(s * tok, (s + 1) * tok)
            gate = jnp.where(wanted, refs[s][:, width:].astype(F32), 0.0)
            gate = jnp.sum(gate, -1, keepdims=True)
            gate_ref[at, :] = gate
            rows_ref[at, :] = (refs[s][:, :width].astype(F32) * gate).astype(BF16)
        act_ref[...] = nt(rows_ref[...], down_ref[...])

    return run_kernel(
        body,
        "grad_rows",
        place,
        [*sum(grad_sets, []), w_down],
        [((total, width), BF16), ((total, 1), F32), ((total, w_down.shape[0]), F32)],
        flops=2 * total * width * w_down.shape[0],
    )


def expert_rows(place, hidden_sets, act_grad, norm_gain, w_gate, w_up):
    n, tok, cols = hidden_sets[0][0].shape
    width, hidden_units = w_gate.shape
    group = n * tok
    total = 4 * group

    def body(place_ref, *refs):
        pieces = refs[: 4 * n]
        act_grad_ref, gain_ref, gate_ref, up_ref = refs[4 * n : 4 * n + 4]
        normed_ref, act_ref, gate_grad_ref, up_grad_ref, own_ref = refs[4 * n + 4 : 4 * n + 9]
        grads, hid = refs[4 * n + 9 : 4 * n + 13], refs[4 * n + 13]
        c = place_ref[0]
        for s in range(4):
            for d in range(n):
                at = pl.multiple_of((c ^ d) * cols, cols)
                for t in range(n):
                    row = s * group + (d ^ t) * tok
                    hid[row : row + tok, pl.ds(at, cols)] = pieces[s * n + d][t]
            rows = slice(s * group, (s + 1) * group)
            value = hid[rows, :].astype(F32)
            inv_rms = lax.rsqrt(jnp.mean(value * value, -1, keepdims=True) + EPS)
            normed_ref[rows, :] = (value * inv_rms * gain_ref[...]).astype(BF16)
        own_ref[...] = hid[:tok, :]
        pre_gate = nn(normed_ref[...], gate_ref[...])
        pre_up = nn(normed_ref[...], up_ref[...])
        sig = jax.nn.sigmoid(pre_gate)
        act_ref[...] = (pre_gate * sig * pre_up).astype(BF16)
        act_grad_value = act_grad_ref[...]
        up_grad_ref[...] = (act_grad_value * pre_gate * sig).astype(BF16)
        gate_grad_ref[...] = (
            act_grad_value * pre_up * sig * (1.0 + pre_gate * (1.0 - sig))
        ).astype(BF16)
        for j in range(n):
            at = slice(j * cols, (j + 1) * cols)
            part = nt(gate_grad_ref[...], gate_ref[at, :]) + nt(up_grad_ref[...], up_ref[at, :])
            for s in range(4):
                block = part[s * group : (s + 1) * group].astype(BF16)
                grads[s][:, :, at] = block.reshape(n, tok, cols)

    units = ((total, hidden_units), BF16)
    return run_kernel(
        body,
        "expert_rows",
        place,
        [*sum(hidden_sets, []), act_grad, norm_gain.reshape(1, width), w_gate, w_up],
        [((total, width), BF16), units, units, units, ((tok, width), BF16)]
        + [((n, tok, width), BF16)] * 4,
        [((total, width), BF16)],
        flops=8 * total * width * hidden_units,
    )


def weighted_rows(place, act_rows, gate, w_down, n):
    total = act_rows.shape[0]
    width = w_down.shape[1]
    group, cols = total // 4, width // n

    def body(place_ref, act_ref, gate_ref, down_ref, *outs):
        for j in range(n):
            at = slice(j * cols, (j + 1) * cols)
            part = nn(act_ref[...], down_ref[:, at]).astype(BF16).astype(F32) * gate_ref[...]
            for s in range(4):
                block = part[s * group : (s + 1) * group].astype(BF16)
                outs[s][:, :, at] = block.reshape(n, group // n, cols)

    return run_kernel(
        body,
        "weighted_rows",
        place,
        [act_rows, gate, w_down],
        [((n, group // n, width), BF16)] * 4,
        flops=2 * total * width * w_down.shape[0],
    )


def sum_back(parts, before_exp=(), before_ctx=(), beside=()):
    def add(*xs):
        return sum([x.astype(F32) for x in xs[1:]], xs[0].astype(F32)).astype(BF16)

    if before_exp:
        parts = [after(x, *before_exp) for x in parts]
    far, near = swapped(parts[3], 1), swapped(parts[2], 1)
    line = {}
    for j in (3, 2, 1, 0):
        part = add(parts[1][j], far[j])
        if j == 1:
            part = after(part, line[3], *beside)
        elif j == 0:
            part = after(part, line[2])
        line[j] = swapped(part, 2)
    sums = [add(parts[0][j], near[j], line[j]) for j in range(4)]
    if before_ctx:
        sums = [after(x, *before_ctx) for x in sums]
    return [sums[0]] + [crossed(sums[j], j) for j in (1, 2, 3)]


def norm_backward(place, summed, hidden, grad_out, norm_gain, cols):
    n = len(summed)
    tok, width = hidden.shape
    blocks = width // cols

    def body(place_ref, *refs):
        hidden_ref, grad_ref, gain_ref = refs[n : n + 3]
        out_ref, part_ref, cuts = refs[n + 3], refs[n + 4], refs[n + 5 :]
        c = place_ref[0]
        normed_grad = sum([r[...].astype(F32) for r in refs[1:n]], refs[0][...].astype(F32))
        value = hidden_ref[...].astype(F32)
        inv_rms = lax.rsqrt(jnp.mean(value * value, -1, keepdims=True) + EPS)
        unit_rows = value * inv_rms
        part_ref[...] = jnp.sum(normed_grad * unit_rows, 0, keepdims=True)
        scaled = gain_ref[...] * normed_grad
        mean = jnp.mean(scaled * unit_rows, -1, keepdims=True)
        grad = grad_ref[...].astype(F32) + inv_rms * (scaled - unit_rows * mean)
        out_ref[...] = grad.astype(BF16)
        for d in range(blocks):
            cuts[d][...] = out_ref[:, pl.ds(pl.multiple_of((c ^ d) * cols, cols), cols)]

    return run_kernel(
        body,
        "norm_backward",
        place,
        [*summed, hidden, grad_out, norm_gain.reshape(1, width)],
        [((tok, width), BF16), ((1, width), F32)] + [((tok, cols), BF16)] * blocks,
    )


def layer_rows(place, summed, hidden):
    def body(place_ref, *refs):
        total = refs[-2][...].astype(F32)
        for r in refs[:-2]:
            total = total + r[...].astype(F32)
        refs[-1][...] = total.astype(BF16)

    return run_kernel(body, "layer_rows", place, [*summed, hidden], [(hidden.shape, BF16)])[0]


def mix_grad_parts(place, cut_sets, out_proj):
    n, tok, cols = cut_sets[0].shape
    rows, width = 4 * tok, out_proj.shape[0]

    def body(place_ref, *refs):
        proj_ref, outs, grads = refs[4], refs[5 : 5 + n], refs[5 + n]
        e = place_ref[1]
        for d in range(n):
            for r in range(4):
                at = pl.multiple_of(d * rows + (e ^ r) * tok, tok)
                grads[pl.ds(at, tok), :] = refs[r][d]
        for half in range(2):
            at = slice(half * width // 2, (half + 1) * width // 2)
            part = nt(grads[...], proj_ref[at, :]).astype(BF16)
            for d in range(n):
                outs[d][:, at] = part[d * rows : (d + 1) * rows]

    return run_kernel(
        body,
        "mix_grad_parts",
        place,
        [*cut_sets, out_proj],
        [((rows, width), BF16)] * n,
        [((n * rows, cols), BF16)],
        flops=2 * n * rows * cols * width,
    )


def attend_backward(place, grad_parts, query, pairs, mix):
    n, g = len(pairs), len(grad_parts)
    rows, width = mix.shape
    heads = width // HEAD_SIZE
    scale = HEAD_SIZE ** (-0.5)

    def body(place_ref, *refs):
        g_refs, query_ref = refs[:g], refs[g]
        p_refs = refs[g + 1 : g + 1 + n]
        mix_ref, dq_ref = refs[g + 1 + n : g + 3 + n]
        outs = refs[g + 3 + n : g + 3 + 2 * n]
        qs, ms, ks, vs, score_half, prob_half = refs[g + 3 + 2 * n :]
        c = place_ref[0]
        visible = visible_keys(rows, n, c, c)
        for d in range(n):
            ks[d * rows : (d + 1) * rows, :] = p_refs[d][:, :HEAD_SIZE]
            vs[d * rows : (d + 1) * rows, :] = p_refs[d][:, HEAD_SIZE:]
        for head in range(heads):
            at = slice(head * HEAD_SIZE, (head + 1) * HEAD_SIZE)
            rs = slice(head * rows, (head + 1) * rows)
            grad = sum([x[:, at].astype(F32) for x in g_refs[1:]], g_refs[0][:, at].astype(F32))
            grad = grad.astype(BF16)
            qs[rs, :] = query_ref[:, at]
            ms[rs, :] = grad
            scores = jnp.where(visible, nt(query_ref[:, at], ks[...]), NEG)
            peak = jnp.max(scores, -1, keepdims=True)
            weights = jnp.exp2((scores - peak) * (scale * LOG2E))
            prob = weights * (1.0 / jnp.sum(weights, -1, keepdims=True))
            delta = jnp.sum(grad.astype(F32) * mix_ref[:, at].astype(F32), -1, keepdims=True)
            score_half[rs, :] = (prob * (nt(grad, vs[...]) - delta)).astype(BF16)
            prob_half[rs, :] = prob.astype(BF16)
            dq_ref[:, at] = (nn(score_half[rs, :], ks[...]) * scale).astype(BF16)
        key_sum = (tn(score_half[...], qs[...]) * scale).astype(BF16)
        value_sum = tn(prob_half[...], ms[...]).astype(BF16)
        for j in range(n):
            rs = slice(j * rows, (j + 1) * rows)
            outs[j][:, :HEAD_SIZE] = key_sum[rs]
            outs[j][:, HEAD_SIZE:] = value_sum[rs]

    stacked = ((heads * rows, HEAD_SIZE), BF16)
    keys = ((n * rows, HEAD_SIZE), BF16)
    halves = ((heads * rows, n * rows), BF16)
    return run_kernel(
        body,
        "attend_backward",
        place,
        [*grad_parts, query, *pairs, mix],
        [((rows, width), BF16)] + [((rows, 2 * HEAD_SIZE), BF16)] * n,
        [stacked, stacked, keys, keys, halves, halves],
        flops=10 * rows * width * n * rows,
    )


def proj_grad(place, mixes, cut_sets):
    n, tok, cols = cut_sets[0].shape
    rows, width = mixes[0].shape

    def body(place_ref, *refs):
        out_ref, grads, mix = refs[n + 4 :]
        e = place_ref[1]
        for d in range(n):
            mix[d * rows : (d + 1) * rows, :] = refs[d][...]
            for r in range(4):
                at = pl.multiple_of(d * rows + (e ^ r) * tok, tok)
                grads[pl.ds(at, tok), :] = refs[n + r][d]
        out_ref[...] = tn(mix[...], grads[...]).astype(BF16)

    return run_kernel(
        body,
        "proj_grad",
        place,
        [*mixes, *cut_sets],
        [((width, cols), BF16)],
        [((n * rows, cols), BF16), ((n * rows, width), BF16)],
        flops=8 * n * tok * cols * width,
    )[0]


def local_dense(
    resid,
    query,
    key,
    value,
    out_proj,
    norm_gain,
    w_gate,
    w_up,
    w_down,
    routes,
    gate_weights,
    grad_out,
):
    n = lax.axis_size("ctx")
    c, e = lax.axis_index("ctx"), lax.axis_index("exp")
    place = jnp.stack([c, e]).astype(jnp.int32)
    tok, width = resid.shape
    cols = out_proj.shape[1]
    experts = 4 * n
    scope = jax.named_scope

    def across(blocks):
        return [blocks[0]] + [crossed(blocks[r], r) for r in range(1, n)]

    with scope("gather_pairs"):
        pairs = from_all(jnp.concatenate([key, value], 1))
    with scope("gather_queries"):
        queries = from_all(query)

    gates = jnp.sum(
        jnp.where(
            routes[:, :, None] == jnp.arange(experts, dtype=jnp.int32), gate_weights[:, :, None], 0.0
        ),
        1,
    )
    gate_high = lax.reduce_precision(gates, 8, 7)
    payload = jnp.concatenate(
        [
            grad_out,
            gate_high.astype(BF16),
            (gates - gate_high).astype(BF16),
            jnp.zeros((tok, 128 - 2 * experts), BF16),
        ],
        1,
    )
    with scope("gather_resid"):
        resid_cut = resid.reshape(tok, n, cols)
        resid_parts = across([pick(resid_cut, c ^ r, 1) for r in range(n)])
    with scope("gather_grads"):
        grad_own = from_all(after(payload, *queries[1:3]))
        grad_line = [swapped(payload, 2)] + [swapped(x, 2) for x in grad_own[1:]]
        grad_sets = [grad_own, grad_line] + [
            [swapped(x, 1) for x in xs] for xs in (grad_own, grad_line)
        ]
    grad_rows, gate, act_grad = grad_rows_of(place, grad_sets, w_down[0], width)

    mixes, keep, send = zip(*[attend(place, r, queries[r], pairs, out_proj) for r in range(n)])
    with scope("sum_heads"):
        received = [swapped(x, 1) for x in send]
        sums = [(k[1].astype(F32) + r[1].astype(F32)).astype(BF16) for k, r in zip(keep, received)]
        sums[3] = after(sums[3], *grad_own[1:3])
        line = [swapped(x, 2) for x in sums]
    hidden_block = hidden_rows(place, keep, received, line, resid_parts)
    with scope("gather_hidden"):
        hidden_own = from_all(after(hidden_block, grad_own[3], *grad_line[:3]))
        hidden_line = [swapped(x, 2) for x in hidden_own]
        hidden_line[-1], act_grad = lax.optimization_barrier((hidden_line[-1], act_grad))
        hidden_sets = [hidden_own, hidden_line] + [
            [swapped(x, 1) for x in xs] for xs in (hidden_own, hidden_line)
        ]

    normed, act_rows, gate_grad, up_grad, hidden, *row_grads = expert_rows(
        place, hidden_sets, act_grad, norm_gain, w_gate[0], w_up[0]
    )
    weighted = weighted_rows(place, act_rows, gate, w_down[0], n)
    with scope("sum_row_grads"):
        summed = sum_back(row_grads, beside=weighted[:1])
    grad_resid, gain_part, *cuts = norm_backward(place, summed, hidden, grad_out, norm_gain, cols)

    with scope("gather_cuts"):
        cut_own = jnp.stack(across(cuts))
        cut_line = swapped(cut_own, 2)
        cut_sets = [cut_own, swapped(cut_own, 1), cut_line, swapped(cut_line, 1)]
    mix_parts = mix_grad_parts(place, cut_sets, out_proj)
    with scope("sum_mix_grad"):
        second = (mix_parts[2].astype(F32) + crossed(mix_parts[3], 1).astype(F32)).astype(BF16)
        mix_grads = [mix_parts[0], crossed(mix_parts[1], 1), crossed(second, 2)]

    normed, act_rows, cut_own = lax.optimization_barrier((normed, act_rows, cut_own, mix_parts[3]))[:3]
    cut_sets[0] = cut_own
    grad_w_gate = tn(normed, gate_grad).astype(BF16)
    grad_w_up = tn(normed, up_grad).astype(BF16)
    grad_w_down = tn(act_rows, grad_rows).astype(BF16)
    grad_out_proj = proj_grad(place, mixes, cut_sets)
    mix_grads[0] = after(mix_grads[0], grad_w_gate, grad_w_up, grad_out_proj)

    grad_query, *pair_parts = attend_backward(place, mix_grads, query, pairs, mixes[0])
    with scope("sum_pairs"):
        pair_parts = across(pair_parts)
        pair_sum = sum([x.astype(F32) for x in pair_parts[1:]], pair_parts[0].astype(F32)).astype(BF16)

    with scope("sum_gain"):
        grad_gain = after(gain_part.reshape(-1, 128), mix_parts[3])
        for bit in (1, 2):
            grad_gain = grad_gain + swapped(grad_gain, bit)
        grad_gain = sum(across([grad_gain] * n)[1:], grad_gain).reshape(width)

    with scope("sum_outputs"):
        layer_out = layer_rows(place, sum_back(weighted, summed[:1], summed[1:]), hidden)
    return (
        layer_out,
        grad_resid,
        grad_query,
        pair_sum[:, :HEAD_SIZE],
        pair_sum[:, HEAD_SIZE:],
        grad_out_proj,
        grad_gain,
        grad_w_gate[None],
        grad_w_up[None],
        grad_w_down[None],
    )


def local(*args):
    key, w_gate, routes = args[2], args[6], args[9]
    ctx_count, exp_count = lax.axis_size("ctx"), lax.axis_size("exp")
    expert_total = w_gate.shape[0] * ctx_count * exp_count
    dense = (
        2 * routes.shape[1] >= expert_total
        and w_gate.shape[0] == 1
        and key.shape[1] == HEAD_SIZE
        and exp_count == 4
        and ctx_count == 4
        and lax.axis_size("groups") == 2
    )
    return (local_dense if dense else local_routed)(*args)


def solution(mesh):
    in_specs = (
        P(("groups", "ctx", "exp"), None),
        P(("groups", "ctx"), "exp"),
        P(("groups", "ctx"), "exp"),
        P(("groups", "ctx"), "exp"),
        P("exp", "ctx"),
        P(),
        P(("ctx", "exp"), None, None),
        P(("ctx", "exp"), None, None),
        P(("ctx", "exp"), None, None),
        P(("groups", "ctx", "exp"), None),
        P(("groups", "ctx", "exp"), None),
        P(("groups", "ctx", "exp"), None),
    )
    out_specs = (
        P(("groups", "ctx", "exp"), None),
        P(("groups", "ctx", "exp"), None),
        P(("groups", "ctx"), "exp"),
        P(("groups", "ctx"), "exp"),
        P(("groups", "ctx"), "exp"),
        P(("groups", "exp"), "ctx"),
        P("groups"),
        P(("groups", "ctx", "exp"), None, None),
        P(("groups", "ctx", "exp"), None, None),
        P(("groups", "ctx", "exp"), None, None),
    )
    return jax.shard_map(local, mesh=mesh, in_specs=in_specs, out_specs=out_specs, check_vma=False)
```

```python
import jax
import jax.numpy as jnp
from jax import lax
from jax.experimental import pallas as pl
from jax.experimental.pallas import tpu as pltpu
from jax.sharding import PartitionSpec as P

HEAD_SIZE = 128


EPS = 1e-06
NEG = -1e30


def attend_block(soft_state, queries, key_rows, val_rows, row_begin, query_pos, score_scale):
    peak_run, total_run, accum_rows = soft_state
    scores = (
        jnp.einsum("bngd,knd->bngk", queries, key_rows, preferred_element_type=jnp.float32)
        * score_scale
    )
    key_pos = row_begin + jnp.arange(key_rows.shape[0], dtype=jnp.int32)
    visible = key_pos[None, :] <= query_pos[:, None]
    scores = jnp.where(visible[:, None, None, :], scores, NEG)
    peak_new = jnp.maximum(peak_run, jnp.max(scores, -1))
    rescale = jnp.exp(peak_run - peak_new)
    weights = jnp.exp(scores - peak_new[..., None])
    total_new = total_run * rescale + jnp.sum(weights, -1)
    mixed_rows = jnp.einsum(
        "bngk,knd->bngd", weights.astype(jnp.bfloat16), val_rows, preferred_element_type=jnp.float32
    )
    return (peak_new, total_new, accum_rows * rescale[..., None] + mixed_rows)


def expert_trade(buffer):
    return lax.all_to_all(buffer, ("ctx", "exp"), split_axis=0, concat_axis=0, tiled=True)


def local_routed(
    resid,
    query,
    key,
    value,
    out_proj,
    norm_gain,
    w_gate,
    w_up,
    w_down,
    routes,
    gate_weights,
    grad_out,
):
    ctx_count = lax.axis_size("ctx")
    exp_count = lax.axis_size("exp")
    ctx_index = lax.axis_index("ctx")
    seq_rows = query.shape[0]
    kv_heads = key.shape[1] // HEAD_SIZE
    group_width = query.shape[1] // HEAD_SIZE // kv_heads
    seq_total = seq_rows * ctx_count
    score_scale = HEAD_SIZE ** (-0.5)
    query_start = ctx_index * seq_rows
    query_pos = query_start + jnp.arange(seq_rows, dtype=jnp.int32)
    queries = query.reshape(seq_rows, kv_heads, group_width, HEAD_SIZE)
    state_shape = (seq_rows, kv_heads, group_width)
    start_state = (
        jnp.full(state_shape, NEG, jnp.float32),
        jnp.zeros(state_shape, jnp.float32),
        jnp.zeros(state_shape + (HEAD_SIZE,), jnp.float32),
    )
    block_len = min(512, seq_total)
    keys_flat, values_flat = (
        lax.all_gather(key, "ctx", axis=0, tiled=True),
        lax.all_gather(value, "ctx", axis=0, tiled=True),
    )
    keys_all = keys_flat.reshape(seq_total, kv_heads, HEAD_SIZE)
    values_all = values_flat.reshape(seq_total, kv_heads, HEAD_SIZE)
    block_count = (query_start + seq_rows + block_len - 1) // block_len

    def forward_turn(loop_turn, soft_state):
        row_begin = loop_turn * block_len
        key_rows = lax.dynamic_slice_in_dim(keys_all, row_begin, block_len, 0)
        val_rows = lax.dynamic_slice_in_dim(values_all, row_begin, block_len, 0)
        return attend_block(
            soft_state, queries, key_rows, val_rows, row_begin, query_pos, score_scale
        )

    soft_state = lax.fori_loop(0, block_count, forward_turn, start_state)
    peak_val, total_val, accum_rows = soft_state
    attention_quad = (accum_rows / total_val[..., None]).astype(jnp.bfloat16)
    attn_mix = attention_quad.reshape(seq_rows, kv_heads * group_width * HEAD_SIZE)
    log_sum_total = peak_val + jnp.log(total_val)
    proj_full = lax.all_gather(out_proj, "ctx", axis=1, tiled=True)
    tok_rows = resid.shape[0]
    proj_sum = lax.psum_scatter(
        jnp.dot(attn_mix, proj_full, preferred_element_type=jnp.float32).astype(jnp.bfloat16),
        "exp",
        scatter_dimension=0,
        tiled=True,
    ).astype(jnp.float32)
    hidden = (resid.astype(jnp.float32) + proj_sum).astype(jnp.bfloat16)
    hidden_f = hidden.astype(jnp.float32)
    inv_rms = lax.rsqrt(jnp.mean(hidden_f * hidden_f, -1, keepdims=True) + EPS)
    unit_rows = hidden_f * inv_rms
    normed = (unit_rows * norm_gain).astype(jnp.bfloat16)
    top_count = routes.shape[1]
    model_width = normed.shape[1]
    experts_local = w_gate.shape[0]
    device_count = ctx_count * exp_count
    expert_total = experts_local * device_count
    capacity = 2 * tok_rows * top_count // expert_total
    flat_routes = routes.reshape(-1)
    member = (flat_routes[:, None] == jnp.arange(expert_total, dtype=jnp.int32)[None, :]).astype(
        jnp.int32
    )
    slot_pos = jnp.sum(jnp.cumsum(member, 0) * member, 1) - 1
    dest_row = flat_routes * capacity + slot_pos
    pair_weights = gate_weights.reshape(-1)

    def place_rows(rows_out):
        return (
            jnp.zeros((expert_total * capacity, model_width), jnp.bfloat16)
            .at[dest_row]
            .set(rows_out)
        )

    def to_experts(buffer):
        return (
            buffer.reshape(device_count, experts_local, capacity, model_width)
            .transpose(1, 0, 2, 3)
            .reshape(experts_local, device_count * capacity, model_width)
        )

    def from_experts(rows_back):
        return (
            rows_back.reshape(experts_local, device_count, capacity, model_width)
            .transpose(1, 0, 2, 3)
            .reshape(device_count * experts_local * capacity, model_width)
        )

    rows_in = to_experts(expert_trade(place_rows(jnp.repeat(normed, top_count, 0))))
    pre_gate = jnp.einsum("erd,edf->erf", rows_in, w_gate, preferred_element_type=jnp.float32)
    pre_up = jnp.einsum("erd,edf->erf", rows_in, w_up, preferred_element_type=jnp.float32)
    sig_gate = jax.nn.sigmoid(pre_gate)
    act_rows = (pre_gate * sig_gate * pre_up).astype(jnp.bfloat16)
    out_rows = jnp.einsum(
        "erf,efd->erd", act_rows, w_down, preferred_element_type=jnp.float32
    ).astype(jnp.bfloat16)
    back_rows = expert_trade(from_experts(out_rows))
    returned = back_rows[dest_row].astype(jnp.float32)
    moe_sum = jnp.sum(
        (returned * pair_weights[:, None]).reshape(tok_rows, top_count, model_width), 1
    )
    layer_out = (hidden_f + moe_sum).astype(jnp.bfloat16)
    grad_f = grad_out.astype(jnp.float32)
    pair_grad = (jnp.repeat(grad_f, top_count, 0) * pair_weights[:, None]).astype(jnp.bfloat16)
    grad_in = to_experts(expert_trade(place_rows(pair_grad)))
    act_grad = jnp.einsum("erd,efd->erf", grad_in, w_down, preferred_element_type=jnp.float32)
    grad_w_down = jnp.einsum(
        "erf,erd->efd", act_rows, grad_in, preferred_element_type=jnp.float32
    ).astype(jnp.bfloat16)
    up_grad = (act_grad * pre_gate * sig_gate).astype(jnp.bfloat16)
    gate_grad = (act_grad * pre_up * sig_gate * (1.0 + pre_gate * (1.0 - sig_gate))).astype(
        jnp.bfloat16
    )
    grad_w_gate = jnp.einsum(
        "erd,erf->edf", rows_in, gate_grad, preferred_element_type=jnp.float32
    ).astype(jnp.bfloat16)
    grad_w_up = jnp.einsum(
        "erd,erf->edf", rows_in, up_grad, preferred_element_type=jnp.float32
    ).astype(jnp.bfloat16)
    row_grad = (
        jnp.einsum("erf,edf->erd", gate_grad, w_gate, preferred_element_type=jnp.float32)
        + jnp.einsum("erf,edf->erd", up_grad, w_up, preferred_element_type=jnp.float32)
    ).astype(jnp.bfloat16)
    back_grad = expert_trade(from_experts(row_grad))
    normed_grad = jnp.sum(
        back_grad[dest_row].astype(jnp.float32).reshape(tok_rows, top_count, model_width), 1
    )
    gain_part = jnp.sum(normed_grad * unit_rows, 0)
    grad_gain = lax.psum(gain_part, ("ctx", "exp"))
    scaled_grad = norm_gain * normed_grad
    hidden_grad = inv_rms * (
        scaled_grad - unit_rows * jnp.mean(scaled_grad * unit_rows, -1, keepdims=True)
    )
    grad_resid = (grad_f + hidden_grad).astype(jnp.bfloat16)
    block_grad = lax.all_gather(grad_resid, "exp", axis=0, tiled=True)
    mixture_gradient = jnp.einsum(
        "td,hd->th", block_grad, proj_full, preferred_element_type=jnp.float32
    ).astype(jnp.bfloat16)
    proj_part = jnp.einsum("th,td->hd", attn_mix, block_grad, preferred_element_type=jnp.float32)
    grad_out_proj = lax.psum_scatter(
        proj_part.astype(jnp.bfloat16), "ctx", scatter_dimension=1, tiled=True
    )
    mixture_quad = mixture_gradient.reshape(seq_rows, kv_heads, group_width, HEAD_SIZE)
    delta_sum = jnp.sum(mixture_quad.astype(jnp.float32) * attention_quad.astype(jnp.float32), -1)
    back_count = (query_start + seq_rows + block_len - 1) // block_len

    def backward_turn(loop_turn, loop_carry):
        query_grad, pair_store = loop_carry
        row_begin = loop_turn * block_len
        key_rows = lax.dynamic_slice_in_dim(keys_all, row_begin, block_len, 0)
        val_rows = lax.dynamic_slice_in_dim(values_all, row_begin, block_len, 0)
        scores = (
            jnp.einsum("bngd,knd->bngk", queries, key_rows, preferred_element_type=jnp.float32)
            * score_scale
        )
        key_pos = row_begin + jnp.arange(block_len, dtype=jnp.int32)
        visible = key_pos[None, :] <= query_pos[:, None]
        prob_full = jnp.where(
            visible[:, None, None, :], jnp.exp(scores - log_sum_total[..., None]), 0.0
        )
        prob_grad = jnp.einsum(
            "bngd,knd->bngk", mixture_quad, val_rows, preferred_element_type=jnp.float32
        )
        score_grad = prob_full * (prob_grad - delta_sum[..., None])
        prob_half = prob_full.astype(jnp.bfloat16)
        score_half = score_grad.astype(jnp.bfloat16)
        query_grad = (
            query_grad
            + jnp.einsum("bngk,knd->bngd", score_half, key_rows, preferred_element_type=jnp.float32)
            * score_scale
        )
        key_grad = (
            jnp.einsum("bngk,bngd->knd", score_half, queries, preferred_element_type=jnp.float32)
            * score_scale
        )
        value_grad = jnp.einsum(
            "bngk,bngd->knd", prob_half, mixture_quad, preferred_element_type=jnp.float32
        )
        pair_store = lax.dynamic_update_slice_in_dim(
            pair_store, jnp.stack([key_grad, value_grad], 2), row_begin, 0
        )
        return (query_grad, pair_store)

    start_back = (
        jnp.zeros(state_shape + (HEAD_SIZE,), jnp.float32),
        jnp.zeros((seq_total, kv_heads, 2, HEAD_SIZE), jnp.float32),
    )
    query_grad, pair_store = lax.fori_loop(0, back_count, backward_turn, start_back)
    grad_query = query_grad.reshape(seq_rows, kv_heads * group_width * HEAD_SIZE).astype(
        jnp.bfloat16
    )
    pair_sum = lax.psum_scatter(
        pair_store.reshape(seq_total, kv_heads * 2 * HEAD_SIZE).astype(jnp.bfloat16),
        "ctx",
        scatter_dimension=0,
        tiled=True,
    ).astype(jnp.float32)
    pair_sum = pair_sum.reshape(seq_rows, kv_heads, 2, HEAD_SIZE)
    key_gradient = pair_sum[:, :, 0].reshape(seq_rows, kv_heads * HEAD_SIZE).astype(jnp.bfloat16)
    value_gradient = pair_sum[:, :, 1].reshape(seq_rows, kv_heads * HEAD_SIZE).astype(jnp.bfloat16)
    return (
        layer_out,
        grad_resid,
        grad_query,
        key_gradient,
        value_gradient,
        grad_out_proj,
        grad_gain,
        grad_w_gate,
        grad_w_up,
        grad_w_down,
    )


F32 = jnp.float32
BF16 = jnp.bfloat16
LOG2E = 1.4426950408889634
SETS = (0, 2, 1, 3)


def crossed(x, bits):
    return lax.ppermute(x, "ctx", [(i, i ^ bits) for i in range(4)])


def swapped(x, bits):
    return lax.ppermute(x, "exp", [(i, i ^ bits) for i in range(4)])


def after(x, *others):
    return lax.optimization_barrier((x, *others))[0]


def nt(a, b):
    return lax.dot_general(a, b, (((1,), (1,)), ((), ())), preferred_element_type=F32)


def tn(a, b):
    return lax.dot_general(a, b, (((0,), (0,)), ((), ())), preferred_element_type=F32)


def nn(a, b):
    return lax.dot_general(a, b, (((1,), (0,)), ((), ())), preferred_element_type=F32)


def run_kernel(body, name, place, args, outs, scratch=(), flops=0, limit=16):
    vmem = pl.BlockSpec(memory_space=pltpu.VMEM)
    shapes = [jax.ShapeDtypeStruct(shape, dtype) for shape, dtype in outs]
    moved = sum(x.size * x.dtype.itemsize for x in list(args) + shapes)
    return pl.pallas_call(
        body,
        in_specs=[pl.BlockSpec(memory_space=pltpu.SMEM)] + [vmem] * len(args),
        out_specs=[vmem] * len(outs),
        out_shape=shapes,
        scratch_shapes=[pltpu.VMEM(shape, dtype) for shape, dtype in scratch],
        compiler_params=pltpu.CompilerParams(vmem_limit_bytes=limit << 20),
        cost_estimate=pl.CostEstimate(flops=flops, bytes_accessed=moved, transcendentals=0),
        name=name,
    )(place, *args)


def visible_keys(rows, count, query_block, base):
    shape = (rows, count * rows)
    key_pos = lax.broadcasted_iota(jnp.int32, shape, 1)
    turn = sum([(key_pos >= i * rows).astype(jnp.int32) for i in range(1, count)])
    offset = key_pos - turn * rows
    diagonal = offset <= lax.broadcasted_iota(jnp.int32, shape, 0)
    block = turn ^ base
    return (block < query_block) | ((block == query_block) & diagonal)


def pack_heads(place, key, value, query):
    rows, width = query.shape

    def body(place_ref, key_ref, value_ref, query_ref, out_ref):
        out_ref[:, :HEAD_SIZE] = key_ref[...]
        out_ref[:, HEAD_SIZE : 2 * HEAD_SIZE] = value_ref[...]
        out_ref[:, 2 * HEAD_SIZE :] = query_ref[...]

    shape = (rows, width + 2 * HEAD_SIZE)
    return run_kernel(body, "pack_heads", place, [key, value, query], [(shape, BF16)])[0]


def pack_rows(place, grad_out, routes, gate_weights, resid, cols):
    tok, width = grad_out.shape
    experts = 4 * (width // cols)

    def body(place_ref, grad_ref, route_ref, weight_ref, resid_ref, far_ref, near_ref, third_ref):
        lane = lax.broadcasted_iota(jnp.int32, (tok, 128), 1)
        weight = weight_ref[...]
        high = weight.astype(BF16).astype(F32)
        low = weight - high
        gates = jnp.zeros((tok, 128), F32)
        for k in range(routes.shape[1]):
            route = route_ref[:, k : k + 1]
            gates = gates + jnp.where(lane == route, high[:, k : k + 1], 0.0)
            gates = gates + jnp.where(lane == route + experts, low[:, k : k + 1], 0.0)

        def columns(turn):
            return resid_ref[:, pl.ds(pl.multiple_of((place_ref[0] ^ turn) * cols, cols), cols)]

        for ref, turn in ((far_ref, 2), (near_ref, 1)):
            ref[:, :width] = grad_ref[...]
            ref[:, width : width + 128] = gates.astype(BF16)
            ref[:, width + 128 :] = columns(turn)
        third_ref[...] = columns(3)

    message = ((tok, width + 128 + cols), BF16)
    return run_kernel(
        body,
        "pack_rows",
        place,
        [grad_out, routes, gate_weights, resid],
        [message, message, ((tok, cols), BF16)],
    )


def attend(place, parts, out_proj):
    n = len(parts)
    rows = parts[0].shape[0]
    width = out_proj.shape[0]
    tok = rows // 4
    cols = out_proj.shape[1]
    heads = width // HEAD_SIZE
    factor = HEAD_SIZE ** (-0.5) * LOG2E

    def body(place_ref, *refs):
        proj_ref, mix_ref, own_ref, keep_ref, send_ref, pairs_ref, everything, ps = refs[n:]
        c, e = place_ref[0], place_ref[1]
        for r in range(n):
            everything[pl.ds(pl.multiple_of((c ^ r) * rows, rows), rows), :] = refs[r][...]
            pairs_ref[r * rows : (r + 1) * rows, :] = refs[r][:, : 2 * HEAD_SIZE]
        keys, values = everything.at[:, :HEAD_SIZE], everything.at[:, HEAD_SIZE : 2 * HEAD_SIZE]
        below = lax.broadcasted_iota(jnp.int32, (rows, rows), 1) <= lax.broadcasted_iota(
            jnp.int32, (rows, rows), 0
        )
        for b in range(n):
            lo, hi = b * rows, (b + 1) * rows
            for head in range(heads):
                at = slice(head * HEAD_SIZE, (head + 1) * HEAD_SIZE)
                query = everything[lo:hi, (head + 2) * HEAD_SIZE : (head + 3) * HEAD_SIZE]
                scores = nt(query, keys[:hi, :])
                last = jnp.where(below, scores[:, lo:], NEG)
                scores = jnp.concatenate([scores[:, :lo], last], 1) if b else last
                peak = jnp.max(scores, -1, keepdims=True)
                weights = jnp.exp2((scores - peak) * factor)
                total = jnp.sum(weights, -1, keepdims=True)
                mix_ref[lo:hi, at] = (nn(weights.astype(BF16), values[:hi, :]) / total).astype(BF16)
            ps[...] = nn(mix_ref[lo:hi, :], proj_ref[...]).astype(BF16)
            for turn in range(2):
                same, other = e ^ (2 * turn), e ^ (2 * turn + 1)
                keep_ref[turn, c ^ b] = ps[pl.ds(pl.multiple_of(same * tok, tok), tok), :]
                send_ref[turn, c ^ b] = ps[pl.ds(pl.multiple_of(other * tok, tok), tok), :]
        own_ref[...] = mix_ref[pl.ds(pl.multiple_of(c * rows, rows), rows), :]

    return run_kernel(
        body,
        "attend",
        place,
        [*parts, out_proj],
        [
            ((n * rows, width), BF16),
            ((rows, width), BF16),
            ((2, n, tok, cols), BF16),
            ((2, n, tok, cols), BF16),
            ((n * rows, 2 * HEAD_SIZE), BF16),
        ],
        [((n * rows, width + 2 * HEAD_SIZE), BF16), ((rows, cols), BF16)],
        flops=4 * n * rows * n * rows * width,
    )


def hidden_rows(place, keep, received, line, resid, near, far, third):
    cols = line.shape[2]
    last = near.shape[1] - cols

    def body(place_ref, keep_ref, received_ref, line_ref, resid_ref, near_ref, far_ref, third_ref, out_ref):
        total = keep_ref[0].astype(F32) + received_ref[0].astype(F32) + line_ref[...].astype(F32)
        own = resid_ref[:, pl.ds(pl.multiple_of(place_ref[0] * cols, cols), cols)]
        blocks = [own, near_ref[:, last:], far_ref[:, last:], third_ref[...]]
        for r, block in enumerate(blocks):
            out_ref[r] = (total[r] + block.astype(F32)).astype(BF16)

    return run_kernel(
        body,
        "hidden_rows",
        place,
        [keep, received, line, resid, near, far, third],
        [(line.shape, BF16)],
    )[0]


def grad_rows_of(place, grad_sets, w_down):
    lead, tok = grad_sets[0][0].shape[:2]
    n = lead + 1
    total = 4 * n * tok
    experts = 4 * n
    units, width = w_down.shape

    def body(place_ref, *refs):
        down_ref, rows_ref, gate_ref, act_ref = refs[8:]
        expert = place_ref[0] * 4 + place_ref[1]
        lane = lax.broadcasted_iota(jnp.int32, (tok, 128), 1)
        wanted = (lane == expert) | (lane == expert + experts)
        for s in range(4):
            for j in range(n):
                at = slice((s * n + j) * tok, (s * n + j + 1) * tok)
                block = refs[2 * s].at[j] if j < lead else refs[2 * s + 1]
                gate = jnp.where(wanted, block[:, width:].astype(F32), 0.0)
                gate = jnp.sum(gate, -1, keepdims=True)
                gate_ref[at, :] = gate
                rows_ref[at, :] = (block[:, :width].astype(F32) * gate).astype(BF16)
        act_ref[...] = nt(rows_ref[...], down_ref[...])

    return run_kernel(
        body,
        "grad_rows",
        place,
        [*sum(grad_sets, []), w_down],
        [((total, width), BF16), ((total, 1), F32), ((total, units), F32)],
        flops=2 * total * width * units,
        limit=24,
    )


def expert_rows(place, hidden_sets, act_grad, norm_gain, w_gate, w_up):
    n, tok, cols = hidden_sets[0][0].shape
    width, hidden_units = w_gate.shape
    group = n * tok
    total = 4 * group

    def body(place_ref, *refs):
        pieces = refs[: 4 * n]
        act_grad_ref, gain_ref, gate_ref, up_ref = refs[4 * n : 4 * n + 4]
        normed_ref, act_ref, gate_grad_ref, up_grad_ref, own_ref = refs[4 * n + 4 : 4 * n + 9]
        grads, sides, hid = refs[4 * n + 9 : 4 * n + 13], refs[4 * n + 13 : 4 * n + 15], refs[4 * n + 15]
        c = place_ref[0]
        for s in range(4):
            for d in range(n):
                at = pl.multiple_of((c ^ d) * cols, cols)
                for t in range(n):
                    row = s * group + (d ^ t) * tok
                    hid[row : row + tok, pl.ds(at, cols)] = pieces[s * n + d][t]
            rows = slice(s * group, (s + 1) * group)
            value = hid[rows, :].astype(F32)
            inv_rms = lax.rsqrt(jnp.mean(value * value, -1, keepdims=True) + EPS)
            normed_ref[rows, :] = (value * inv_rms * gain_ref[...]).astype(BF16)
        own_ref[...] = hid[:tok, :]
        pre_gate = nn(normed_ref[...], gate_ref[...])
        pre_up = nn(normed_ref[...], up_ref[...])
        sig = jax.nn.sigmoid(pre_gate)
        act_ref[...] = (pre_gate * sig * pre_up).astype(BF16)
        act_grad_value = act_grad_ref[...]
        up_grad_ref[...] = (act_grad_value * pre_gate * sig).astype(BF16)
        gate_grad_ref[...] = (
            act_grad_value * pre_up * sig * (1.0 + pre_gate * (1.0 - sig))
        ).astype(BF16)
        for j in range(n):
            at = slice(j * cols, (j + 1) * cols)
            part = nt(gate_grad_ref[...], gate_ref[at, :]) + nt(up_grad_ref[...], up_ref[at, :])
            for s in range(4):
                block = part[s * group : (s + 1) * group].astype(BF16).reshape(n, tok, cols)
                if j < n - 1:
                    grads[s][:, :, at] = block
                else:
                    sides[s // 2][:, s % 2] = block

    units = ((total, hidden_units), BF16)
    return run_kernel(
        body,
        "expert_rows",
        place,
        [*sum(hidden_sets, []), act_grad, norm_gain.reshape(1, width), w_gate, w_up],
        [((total, width), BF16), units, units, units, ((tok, width), BF16)]
        + [((n, tok, width - cols), BF16)] * 4
        + [((n, 2, tok, cols), BF16)] * 2,
        [((total, width), BF16)],
        flops=8 * total * width * hidden_units,
        limit=32,
    )


def weighted_rows(place, act_rows, gate, w_down, n):
    total = act_rows.shape[0]
    width = w_down.shape[1]
    group, cols = total // 4, width // n

    def body(place_ref, act_ref, gate_ref, down_ref, *outs):
        for j in range(n):
            at = slice(j * cols, (j + 1) * cols)
            part = nn(act_ref[...], down_ref[:, at]).astype(BF16).astype(F32) * gate_ref[...]
            for s in range(4):
                block = part[s * group : (s + 1) * group].astype(BF16)
                outs[s // 2][s % 2, :, :, at] = block.reshape(n, group // n, cols)

    return run_kernel(
        body,
        "weighted_rows",
        place,
        [act_rows, gate, w_down],
        [((2, n, group // n, width), BF16)] * 2,
        flops=2 * total * width * w_down.shape[0],
    )


def add(*xs):
    return sum([x.astype(F32) for x in xs[1:]], xs[0].astype(F32)).astype(BF16)


def sum_rows(parts, keep, send, beside, ready):
    side = swapped(send, 1)
    far = after(swapped(parts[3], 1), beside, side, ready)
    near = swapped(parts[2], 1)
    line = swapped(add(parts[1], far), 2)
    sides = [add(keep[j], side[j]) for j in range(4)]
    got = [crossed(sides[j], j) for j in range(1, 4)]
    total = add(sides[0], *got)
    sums = [after(add(parts[0][j], near[j], line[j]), total) for j in range(4)]
    wide = [sums[0]] + [crossed(sums[j], j) for j in range(1, 4)]
    return wide, [total[0], swapped(total[1], 2)]


def norm_backward(place, wide, narrow, hidden, grad_out, norm_gain, cols):
    n = len(wide) + len(narrow)
    tok, width = hidden.shape
    blocks = width // cols

    def body(place_ref, *refs):
        hidden_ref, grad_ref, gain_ref = refs[n : n + 3]
        out_ref, cuts, part_ref = refs[n + 3], refs[n + 4 : -1], refs[-1]
        c = place_ref[0]
        sums = [[r[...].astype(F32) for r in rs] for rs in (refs[: len(wide)], refs[len(wide) : n])]
        normed_grad = jnp.concatenate([sum(x[1:], x[0]) for x in sums], 1)
        value = hidden_ref[...].astype(F32)
        inv_rms = lax.rsqrt(jnp.mean(value * value, -1, keepdims=True) + EPS)
        unit_rows = value * inv_rms
        part = jnp.sum(normed_grad * unit_rows, 0, keepdims=True)
        high = part.astype(BF16)
        spare = jnp.zeros((14, width), BF16)
        part_ref[...] = jnp.concatenate([high, (part - high.astype(F32)).astype(BF16), spare], 0)
        scaled = gain_ref[...] * normed_grad
        mean = jnp.mean(scaled * unit_rows, -1, keepdims=True)
        grad = grad_ref[...].astype(F32) + inv_rms * (scaled - unit_rows * mean)
        out_ref[...] = grad.astype(BF16)
        for d in range(blocks):
            at = pl.ds(pl.multiple_of((c ^ d) * cols, cols), cols)
            to = slice(d % 2 * cols, (d % 2 + 1) * cols)
            cuts[d // 2][:tok, to] = out_ref[:, at]
            cuts[d // 2][tok:, to] = part_ref[:, at]

    return run_kernel(
        body,
        "norm_backward",
        place,
        [*wide, *narrow, hidden, grad_out, norm_gain.reshape(1, width)],
        [((tok, width), BF16)] + [((tok + 16, 2 * cols), BF16)] * (blocks // 2),
        [((16, width), BF16)],
    )


def layer_rows(place, summed, hidden):
    def body(place_ref, *refs):
        total = refs[-2][...].astype(F32)
        for r in refs[:-2]:
            total = total + r[...].astype(F32)
        refs[-1][...] = total.astype(BF16)

    return run_kernel(body, "layer_rows", place, [*summed, hidden], [(hidden.shape, BF16)])[0]


def mix_grad_parts(place, cut_sets, out_proj, proj_here, proj_there):
    count, cut, cols = cut_sets[0].shape
    tok, cols = cut - 16, cols // 2
    rows, width = 4 * tok, out_proj.shape[0]

    def body(place_ref, *refs):
        proj_ref, here_ref, there_ref, own_ref, far_ref, keep_ref, send_ref, grads, acc = refs[4:]
        e, g = place_ref[1], place_ref[2]
        gain = sum([refs[r][i, tok : tok + 2, :].astype(F32) for r in range(4) for i in range(count)])
        gain = jnp.sum(gain, 0, keepdims=True)
        high = gain.astype(BF16)
        spare = jnp.zeros((14, 2 * cols), BF16)
        gain = jnp.concatenate([high, (gain - high.astype(F32)).astype(BF16), spare], 0)
        for i in range(count):
            for r in range(4):
                at = pl.multiple_of(i * rows + (e ^ r) * tok, tok)
                grads[pl.ds(at, tok), :] = refs[r][i, :tok, :]
        for ref, at in ((keep_ref, slice(0, cols)), (send_ref, slice(cols, 2 * cols))):
            ref[: count * rows, :] = grads[:, at]
            ref[count * rows :, :] = gain[:, at]
        half = width // 2
        for ref, index in ((here_ref, g), (there_ref, 1 - g)):
            at = pl.ds(pl.multiple_of(index * half, half), half)
            acc[:, at] = nt(grads[:, cols:], ref[...])
        for h in range(2):
            at = slice(h * half, (h + 1) * half)
            total = (acc[:, at] + nt(grads[:, :cols], proj_ref[at, :])).astype(BF16)
            own_ref[:, at] = total[:rows]
            far_ref[:, at] = total[rows:]

    return run_kernel(
        body,
        "mix_grad_parts",
        place,
        [*cut_sets, out_proj, proj_here, proj_there],
        [((rows, width), BF16)] * 2 + [((count * rows + 16, cols), BF16)] * 2,
        [((count * rows, 2 * cols), BF16), ((count * rows, width), F32)],
        flops=4 * count * rows * cols * width,
    )


def attend_backward(place, grad_parts, query, pairs, mix, gain):
    g = len(grad_parts)
    rows, width = mix.shape
    n = pairs.shape[0] // rows
    heads = width // HEAD_SIZE
    scale = HEAD_SIZE ** (-0.5)

    def body(place_ref, *refs):
        g_refs, (query_ref, pairs_ref, mix_ref, gain_ref, dq_ref) = refs[:g], refs[g : g + 5]
        outs = refs[g + 5 : g + 5 + n]
        qs, ms, score_half, prob_half = refs[g + 5 + n :]
        ks, vs = pairs_ref.at[:, :HEAD_SIZE], pairs_ref.at[:, HEAD_SIZE:]
        c = place_ref[0]
        visible = visible_keys(rows, n, c, c)
        for head in range(heads):
            at = slice(head * HEAD_SIZE, (head + 1) * HEAD_SIZE)
            rs = slice(head * rows, (head + 1) * rows)
            grad = sum([x[:, at].astype(F32) for x in g_refs[1:]], g_refs[0][:, at].astype(F32))
            grad = grad.astype(BF16)
            qs[rs, :] = query_ref[:, at]
            ms[rs, :] = grad
            scores = jnp.where(visible, nt(query_ref[:, at], ks[...]), NEG)
            peak = jnp.max(scores, -1, keepdims=True)
            weights = jnp.exp2((scores - peak) * (scale * LOG2E))
            prob = weights * (1.0 / jnp.sum(weights, -1, keepdims=True))
            delta = jnp.sum(grad.astype(F32) * mix_ref[:, at].astype(F32), -1, keepdims=True)
            score_half[rs, :] = (prob * (nt(grad, vs[...]) - delta)).astype(BF16)
            prob_half[rs, :] = prob.astype(BF16)
            dq_ref[:, at] = (nn(score_half[rs, :], ks[...]) * scale).astype(BF16)
        key_sum = (tn(score_half[...], qs[...]) * scale).astype(BF16)
        value_sum = tn(prob_half[...], ms[...]).astype(BF16)
        for j in range(n):
            rs = slice(j * rows, (j + 1) * rows)
            outs[j][:rows, :HEAD_SIZE] = key_sum[rs]
            outs[j][:rows, HEAD_SIZE:] = value_sum[rs]
            outs[j][rows:, :] = gain_ref[...]

    stacked = ((heads * rows, HEAD_SIZE), BF16)
    halves = ((heads * rows, n * rows), BF16)
    return run_kernel(
        body,
        "attend_backward",
        place,
        [*grad_parts, query, pairs, mix, gain],
        [((rows, width), BF16)] + [((rows + 16, 2 * HEAD_SIZE), BF16)] * n,
        [stacked, stacked, halves, halves],
        flops=10 * rows * width * n * rows,
    )


def proj_grad(place, mix_all, keep, near):
    total, width = mix_all.shape
    rows, cols = total // 4, keep.shape[1]

    def body(place_ref, mix_ref, keep_ref, near_ref, out_ref, gain_ref, grads):
        c = place_ref[0]
        for d in range(4):
            ref = near_ref if d % 2 else keep_ref
            at = pl.multiple_of((c ^ d) * rows, rows)
            grads[pl.ds(at, rows), :] = ref[d // 2 * rows : (d // 2 + 1) * rows, :]
        out_ref[...] = tn(mix_ref[...], grads[...]).astype(BF16)
        gain = keep_ref[2 * rows :, :].astype(F32) + near_ref[2 * rows :, :].astype(F32)
        gain = jnp.sum(gain[:2], 0, keepdims=True)
        high = gain.astype(BF16)
        low = (gain - high.astype(F32)).astype(BF16)
        pieces = [x[:, i : i + cols // 2] for x in (high, low) for i in (0, cols // 2)]
        gain_ref[...] = jnp.concatenate([*pieces, jnp.zeros((12, cols // 2), BF16)], 0)

    return run_kernel(
        body,
        "proj_grad",
        place,
        [mix_all, keep, near],
        [((width, cols), BF16), ((16, cols // 2), BF16)],
        [((total, cols), BF16)],
        flops=2 * total * cols * width,
    )


def pair_sums(place, parts):
    n = len(parts)
    rows = parts[0].shape[0] - 16
    half = parts[0].shape[1]

    def body(place_ref, *refs):
        key_ref, value_ref, gain_ref = refs[n:]
        c = place_ref[0]
        total = sum([r[:rows, :].astype(F32) for r in refs[1:n]], refs[0][:rows, :].astype(F32))
        key_ref[...] = total[:, :HEAD_SIZE].astype(BF16)
        value_ref[...] = total[:, HEAD_SIZE:].astype(BF16)
        for j in range(n):
            tail = refs[j][rows:, :].astype(F32)
            for i in range(2):
                at = pl.multiple_of(((c ^ j) * 2 + i) * half, half)
                gain_ref[:, pl.ds(at, half)] = tail[i : i + 1] + tail[i + 2 : i + 3]

    return run_kernel(
        body,
        "pair_sums",
        place,
        parts,
        [((rows, HEAD_SIZE), BF16), ((rows, HEAD_SIZE), BF16), ((1, 2 * n * half), F32)],
    )


def local_dense(
    resid,
    query,
    key,
    value,
    out_proj,
    norm_gain,
    w_gate,
    w_up,
    w_down,
    routes,
    gate_weights,
    grad_out,
):
    n = lax.axis_size("ctx")
    c, e, g = lax.axis_index("ctx"), lax.axis_index("exp"), lax.axis_index("groups")
    place = jnp.stack([c, e, g]).astype(jnp.int32)
    tok, width = resid.shape
    cols = out_proj.shape[1]
    scope = jax.named_scope

    def across(blocks):
        return [blocks[0]] + [crossed(blocks[r], r) for r in range(1, n)]

    with scope("gather_rows"):
        to_far, to_near, to_third = pack_rows(place, grad_out, routes, gate_weights, resid, cols)
    with scope("gather_heads"):
        heads = pack_heads(place, key, value, query)
        far, near = crossed(heads, 2), crossed(heads, 1)
        parts = [heads, near, far, crossed(after(far, to_far, to_near, to_third), 1)]

    with scope("gather_rows"):
        row_third = crossed(after(to_third, far, near), 3)
        parts[3] = after(parts[3], row_third)
        to_far, to_near = lax.optimization_barrier((to_far, to_near, parts[3]))[:2]
        row_far, row_near = crossed(to_far, 2), crossed(to_near, 1)

    mix_all, mix, keep, send, pairs = attend(place, parts, out_proj)
    with scope("sum_heads"):
        received = swapped(send, 1)
        line = swapped(add(keep[1], received[1]), 2)
    hidden_block = hidden_rows(
        place, keep, received, line, resid, row_near, row_far, row_third
    )
    with scope("gather_rows"):
        size = width + 128
        to_far, row_far, row_near = lax.optimization_barrier((to_far, row_far, row_near, line))[:3]
        rest = crossed(row_far[:, :size], 1)
        grad_own = jnp.stack([to_far[:, :size], row_near[:, :size], row_far[:, :size]])
        grad_own, grad_line = [grad_own, rest], [swapped(grad_own, 2), swapped(rest, 2)]
        grad_sets = [grad_own, grad_line] + [
            [swapped(after(x, grad_line[1]), 1) for x in xs] for xs in (grad_own, grad_line)
        ]
    grad_rows, gate, act_grad = grad_rows_of(place, grad_sets, w_down[0])

    with scope("gather_hidden"):
        far, near = crossed(hidden_block, 2), crossed(hidden_block, 1)
        line = swapped(hidden_block, 2)
        hidden_own = [hidden_block, near, far, crossed(after(far, near), 1)]
        hidden_line = [line] + [swapped(after(x, line), 2) for x in hidden_own[1:3]]
        hidden_line.append(swapped(after(hidden_own[3], *hidden_line), 2))
    with scope("gather_proj"):
        half = out_proj.shape[0] // 2
        proj_half = lax.dynamic_slice_in_dim(out_proj, g * half, half, 0)
        proj_here = crossed(after(proj_half, hidden_own[3]), 1)
    with scope("gather_hidden"):
        hidden_line[-1], act_grad, proj_here = lax.optimization_barrier(
            (hidden_line[-1], act_grad, proj_here)
        )
        hidden_sets = [hidden_own, hidden_line] + [
            [swapped(x, 1) for x in xs] for xs in (hidden_own, hidden_line)
        ]

    with scope("gather_proj"):
        proj_there = lax.ppermute(proj_here, "groups", [(0, 1), (1, 0)])

    normed, act_rows, gate_grad, up_grad, hidden, *row_grads = expert_rows(
        place, hidden_sets, act_grad, norm_gain, w_gate[0], w_up[0]
    )
    out_keep, out_send = weighted_rows(place, act_rows, gate, w_down[0], n)
    with scope("sum_row_grads"):
        wide, narrow = sum_rows(row_grads[:4], *row_grads[4:], out_keep, proj_there)

    with scope("sum_outputs"):
        out_sent = swapped(out_send, 1)
        out_line = swapped(after(add(out_keep[1], out_sent[1]), wide[0]), 2)
    grad_resid, *cuts = norm_backward(
        place, wide, narrow, after(hidden, out_line), grad_out, norm_gain, cols
    )

    with scope("gather_cuts"):
        cut_own = jnp.stack([cuts[0], crossed(cuts[1], 2)])
        cut_line = swapped(cut_own, 2)
        cut_sets = [cut_own, swapped(cut_own, 1), cut_line, swapped(cut_line, 1)]
    mix_own, mix_far, cut_keep, cut_send = mix_grad_parts(
        place, cut_sets, out_proj, proj_here, proj_there
    )
    with scope("sum_mix_grad"):
        mix_grads = [mix_own, crossed(mix_far, 2)]
    with scope("gather_cuts"):
        cut_near = crossed(cut_send, 1)

    with scope("sum_outputs"):
        out_sums = [add(out_keep[0][j], out_sent[0][j], out_line[j]) for j in range(n)]
        out_sums = [after(x, cut_own) for x in out_sums]
        out_sums = [out_sums[0]] + [crossed(out_sums[j], j) for j in range(1, n)]
    normed, act_rows = lax.optimization_barrier((normed, act_rows, mix_own))[:2]
    grad_w_gate = tn(normed, gate_grad).astype(BF16)
    grad_w_up = tn(normed, up_grad).astype(BF16)
    grad_w_down = tn(act_rows, grad_rows).astype(BF16)
    grad_out_proj, gain_rows = proj_grad(place, mix_all, cut_keep, cut_near)
    mix_grads[0] = after(mix_own, grad_w_gate, grad_w_up, *out_sums[1:])

    grad_query, *pair_parts = attend_backward(place, mix_grads, query, pairs, mix, gain_rows)
    with scope("sum_pairs"):
        key_gradient, value_gradient, grad_gain = pair_sums(place, across(pair_parts))
    layer_out = layer_rows(place, out_sums, after(hidden, grad_query))

    return (
        layer_out,
        grad_resid,
        grad_query,
        key_gradient,
        value_gradient,
        grad_out_proj,
        grad_gain.reshape(width),
        grad_w_gate[None],
        grad_w_up[None],
        grad_w_down[None],
    )


def local(*args):
    key, w_gate, routes = args[2], args[6], args[9]
    ctx_count, exp_count = lax.axis_size("ctx"), lax.axis_size("exp")
    expert_total = w_gate.shape[0] * ctx_count * exp_count
    dense = (
        2 * routes.shape[1] >= expert_total
        and w_gate.shape[0] == 1
        and key.shape[1] == HEAD_SIZE
        and exp_count == 4
        and ctx_count == 4
        and lax.axis_size("groups") == 2
    )
    return (local_dense if dense else local_routed)(*args)


def solution(mesh):
    in_specs = (
        P(("groups", "ctx", "exp"), None),
        P(("groups", "ctx"), "exp"),
        P(("groups", "ctx"), "exp"),
        P(("groups", "ctx"), "exp"),
        P("exp", "ctx"),
        P(),
        P(("ctx", "exp"), None, None),
        P(("ctx", "exp"), None, None),
        P(("ctx", "exp"), None, None),
        P(("groups", "ctx", "exp"), None),
        P(("groups", "ctx", "exp"), None),
        P(("groups", "ctx", "exp"), None),
    )
    out_specs = (
        P(("groups", "ctx", "exp"), None),
        P(("groups", "ctx", "exp"), None),
        P(("groups", "ctx"), "exp"),
        P(("groups", "ctx"), "exp"),
        P(("groups", "ctx"), "exp"),
        P(("groups", "exp"), "ctx"),
        P("groups"),
        P(("groups", "ctx", "exp"), None, None),
        P(("groups", "ctx", "exp"), None, None),
        P(("groups", "ctx", "exp"), None, None),
    )
    return jax.shard_map(local, mesh=mesh, in_specs=in_specs, out_specs=out_specs, check_vma=False)
```

```python
import jax
import jax.numpy as jnp
from jax import lax
from jax.experimental import pallas as pl
from jax.experimental.pallas import tpu as pltpu
from jax.sharding import PartitionSpec as P

HEAD_SIZE = 128


EPS = 1e-06
NEG = -1e30


def attend_block(soft_state, queries, key_rows, val_rows, row_begin, query_pos, score_scale):
    peak_run, total_run, accum_rows = soft_state
    scores = (
        jnp.einsum("bngd,knd->bngk", queries, key_rows, preferred_element_type=jnp.float32)
        * score_scale
    )
    key_pos = row_begin + jnp.arange(key_rows.shape[0], dtype=jnp.int32)
    visible = key_pos[None, :] <= query_pos[:, None]
    scores = jnp.where(visible[:, None, None, :], scores, NEG)
    peak_new = jnp.maximum(peak_run, jnp.max(scores, -1))
    rescale = jnp.exp(peak_run - peak_new)
    weights = jnp.exp(scores - peak_new[..., None])
    total_new = total_run * rescale + jnp.sum(weights, -1)
    mixed_rows = jnp.einsum(
        "bngk,knd->bngd", weights.astype(jnp.bfloat16), val_rows, preferred_element_type=jnp.float32
    )
    return (peak_new, total_new, accum_rows * rescale[..., None] + mixed_rows)


def expert_trade(buffer):
    return lax.all_to_all(buffer, ("ctx", "exp"), split_axis=0, concat_axis=0, tiled=True)


def local_routed(
    resid,
    query,
    key,
    value,
    out_proj,
    norm_gain,
    w_gate,
    w_up,
    w_down,
    routes,
    gate_weights,
    grad_out,
):
    ctx_count = lax.axis_size("ctx")
    exp_count = lax.axis_size("exp")
    ctx_index = lax.axis_index("ctx")
    seq_rows = query.shape[0]
    kv_heads = key.shape[1] // HEAD_SIZE
    group_width = query.shape[1] // HEAD_SIZE // kv_heads
    seq_total = seq_rows * ctx_count
    score_scale = HEAD_SIZE ** (-0.5)
    query_start = ctx_index * seq_rows
    query_pos = query_start + jnp.arange(seq_rows, dtype=jnp.int32)
    queries = query.reshape(seq_rows, kv_heads, group_width, HEAD_SIZE)
    state_shape = (seq_rows, kv_heads, group_width)
    start_state = (
        jnp.full(state_shape, NEG, jnp.float32),
        jnp.zeros(state_shape, jnp.float32),
        jnp.zeros(state_shape + (HEAD_SIZE,), jnp.float32),
    )
    block_len = min(512, seq_total)
    keys_flat, values_flat = (
        lax.all_gather(key, "ctx", axis=0, tiled=True),
        lax.all_gather(value, "ctx", axis=0, tiled=True),
    )
    keys_all = keys_flat.reshape(seq_total, kv_heads, HEAD_SIZE)
    values_all = values_flat.reshape(seq_total, kv_heads, HEAD_SIZE)
    block_count = (query_start + seq_rows + block_len - 1) // block_len

    def forward_turn(loop_turn, soft_state):
        row_begin = loop_turn * block_len
        key_rows = lax.dynamic_slice_in_dim(keys_all, row_begin, block_len, 0)
        val_rows = lax.dynamic_slice_in_dim(values_all, row_begin, block_len, 0)
        return attend_block(
            soft_state, queries, key_rows, val_rows, row_begin, query_pos, score_scale
        )

    soft_state = lax.fori_loop(0, block_count, forward_turn, start_state)
    peak_val, total_val, accum_rows = soft_state
    attention_quad = (accum_rows / total_val[..., None]).astype(jnp.bfloat16)
    attn_mix = attention_quad.reshape(seq_rows, kv_heads * group_width * HEAD_SIZE)
    log_sum_total = peak_val + jnp.log(total_val)
    proj_full = lax.all_gather(out_proj, "ctx", axis=1, tiled=True)
    tok_rows = resid.shape[0]
    proj_sum = lax.psum_scatter(
        jnp.dot(attn_mix, proj_full, preferred_element_type=jnp.float32).astype(jnp.bfloat16),
        "exp",
        scatter_dimension=0,
        tiled=True,
    ).astype(jnp.float32)
    hidden = (resid.astype(jnp.float32) + proj_sum).astype(jnp.bfloat16)
    hidden_f = hidden.astype(jnp.float32)
    inv_rms = lax.rsqrt(jnp.mean(hidden_f * hidden_f, -1, keepdims=True) + EPS)
    unit_rows = hidden_f * inv_rms
    normed = (unit_rows * norm_gain).astype(jnp.bfloat16)
    top_count = routes.shape[1]
    model_width = normed.shape[1]
    experts_local = w_gate.shape[0]
    device_count = ctx_count * exp_count
    expert_total = experts_local * device_count
    capacity = 2 * tok_rows * top_count // expert_total
    flat_routes = routes.reshape(-1)
    member = (flat_routes[:, None] == jnp.arange(expert_total, dtype=jnp.int32)[None, :]).astype(
        jnp.int32
    )
    slot_pos = jnp.sum(jnp.cumsum(member, 0) * member, 1) - 1
    dest_row = flat_routes * capacity + slot_pos
    pair_weights = gate_weights.reshape(-1)

    def place_rows(rows_out):
        return (
            jnp.zeros((expert_total * capacity, model_width), jnp.bfloat16)
            .at[dest_row]
            .set(rows_out)
        )

    def to_experts(buffer):
        return (
            buffer.reshape(device_count, experts_local, capacity, model_width)
            .transpose(1, 0, 2, 3)
            .reshape(experts_local, device_count * capacity, model_width)
        )

    def from_experts(rows_back):
        return (
            rows_back.reshape(experts_local, device_count, capacity, model_width)
            .transpose(1, 0, 2, 3)
            .reshape(device_count * experts_local * capacity, model_width)
        )

    rows_in = to_experts(expert_trade(place_rows(jnp.repeat(normed, top_count, 0))))
    pre_gate = jnp.einsum("erd,edf->erf", rows_in, w_gate, preferred_element_type=jnp.float32)
    pre_up = jnp.einsum("erd,edf->erf", rows_in, w_up, preferred_element_type=jnp.float32)
    sig_gate = jax.nn.sigmoid(pre_gate)
    act_rows = (pre_gate * sig_gate * pre_up).astype(jnp.bfloat16)
    out_rows = jnp.einsum(
        "erf,efd->erd", act_rows, w_down, preferred_element_type=jnp.float32
    ).astype(jnp.bfloat16)
    back_rows = expert_trade(from_experts(out_rows))
    returned = back_rows[dest_row].astype(jnp.float32)
    moe_sum = jnp.sum(
        (returned * pair_weights[:, None]).reshape(tok_rows, top_count, model_width), 1
    )
    layer_out = (hidden_f + moe_sum).astype(jnp.bfloat16)
    grad_f = grad_out.astype(jnp.float32)
    pair_grad = (jnp.repeat(grad_f, top_count, 0) * pair_weights[:, None]).astype(jnp.bfloat16)
    grad_in = to_experts(expert_trade(place_rows(pair_grad)))
    act_grad = jnp.einsum("erd,efd->erf", grad_in, w_down, preferred_element_type=jnp.float32)
    grad_w_down = jnp.einsum(
        "erf,erd->efd", act_rows, grad_in, preferred_element_type=jnp.float32
    ).astype(jnp.bfloat16)
    up_grad = (act_grad * pre_gate * sig_gate).astype(jnp.bfloat16)
    gate_grad = (act_grad * pre_up * sig_gate * (1.0 + pre_gate * (1.0 - sig_gate))).astype(
        jnp.bfloat16
    )
    grad_w_gate = jnp.einsum(
        "erd,erf->edf", rows_in, gate_grad, preferred_element_type=jnp.float32
    ).astype(jnp.bfloat16)
    grad_w_up = jnp.einsum(
        "erd,erf->edf", rows_in, up_grad, preferred_element_type=jnp.float32
    ).astype(jnp.bfloat16)
    row_grad = (
        jnp.einsum("erf,edf->erd", gate_grad, w_gate, preferred_element_type=jnp.float32)
        + jnp.einsum("erf,edf->erd", up_grad, w_up, preferred_element_type=jnp.float32)
    ).astype(jnp.bfloat16)
    back_grad = expert_trade(from_experts(row_grad))
    normed_grad = jnp.sum(
        back_grad[dest_row].astype(jnp.float32).reshape(tok_rows, top_count, model_width), 1
    )
    gain_part = jnp.sum(normed_grad * unit_rows, 0)
    grad_gain = lax.psum(gain_part, ("ctx", "exp"))
    scaled_grad = norm_gain * normed_grad
    hidden_grad = inv_rms * (
        scaled_grad - unit_rows * jnp.mean(scaled_grad * unit_rows, -1, keepdims=True)
    )
    grad_resid = (grad_f + hidden_grad).astype(jnp.bfloat16)
    block_grad = lax.all_gather(grad_resid, "exp", axis=0, tiled=True)
    mixture_gradient = jnp.einsum(
        "td,hd->th", block_grad, proj_full, preferred_element_type=jnp.float32
    ).astype(jnp.bfloat16)
    proj_part = jnp.einsum("th,td->hd", attn_mix, block_grad, preferred_element_type=jnp.float32)
    grad_out_proj = lax.psum_scatter(
        proj_part.astype(jnp.bfloat16), "ctx", scatter_dimension=1, tiled=True
    )
    mixture_quad = mixture_gradient.reshape(seq_rows, kv_heads, group_width, HEAD_SIZE)
    delta_sum = jnp.sum(mixture_quad.astype(jnp.float32) * attention_quad.astype(jnp.float32), -1)
    back_count = (query_start + seq_rows + block_len - 1) // block_len

    def backward_turn(loop_turn, loop_carry):
        query_grad, pair_store = loop_carry
        row_begin = loop_turn * block_len
        key_rows = lax.dynamic_slice_in_dim(keys_all, row_begin, block_len, 0)
        val_rows = lax.dynamic_slice_in_dim(values_all, row_begin, block_len, 0)
        scores = (
            jnp.einsum("bngd,knd->bngk", queries, key_rows, preferred_element_type=jnp.float32)
            * score_scale
        )
        key_pos = row_begin + jnp.arange(block_len, dtype=jnp.int32)
        visible = key_pos[None, :] <= query_pos[:, None]
        prob_full = jnp.where(
            visible[:, None, None, :], jnp.exp(scores - log_sum_total[..., None]), 0.0
        )
        prob_grad = jnp.einsum(
            "bngd,knd->bngk", mixture_quad, val_rows, preferred_element_type=jnp.float32
        )
        score_grad = prob_full * (prob_grad - delta_sum[..., None])
        prob_half = prob_full.astype(jnp.bfloat16)
        score_half = score_grad.astype(jnp.bfloat16)
        query_grad = (
            query_grad
            + jnp.einsum("bngk,knd->bngd", score_half, key_rows, preferred_element_type=jnp.float32)
            * score_scale
        )
        key_grad = (
            jnp.einsum("bngk,bngd->knd", score_half, queries, preferred_element_type=jnp.float32)
            * score_scale
        )
        value_grad = jnp.einsum(
            "bngk,bngd->knd", prob_half, mixture_quad, preferred_element_type=jnp.float32
        )
        pair_store = lax.dynamic_update_slice_in_dim(
            pair_store, jnp.stack([key_grad, value_grad], 2), row_begin, 0
        )
        return (query_grad, pair_store)

    start_back = (
        jnp.zeros(state_shape + (HEAD_SIZE,), jnp.float32),
        jnp.zeros((seq_total, kv_heads, 2, HEAD_SIZE), jnp.float32),
    )
    query_grad, pair_store = lax.fori_loop(0, back_count, backward_turn, start_back)
    grad_query = query_grad.reshape(seq_rows, kv_heads * group_width * HEAD_SIZE).astype(
        jnp.bfloat16
    )
    pair_sum = lax.psum_scatter(
        pair_store.reshape(seq_total, kv_heads * 2 * HEAD_SIZE).astype(jnp.bfloat16),
        "ctx",
        scatter_dimension=0,
        tiled=True,
    ).astype(jnp.float32)
    pair_sum = pair_sum.reshape(seq_rows, kv_heads, 2, HEAD_SIZE)
    key_gradient = pair_sum[:, :, 0].reshape(seq_rows, kv_heads * HEAD_SIZE).astype(jnp.bfloat16)
    value_gradient = pair_sum[:, :, 1].reshape(seq_rows, kv_heads * HEAD_SIZE).astype(jnp.bfloat16)
    return (
        layer_out,
        grad_resid,
        grad_query,
        key_gradient,
        value_gradient,
        grad_out_proj,
        grad_gain,
        grad_w_gate,
        grad_w_up,
        grad_w_down,
    )


F32 = jnp.float32
BF16 = jnp.bfloat16
LOG2E = 1.4426950408889634
SETS = (0, 2, 1, 3)


def crossed(x, bits):
    return lax.ppermute(x, "ctx", [(i, i ^ bits) for i in range(4)])


def swapped(x, bits):
    return lax.ppermute(x, "exp", [(i, i ^ bits) for i in range(4)])


def after(x, *others):
    return lax.optimization_barrier((x, *others))[0]


def nt(a, b):
    return lax.dot_general(a, b, (((1,), (1,)), ((), ())), preferred_element_type=F32)


def tn(a, b):
    return lax.dot_general(a, b, (((0,), (0,)), ((), ())), preferred_element_type=F32)


def nn(a, b):
    return lax.dot_general(a, b, (((1,), (0,)), ((), ())), preferred_element_type=F32)


def run_kernel(body, name, place, args, outs, scratch=(), flops=0, limit=16):
    vmem = pl.BlockSpec(memory_space=pltpu.VMEM)
    shapes = [jax.ShapeDtypeStruct(shape, dtype) for shape, dtype in outs]
    moved = sum(x.size * x.dtype.itemsize for x in list(args) + shapes)
    return pl.pallas_call(
        body,
        in_specs=[pl.BlockSpec(memory_space=pltpu.SMEM)] + [vmem] * len(args),
        out_specs=[vmem] * len(outs),
        out_shape=shapes,
        scratch_shapes=[pltpu.VMEM(shape, dtype) for shape, dtype in scratch],
        compiler_params=pltpu.CompilerParams(vmem_limit_bytes=limit << 20),
        cost_estimate=pl.CostEstimate(flops=flops, bytes_accessed=moved, transcendentals=0),
        name=name,
    )(place, *args)


def visible_keys(rows, count, query_block, base):
    shape = (rows, count * rows)
    key_pos = lax.broadcasted_iota(jnp.int32, shape, 1)
    turn = sum([(key_pos >= i * rows).astype(jnp.int32) for i in range(1, count)])
    offset = key_pos - turn * rows
    diagonal = offset <= lax.broadcasted_iota(jnp.int32, shape, 0)
    block = turn ^ base
    return (block < query_block) | ((block == query_block) & diagonal)


def pack_heads(place, key, value, query):
    rows, width = query.shape

    def body(place_ref, key_ref, value_ref, query_ref, out_ref):
        out_ref[:, :HEAD_SIZE] = key_ref[...]
        out_ref[:, HEAD_SIZE : 2 * HEAD_SIZE] = value_ref[...]
        out_ref[:, 2 * HEAD_SIZE :] = query_ref[...]

    shape = (rows, width + 2 * HEAD_SIZE)
    return run_kernel(body, "pack_heads", place, [key, value, query], [(shape, BF16)])[0]


def pack_rows(place, grad_out, routes, gate_weights, resid, cols):
    tok, width = grad_out.shape
    experts = 4 * (width // cols)

    def body(place_ref, grad_ref, route_ref, weight_ref, resid_ref, far_ref, near_ref, third_ref):
        lane = lax.broadcasted_iota(jnp.int32, (tok, 128), 1)
        weight = weight_ref[...]
        high = weight.astype(BF16).astype(F32)
        low = weight - high
        gates = jnp.zeros((tok, 128), F32)
        for k in range(routes.shape[1]):
            route = route_ref[:, k : k + 1]
            gates = gates + jnp.where(lane == route, high[:, k : k + 1], 0.0)
            gates = gates + jnp.where(lane == route + experts, low[:, k : k + 1], 0.0)

        def columns(turn):
            return resid_ref[:, pl.ds(pl.multiple_of((place_ref[0] ^ turn) * cols, cols), cols)]

        for ref, turn in ((far_ref, 2), (near_ref, 1)):
            ref[:, :width] = grad_ref[...]
            ref[:, width : width + 128] = gates.astype(BF16)
            ref[:, width + 128 :] = columns(turn)
        third_ref[...] = columns(3)

    message = ((tok, width + 128 + cols), BF16)
    return run_kernel(
        body,
        "pack_rows",
        place,
        [grad_out, routes, gate_weights, resid],
        [message, message, ((tok, cols), BF16)],
    )


def attend(place, parts, out_proj):
    n = len(parts)
    rows = parts[0].shape[0]
    width = out_proj.shape[0]
    tok = rows // 4
    cols = out_proj.shape[1]
    heads = width // HEAD_SIZE
    factor = HEAD_SIZE ** (-0.5) * LOG2E

    def body(place_ref, *refs):
        proj_ref, mix_ref, own_ref, keep_ref, send_ref, pairs_ref, everything, ps = refs[n:]
        c, e = place_ref[0], place_ref[1]
        for r in range(n):
            everything[pl.ds(pl.multiple_of((c ^ r) * rows, rows), rows), :] = refs[r][...]
            pairs_ref[r * rows : (r + 1) * rows, :] = refs[r][:, : 2 * HEAD_SIZE]
        keys, values = everything.at[:, :HEAD_SIZE], everything.at[:, HEAD_SIZE : 2 * HEAD_SIZE]
        below = lax.broadcasted_iota(jnp.int32, (rows, rows), 1) <= lax.broadcasted_iota(
            jnp.int32, (rows, rows), 0
        )
        for b in range(n):
            lo, hi = b * rows, (b + 1) * rows
            for first in range(0, heads, 8):
                queries = [
                    everything[lo:hi, (first + i + 2) * HEAD_SIZE : (first + i + 3) * HEAD_SIZE]
                    for i in range(8)
                ]
                scores = nt(jnp.concatenate(queries, 0), keys[:hi, :])
                last = jnp.where(jnp.concatenate([below] * 8, 0), scores[:, lo:], NEG)
                scores = jnp.concatenate([scores[:, :lo], last], 1) if b else last
                peak = jnp.max(scores, -1, keepdims=True)
                weights = jnp.exp2((scores - peak) * factor)
                total = jnp.sum(weights, -1, keepdims=True)
                mixed = nn(weights.astype(BF16), values[:hi, :]) * (1.0 / total)
                for i in range(8):
                    at = slice((first + i) * HEAD_SIZE, (first + i + 1) * HEAD_SIZE)
                    mix_ref[lo:hi, at] = mixed[i * rows : (i + 1) * rows].astype(BF16)
            ps[...] = nn(mix_ref[lo:hi, :], proj_ref[...]).astype(BF16)
            for turn in range(2):
                same, other = e ^ (2 * turn), e ^ (2 * turn + 1)
                keep_ref[turn, c ^ b] = ps[pl.ds(pl.multiple_of(same * tok, tok), tok), :]
                send_ref[turn, c ^ b] = ps[pl.ds(pl.multiple_of(other * tok, tok), tok), :]
        own_ref[...] = mix_ref[pl.ds(pl.multiple_of(c * rows, rows), rows), :]

    return run_kernel(
        body,
        "attend",
        place,
        [*parts, out_proj],
        [
            ((n * rows, width), BF16),
            ((rows, width), BF16),
            ((2, n, tok, cols), BF16),
            ((2, n, tok, cols), BF16),
            ((n * rows, 2 * HEAD_SIZE), BF16),
        ],
        [((n * rows, width + 2 * HEAD_SIZE), BF16), ((rows, cols), BF16)],
        flops=4 * n * rows * n * rows * width,
    )


def hidden_rows(place, keep, received, line, resid, near, far, third):
    cols = line.shape[2]
    last = near.shape[1] - cols

    def body(place_ref, keep_ref, received_ref, line_ref, resid_ref, near_ref, far_ref, third_ref, out_ref):
        total = keep_ref[0].astype(F32) + received_ref[0].astype(F32) + line_ref[...].astype(F32)
        own = resid_ref[:, pl.ds(pl.multiple_of(place_ref[0] * cols, cols), cols)]
        blocks = [own, near_ref[:, last:], far_ref[:, last:], third_ref[...]]
        for r, block in enumerate(blocks):
            out_ref[r] = (total[r] + block.astype(F32)).astype(BF16)

    return run_kernel(
        body,
        "hidden_rows",
        place,
        [keep, received, line, resid, near, far, third],
        [(line.shape, BF16)],
    )[0]


def grad_rows_of(place, grad_sets, w_down):
    lead, tok = grad_sets[0][0].shape[:2]
    n = lead + 1
    total = 4 * n * tok
    experts = 4 * n
    units, width = w_down.shape

    def body(place_ref, *refs):
        down_ref, rows_ref, gate_ref, act_ref = refs[8:]
        expert = place_ref[0] * 4 + place_ref[1]
        lane = lax.broadcasted_iota(jnp.int32, (tok, 128), 1)
        wanted = (lane == expert) | (lane == expert + experts)
        for s in range(4):
            for j in range(n):
                at = slice((s * n + j) * tok, (s * n + j + 1) * tok)
                block = refs[2 * s].at[j] if j < lead else refs[2 * s + 1]
                gate = jnp.where(wanted, block[:, width:].astype(F32), 0.0)
                gate = jnp.sum(gate, -1, keepdims=True)
                gate_ref[at, :] = gate
                rows_ref[at, :] = (block[:, :width].astype(F32) * gate).astype(BF16)
        act_ref[...] = nt(rows_ref[...], down_ref[...])

    return run_kernel(
        body,
        "grad_rows",
        place,
        [*sum(grad_sets, []), w_down],
        [((total, width), BF16), ((total, 1), F32), ((total, units), F32)],
        flops=2 * total * width * units,
        limit=24,
    )


def expert_rows(place, hidden_sets, act_grad, norm_gain, w_gate, w_up):
    n, tok, cols = hidden_sets[0][0].shape
    width, hidden_units = w_gate.shape
    group = n * tok
    total = 4 * group

    def body(place_ref, *refs):
        pieces = refs[: 4 * n]
        act_grad_ref, gain_ref, gate_ref, up_ref = refs[4 * n : 4 * n + 4]
        normed_ref, act_ref, gate_grad_ref, up_grad_ref, own_ref = refs[4 * n + 4 : 4 * n + 9]
        grads, sides, hid = refs[4 * n + 9 : 4 * n + 13], refs[4 * n + 13 : 4 * n + 15], refs[4 * n + 15]
        c = place_ref[0]
        for s in range(4):
            for d in range(n):
                at = pl.multiple_of((c ^ d) * cols, cols)
                for t in range(n):
                    row = s * group + (d ^ t) * tok
                    hid[row : row + tok, pl.ds(at, cols)] = pieces[s * n + d][t]
            rows = slice(s * group, (s + 1) * group)
            value = hid[rows, :].astype(F32)
            inv_rms = lax.rsqrt(jnp.mean(value * value, -1, keepdims=True) + EPS)
            normed_ref[rows, :] = (value * inv_rms * gain_ref[...]).astype(BF16)
        own_ref[...] = hid[:tok, :]
        pre_gate = nn(normed_ref[...], gate_ref[...])
        pre_up = nn(normed_ref[...], up_ref[...])
        sig = jax.nn.sigmoid(pre_gate)
        act_ref[...] = (pre_gate * sig * pre_up).astype(BF16)
        act_grad_value = act_grad_ref[...]
        up_grad_ref[...] = (act_grad_value * pre_gate * sig).astype(BF16)
        gate_grad_ref[...] = (
            act_grad_value * pre_up * sig * (1.0 + pre_gate * (1.0 - sig))
        ).astype(BF16)
        for j in range(n):
            at = slice(j * cols, (j + 1) * cols)
            part = nt(gate_grad_ref[...], gate_ref[at, :]) + nt(up_grad_ref[...], up_ref[at, :])
            for s in range(4):
                block = part[s * group : (s + 1) * group].astype(BF16).reshape(n, tok, cols)
                if j < n - 1:
                    grads[s][:, :, at] = block
                else:
                    sides[s // 2][:, s % 2] = block

    units = ((total, hidden_units), BF16)
    return run_kernel(
        body,
        "expert_rows",
        place,
        [*sum(hidden_sets, []), act_grad, norm_gain.reshape(1, width), w_gate, w_up],
        [((total, width), BF16), units, units, units, ((tok, width), BF16)]
        + [((n, tok, width - cols), BF16)] * 4
        + [((n, 2, tok, cols), BF16)] * 2,
        [((total, width), BF16)],
        flops=8 * total * width * hidden_units,
        limit=32,
    )


def weighted_rows(place, act_rows, gate, w_down, n):
    total = act_rows.shape[0]
    width = w_down.shape[1]
    group, cols = total // 4, width // n

    def body(place_ref, act_ref, gate_ref, down_ref, *outs):
        for j in range(n):
            at = slice(j * cols, (j + 1) * cols)
            part = nn(act_ref[...], down_ref[:, at]).astype(BF16).astype(F32) * gate_ref[...]
            for s in range(4):
                block = part[s * group : (s + 1) * group].astype(BF16)
                outs[s // 2][s % 2, :, :, at] = block.reshape(n, group // n, cols)

    return run_kernel(
        body,
        "weighted_rows",
        place,
        [act_rows, gate, w_down],
        [((2, n, group // n, width), BF16)] * 2,
        flops=2 * total * width * w_down.shape[0],
    )


def add(*xs):
    return sum([x.astype(F32) for x in xs[1:]], xs[0].astype(F32)).astype(BF16)


def sum_rows(parts, keep, send, beside, ready):
    side = swapped(send, 1)
    far = after(swapped(parts[3], 1), beside, side, ready)
    near = swapped(parts[2], 1)
    line = swapped(add(parts[1], far), 2)
    sides = [add(keep[j], side[j]) for j in range(4)]
    got = [crossed(sides[j], j) for j in range(1, 4)]
    total = add(sides[0], *got)
    sums = [after(add(parts[0][j], near[j], line[j]), total) for j in range(4)]
    wide = [sums[0]] + [crossed(sums[j], j) for j in range(1, 4)]
    return wide, [total[0], swapped(total[1], 2)]


def norm_backward(place, wide, narrow, hidden, grad_out, norm_gain, cols):
    n = len(wide) + len(narrow)
    tok, width = hidden.shape
    blocks = width // cols

    def body(place_ref, *refs):
        hidden_ref, grad_ref, gain_ref = refs[n : n + 3]
        out_ref, cuts, part_ref = refs[n + 3], refs[n + 4 : -1], refs[-1]
        c = place_ref[0]
        sums = [[r[...].astype(F32) for r in rs] for rs in (refs[: len(wide)], refs[len(wide) : n])]
        normed_grad = jnp.concatenate([sum(x[1:], x[0]) for x in sums], 1)
        value = hidden_ref[...].astype(F32)
        inv_rms = lax.rsqrt(jnp.mean(value * value, -1, keepdims=True) + EPS)
        unit_rows = value * inv_rms
        part = jnp.sum(normed_grad * unit_rows, 0, keepdims=True)
        high = part.astype(BF16)
        spare = jnp.zeros((14, width), BF16)
        part_ref[...] = jnp.concatenate([high, (part - high.astype(F32)).astype(BF16), spare], 0)
        scaled = gain_ref[...] * normed_grad
        mean = jnp.mean(scaled * unit_rows, -1, keepdims=True)
        grad = grad_ref[...].astype(F32) + inv_rms * (scaled - unit_rows * mean)
        out_ref[...] = grad.astype(BF16)
        for d in range(blocks):
            at = pl.ds(pl.multiple_of((c ^ d) * cols, cols), cols)
            to = slice(d % 2 * cols, (d % 2 + 1) * cols)
            cuts[d // 2][:tok, to] = out_ref[:, at]
            cuts[d // 2][tok:, to] = part_ref[:, at]

    return run_kernel(
        body,
        "norm_backward",
        place,
        [*wide, *narrow, hidden, grad_out, norm_gain.reshape(1, width)],
        [((tok, width), BF16)] + [((tok + 16, 2 * cols), BF16)] * (blocks // 2),
        [((16, width), BF16)],
    )


def layer_rows(place, summed, hidden):
    def body(place_ref, *refs):
        total = refs[-2][...].astype(F32)
        for r in refs[:-2]:
            total = total + r[...].astype(F32)
        refs[-1][...] = total.astype(BF16)

    return run_kernel(body, "layer_rows", place, [*summed, hidden], [(hidden.shape, BF16)])[0]


def mix_grad_parts(place, cut_sets, out_proj, proj_here, proj_there):
    count, cut, cols = cut_sets[0].shape
    tok, cols = cut - 16, cols // 2
    rows, width = 4 * tok, out_proj.shape[0]

    def body(place_ref, *refs):
        proj_ref, here_ref, there_ref, own_ref, far_ref, keep_ref, send_ref, gain_ref, grads, acc = refs[4:]
        e, g = place_ref[1], place_ref[2]
        gain = sum([refs[r][i, tok : tok + 2, :].astype(F32) for r in range(4) for i in range(count)])
        gain = jnp.sum(gain, 0, keepdims=True)
        high = gain.astype(BF16)
        low = (gain - high.astype(F32)).astype(BF16)
        half = cols // 2
        pieces = [x[:, i * half : (i + 1) * half] for x in (high, low) for i in range(4)]
        gain_ref[...] = jnp.concatenate([*pieces, jnp.zeros((8, half), BF16)], 0)
        for i in range(count):
            for r in range(4):
                at = pl.multiple_of(i * rows + (e ^ r) * tok, tok)
                grads[pl.ds(at, tok), :] = refs[r][i, :tok, :]
        for ref, at in ((keep_ref, slice(0, cols)), (send_ref, slice(cols, 2 * cols))):
            ref[...] = grads[:, at]
        half = width // 2
        for ref, index in ((here_ref, g), (there_ref, 1 - g)):
            at = pl.ds(pl.multiple_of(index * half, half), half)
            acc[:, at] = nt(grads[:, cols:], ref[...])
        for h in range(2):
            at = slice(h * half, (h + 1) * half)
            total = (acc[:, at] + nt(grads[:, :cols], proj_ref[at, :])).astype(BF16)
            own_ref[:, at] = total[:rows]
            far_ref[:, at] = total[rows:]

    return run_kernel(
        body,
        "mix_grad_parts",
        place,
        [*cut_sets, out_proj, proj_here, proj_there],
        [((rows, width), BF16)] * 2 + [((count * rows, cols), BF16)] * 2 + [((16, cols // 2), BF16)],
        [((count * rows, 2 * cols), BF16), ((count * rows, width), F32)],
        flops=4 * count * rows * cols * width,
    )


def attend_backward(place, grad_parts, query, pairs, mix, gain):
    g = len(grad_parts)
    rows, width = mix.shape
    n = pairs.shape[0] // rows
    heads = width // HEAD_SIZE
    scale = HEAD_SIZE ** (-0.5)

    def body(place_ref, *refs):
        g_refs, (query_ref, pairs_ref, mix_ref, gain_ref, dq_ref) = refs[:g], refs[g : g + 5]
        outs = refs[g + 5 : g + 5 + n]
        qs, ms, score_half, prob_half = refs[g + 5 + n :]
        ks, vs = pairs_ref.at[:, :HEAD_SIZE], pairs_ref.at[:, HEAD_SIZE:]
        c = place_ref[0]
        visible = visible_keys(rows, n, c, c)
        for head in range(heads):
            at = slice(head * HEAD_SIZE, (head + 1) * HEAD_SIZE)
            rs = slice(head * rows, (head + 1) * rows)
            grad = sum([x[:, at].astype(F32) for x in g_refs[1:]], g_refs[0][:, at].astype(F32))
            qs[rs, :] = query_ref[:, at]
            ms[rs, :] = grad.astype(BF16)
        for first in range(0, heads, 2):
            rs = slice(first * rows, (first + 2) * rows)
            scores = nt(qs[rs, :], ks[...]).reshape(2, rows, n * rows)
            scores = jnp.where(visible[None], scores, NEG).reshape(2 * rows, n * rows)
            peak = jnp.max(scores, -1, keepdims=True)
            weights = jnp.exp2((scores - peak) * (scale * LOG2E))
            prob = weights * (1.0 / jnp.sum(weights, -1, keepdims=True))
            mixes = [
                mix_ref[:, (first + i) * HEAD_SIZE : (first + i + 1) * HEAD_SIZE] for i in range(2)
            ]
            mixes = jnp.concatenate(mixes, 0).astype(F32)
            delta = jnp.sum(ms[rs, :].astype(F32) * mixes, -1, keepdims=True)
            score_half[rs, :] = (prob * (nt(ms[rs, :], vs[...]) - delta)).astype(BF16)
            prob_half[rs, :] = prob.astype(BF16)
        query_grad = nn(score_half[...], ks[...]) * scale
        for head in range(heads):
            at = slice(head * HEAD_SIZE, (head + 1) * HEAD_SIZE)
            dq_ref[:, at] = query_grad[head * rows : (head + 1) * rows].astype(BF16)
        key_sum = (tn(score_half[...], qs[...]) * scale).astype(BF16)
        value_sum = tn(prob_half[...], ms[...]).astype(BF16)
        for j in range(n):
            rs = slice(j * rows, (j + 1) * rows)
            outs[j][:rows, :HEAD_SIZE] = key_sum[rs]
            outs[j][:rows, HEAD_SIZE:] = value_sum[rs]
            outs[j][rows:, :] = gain_ref[...]

    stacked = ((heads * rows, HEAD_SIZE), BF16)
    halves = ((heads * rows, n * rows), BF16)
    return run_kernel(
        body,
        "attend_backward",
        place,
        [*grad_parts, query, pairs, mix, gain],
        [((rows, width), BF16)] + [((rows + 16, 2 * HEAD_SIZE), BF16)] * n,
        [stacked, stacked, halves, halves],
        flops=10 * rows * width * n * rows,
    )


def proj_grad(place, mix_all, keep, near):
    total, width = mix_all.shape
    rows, cols = total // 4, keep.shape[1]

    def body(place_ref, mix_ref, keep_ref, near_ref, out_ref, grads):
        c = place_ref[0]
        for d in range(4):
            ref = near_ref if d % 2 else keep_ref
            at = pl.multiple_of((c ^ d) * rows, rows)
            grads[pl.ds(at, rows), :] = ref[d // 2 * rows : (d // 2 + 1) * rows, :]
        out_ref[...] = tn(mix_ref[...], grads[...]).astype(BF16)

    return run_kernel(
        body,
        "proj_grad",
        place,
        [mix_all, keep, near],
        [((width, cols), BF16)],
        [((total, cols), BF16)],
        flops=2 * total * cols * width,
    )[0]


def pair_sums(place, parts):
    n = len(parts)
    rows = parts[0].shape[0] - 16
    half = parts[0].shape[1]

    def body(place_ref, *refs):
        key_ref, value_ref, gain_ref = refs[n:]
        c = place_ref[0]
        total = sum([r[:rows, :].astype(F32) for r in refs[1:n]], refs[0][:rows, :].astype(F32))
        key_ref[...] = total[:, :HEAD_SIZE].astype(BF16)
        value_ref[...] = total[:, HEAD_SIZE:].astype(BF16)
        gain_ref[...] = jnp.zeros(gain_ref.shape, F32)
        for j in range(n):
            tail = refs[j][rows : rows + 8, :].astype(F32)
            for i in range(4):
                at = pl.multiple_of(((c ^ j ^ (i // 2)) * 2 + i % 2) * half, half)
                gain_ref[:, pl.ds(at, half)] += tail[i : i + 1] + tail[i + 4 : i + 5]

    return run_kernel(
        body,
        "pair_sums",
        place,
        parts,
        [((rows, HEAD_SIZE), BF16), ((rows, HEAD_SIZE), BF16), ((1, 2 * n * half), F32)],
    )


def local_dense(
    resid,
    query,
    key,
    value,
    out_proj,
    norm_gain,
    w_gate,
    w_up,
    w_down,
    routes,
    gate_weights,
    grad_out,
):
    n = lax.axis_size("ctx")
    c, e, g = lax.axis_index("ctx"), lax.axis_index("exp"), lax.axis_index("groups")
    place = jnp.stack([c, e, g]).astype(jnp.int32)
    tok, width = resid.shape
    cols = out_proj.shape[1]
    scope = jax.named_scope

    def across(blocks):
        return [blocks[0]] + [crossed(blocks[r], r) for r in range(1, n)]

    with scope("gather_rows"):
        to_far, to_near, to_third = pack_rows(place, grad_out, routes, gate_weights, resid, cols)
    with scope("gather_heads"):
        heads = pack_heads(place, key, value, query)
        far, near = crossed(heads, 2), crossed(heads, 1)
        row_third = crossed(to_third, 3)
        parts = [heads, near, far, crossed(after(far, near, to_far, to_near, row_third), 1)]

    with scope("gather_rows"):
        to_far, to_near = lax.optimization_barrier((to_far, to_near, parts[3]))[:2]
        row_far, row_near = crossed(to_far, 2), crossed(to_near, 1)

    mix_all, mix, keep, send, pairs = attend(place, parts, out_proj)
    with scope("sum_heads"):
        received = swapped(send, 1)
        line = swapped(add(keep[1], received[1]), 2)
    hidden_block = hidden_rows(
        place, keep, received, line, resid, row_near, row_far, row_third
    )
    with scope("gather_rows"):
        size = width + 128
        rest = crossed(after(row_far[:, :size], line), 1)
        to_far, row_far, row_near = lax.optimization_barrier((to_far, row_far, row_near, hidden_block))[:3]
        grad_own = jnp.stack([to_far[:, :size], row_near[:, :size], row_far[:, :size]])
        grad_own, grad_line = [grad_own, rest], [swapped(grad_own, 2), swapped(rest, 2)]
        grad_sets = [grad_own, grad_line] + [
            [swapped(x, 1) for x in xs] for xs in (grad_own, grad_line)
        ]
    grad_rows, gate, act_grad = grad_rows_of(place, grad_sets, w_down[0])

    with scope("gather_hidden"):
        far, near = crossed(hidden_block, 2), crossed(hidden_block, 1)
        line = swapped(hidden_block, 2)
        hidden_own = [hidden_block, near, far, crossed(after(far, near), 1)]
        hidden_line = [line] + [swapped(after(x, line), 2) for x in hidden_own[1:3]]
        hidden_line.append(swapped(after(hidden_own[3], *hidden_line), 2))
    with scope("gather_proj"):
        half = out_proj.shape[0] // 2
        proj_half = lax.dynamic_slice_in_dim(out_proj, g * half, half, 0)
        proj_here = crossed(after(proj_half, hidden_own[3]), 1)
    with scope("gather_hidden"):
        hidden_line[-1], act_grad, proj_here = lax.optimization_barrier(
            (hidden_line[-1], act_grad, proj_here)
        )
        hidden_sets = [hidden_own, hidden_line] + [
            [swapped(x, 1) for x in xs] for xs in (hidden_own, hidden_line)
        ]

    with scope("gather_proj"):
        proj_there = lax.ppermute(proj_here, "groups", [(0, 1), (1, 0)])

    normed, act_rows, gate_grad, up_grad, hidden, *row_grads = expert_rows(
        place, hidden_sets, act_grad, norm_gain, w_gate[0], w_up[0]
    )
    out_keep, out_send = weighted_rows(place, act_rows, gate, w_down[0], n)
    with scope("sum_row_grads"):
        wide, narrow = sum_rows(row_grads[:4], *row_grads[4:], out_keep, proj_there)

    with scope("sum_outputs"):
        out_sent = swapped(out_send, 1)
        out_line = swapped(after(add(out_keep[1], out_sent[1]), wide[0]), 2)
    grad_w_down = tn(after(act_rows, wide[0]), grad_rows).astype(BF16)
    grad_resid, *cuts = norm_backward(
        place, wide, narrow, after(hidden, out_line, grad_w_down), grad_out, norm_gain, cols
    )

    with scope("gather_cuts"):
        cut_own = jnp.stack([cuts[0], crossed(cuts[1], 2)])
        cut_line = swapped(cut_own, 2)
        cut_sets = [cut_own, swapped(cut_own, 1), cut_line, swapped(cut_line, 1)]
    mix_own, mix_far, cut_keep, cut_send, gain_rows = mix_grad_parts(
        place, cut_sets, out_proj, proj_here, proj_there
    )
    with scope("sum_mix_grad"):
        mix_grads = [mix_own, crossed(mix_far, 2)]
    with scope("gather_cuts"):
        cut_near = crossed(cut_send, 1)

    with scope("sum_outputs"):
        out_sums = [add(out_keep[0][j], out_sent[0][j], out_line[j]) for j in range(n)]
        out_sums = [after(x, cut_own) for x in out_sums]
        second = add(out_sums[2], crossed(out_sums[3], 1))
        out_sums = [out_sums[0], crossed(out_sums[1], 1), crossed(second, 2)]
    normed, act_rows = lax.optimization_barrier((normed, act_rows, mix_own))[:2]
    grad_w_gate = tn(normed, gate_grad).astype(BF16)
    grad_w_up = tn(normed, up_grad).astype(BF16)
    grad_out_proj = proj_grad(place, mix_all, cut_keep, cut_near)
    mix_grads[0] = after(mix_own, grad_w_gate, grad_w_up, *out_sums[1:])

    grad_query, *pair_parts = attend_backward(place, mix_grads, query, pairs, mix, gain_rows)
    with scope("sum_pairs"):
        key_gradient, value_gradient, grad_gain = pair_sums(place, across(pair_parts))
    layer_out = layer_rows(place, out_sums, after(hidden, grad_query))

    return (
        layer_out,
        grad_resid,
        grad_query,
        key_gradient,
        value_gradient,
        grad_out_proj,
        grad_gain.reshape(width),
        grad_w_gate[None],
        grad_w_up[None],
        grad_w_down[None],
    )


def local(*args):
    key, w_gate, routes = args[2], args[6], args[9]
    ctx_count, exp_count = lax.axis_size("ctx"), lax.axis_size("exp")
    expert_total = w_gate.shape[0] * ctx_count * exp_count
    dense = (
        2 * routes.shape[1] >= expert_total
        and w_gate.shape[0] == 1
        and key.shape[1] == HEAD_SIZE
        and exp_count == 4
        and ctx_count == 4
        and lax.axis_size("groups") == 2
    )
    return (local_dense if dense else local_routed)(*args)


def solution(mesh):
    in_specs = (
        P(("groups", "ctx", "exp"), None),
        P(("groups", "ctx"), "exp"),
        P(("groups", "ctx"), "exp"),
        P(("groups", "ctx"), "exp"),
        P("exp", "ctx"),
        P(),
        P(("ctx", "exp"), None, None),
        P(("ctx", "exp"), None, None),
        P(("ctx", "exp"), None, None),
        P(("groups", "ctx", "exp"), None),
        P(("groups", "ctx", "exp"), None),
        P(("groups", "ctx", "exp"), None),
    )
    out_specs = (
        P(("groups", "ctx", "exp"), None),
        P(("groups", "ctx", "exp"), None),
        P(("groups", "ctx"), "exp"),
        P(("groups", "ctx"), "exp"),
        P(("groups", "ctx"), "exp"),
        P(("groups", "exp"), "ctx"),
        P("groups"),
        P(("groups", "ctx", "exp"), None, None),
        P(("groups", "ctx", "exp"), None, None),
        P(("groups", "ctx", "exp"), None, None),
    )
    return jax.shard_map(local, mesh=mesh, in_specs=in_specs, out_specs=out_specs, check_vma=False)
```

```python
import jax
import jax.numpy as jnp
from jax import lax
from jax.experimental import pallas as pl
from jax.experimental.pallas import tpu as pltpu
from jax.sharding import PartitionSpec as P

HEAD_SIZE = 128


EPS = 1e-06
NEG = -1e30


def attend_block(soft_state, queries, key_rows, val_rows, row_begin, query_pos, score_scale):
    peak_run, total_run, accum_rows = soft_state
    scores = (
        jnp.einsum("bngd,knd->bngk", queries, key_rows, preferred_element_type=jnp.float32)
        * score_scale
    )
    key_pos = row_begin + jnp.arange(key_rows.shape[0], dtype=jnp.int32)
    visible = key_pos[None, :] <= query_pos[:, None]
    scores = jnp.where(visible[:, None, None, :], scores, NEG)
    peak_new = jnp.maximum(peak_run, jnp.max(scores, -1))
    rescale = jnp.exp(peak_run - peak_new)
    weights = jnp.exp(scores - peak_new[..., None])
    total_new = total_run * rescale + jnp.sum(weights, -1)
    mixed_rows = jnp.einsum(
        "bngk,knd->bngd", weights.astype(jnp.bfloat16), val_rows, preferred_element_type=jnp.float32
    )
    return (peak_new, total_new, accum_rows * rescale[..., None] + mixed_rows)


def expert_trade(buffer):
    return lax.all_to_all(buffer, ("ctx", "exp"), split_axis=0, concat_axis=0, tiled=True)


def local_routed(
    resid,
    query,
    key,
    value,
    out_proj,
    norm_gain,
    w_gate,
    w_up,
    w_down,
    routes,
    gate_weights,
    grad_out,
):
    ctx_count = lax.axis_size("ctx")
    exp_count = lax.axis_size("exp")
    ctx_index = lax.axis_index("ctx")
    seq_rows = query.shape[0]
    kv_heads = key.shape[1] // HEAD_SIZE
    group_width = query.shape[1] // HEAD_SIZE // kv_heads
    seq_total = seq_rows * ctx_count
    score_scale = HEAD_SIZE ** (-0.5)
    query_start = ctx_index * seq_rows
    query_pos = query_start + jnp.arange(seq_rows, dtype=jnp.int32)
    queries = query.reshape(seq_rows, kv_heads, group_width, HEAD_SIZE)
    state_shape = (seq_rows, kv_heads, group_width)
    start_state = (
        jnp.full(state_shape, NEG, jnp.float32),
        jnp.zeros(state_shape, jnp.float32),
        jnp.zeros(state_shape + (HEAD_SIZE,), jnp.float32),
    )
    block_len = min(512, seq_total)
    keys_flat, values_flat = (
        lax.all_gather(key, "ctx", axis=0, tiled=True),
        lax.all_gather(value, "ctx", axis=0, tiled=True),
    )
    keys_all = keys_flat.reshape(seq_total, kv_heads, HEAD_SIZE)
    values_all = values_flat.reshape(seq_total, kv_heads, HEAD_SIZE)
    block_count = (query_start + seq_rows + block_len - 1) // block_len

    def forward_turn(loop_turn, soft_state):
        row_begin = loop_turn * block_len
        key_rows = lax.dynamic_slice_in_dim(keys_all, row_begin, block_len, 0)
        val_rows = lax.dynamic_slice_in_dim(values_all, row_begin, block_len, 0)
        return attend_block(
            soft_state, queries, key_rows, val_rows, row_begin, query_pos, score_scale
        )

    soft_state = lax.fori_loop(0, block_count, forward_turn, start_state)
    peak_val, total_val, accum_rows = soft_state
    attention_quad = (accum_rows / total_val[..., None]).astype(jnp.bfloat16)
    attn_mix = attention_quad.reshape(seq_rows, kv_heads * group_width * HEAD_SIZE)
    log_sum_total = peak_val + jnp.log(total_val)
    proj_full = lax.all_gather(out_proj, "ctx", axis=1, tiled=True)
    tok_rows = resid.shape[0]
    proj_sum = lax.psum_scatter(
        jnp.dot(attn_mix, proj_full, preferred_element_type=jnp.float32).astype(jnp.bfloat16),
        "exp",
        scatter_dimension=0,
        tiled=True,
    ).astype(jnp.float32)
    hidden = (resid.astype(jnp.float32) + proj_sum).astype(jnp.bfloat16)
    hidden_f = hidden.astype(jnp.float32)
    inv_rms = lax.rsqrt(jnp.mean(hidden_f * hidden_f, -1, keepdims=True) + EPS)
    unit_rows = hidden_f * inv_rms
    normed = (unit_rows * norm_gain).astype(jnp.bfloat16)
    top_count = routes.shape[1]
    model_width = normed.shape[1]
    experts_local = w_gate.shape[0]
    device_count = ctx_count * exp_count
    expert_total = experts_local * device_count
    capacity = 2 * tok_rows * top_count // expert_total
    flat_routes = routes.reshape(-1)
    member = (flat_routes[:, None] == jnp.arange(expert_total, dtype=jnp.int32)[None, :]).astype(
        jnp.int32
    )
    slot_pos = jnp.sum(jnp.cumsum(member, 0) * member, 1) - 1
    dest_row = flat_routes * capacity + slot_pos
    pair_weights = gate_weights.reshape(-1)

    def place_rows(rows_out):
        return (
            jnp.zeros((expert_total * capacity, model_width), jnp.bfloat16)
            .at[dest_row]
            .set(rows_out)
        )

    def to_experts(buffer):
        return (
            buffer.reshape(device_count, experts_local, capacity, model_width)
            .transpose(1, 0, 2, 3)
            .reshape(experts_local, device_count * capacity, model_width)
        )

    def from_experts(rows_back):
        return (
            rows_back.reshape(experts_local, device_count, capacity, model_width)
            .transpose(1, 0, 2, 3)
            .reshape(device_count * experts_local * capacity, model_width)
        )

    rows_in = to_experts(expert_trade(place_rows(jnp.repeat(normed, top_count, 0))))
    pre_gate = jnp.einsum("erd,edf->erf", rows_in, w_gate, preferred_element_type=jnp.float32)
    pre_up = jnp.einsum("erd,edf->erf", rows_in, w_up, preferred_element_type=jnp.float32)
    sig_gate = jax.nn.sigmoid(pre_gate)
    act_rows = (pre_gate * sig_gate * pre_up).astype(jnp.bfloat16)
    out_rows = jnp.einsum(
        "erf,efd->erd", act_rows, w_down, preferred_element_type=jnp.float32
    ).astype(jnp.bfloat16)
    back_rows = expert_trade(from_experts(out_rows))
    returned = back_rows[dest_row].astype(jnp.float32)
    moe_sum = jnp.sum(
        (returned * pair_weights[:, None]).reshape(tok_rows, top_count, model_width), 1
    )
    layer_out = (hidden_f + moe_sum).astype(jnp.bfloat16)
    grad_f = grad_out.astype(jnp.float32)
    pair_grad = (jnp.repeat(grad_f, top_count, 0) * pair_weights[:, None]).astype(jnp.bfloat16)
    grad_in = to_experts(expert_trade(place_rows(pair_grad)))
    act_grad = jnp.einsum("erd,efd->erf", grad_in, w_down, preferred_element_type=jnp.float32)
    grad_w_down = jnp.einsum(
        "erf,erd->efd", act_rows, grad_in, preferred_element_type=jnp.float32
    ).astype(jnp.bfloat16)
    up_grad = (act_grad * pre_gate * sig_gate).astype(jnp.bfloat16)
    gate_grad = (act_grad * pre_up * sig_gate * (1.0 + pre_gate * (1.0 - sig_gate))).astype(
        jnp.bfloat16
    )
    grad_w_gate = jnp.einsum(
        "erd,erf->edf", rows_in, gate_grad, preferred_element_type=jnp.float32
    ).astype(jnp.bfloat16)
    grad_w_up = jnp.einsum(
        "erd,erf->edf", rows_in, up_grad, preferred_element_type=jnp.float32
    ).astype(jnp.bfloat16)
    row_grad = (
        jnp.einsum("erf,edf->erd", gate_grad, w_gate, preferred_element_type=jnp.float32)
        + jnp.einsum("erf,edf->erd", up_grad, w_up, preferred_element_type=jnp.float32)
    ).astype(jnp.bfloat16)
    back_grad = expert_trade(from_experts(row_grad))
    normed_grad = jnp.sum(
        back_grad[dest_row].astype(jnp.float32).reshape(tok_rows, top_count, model_width), 1
    )
    gain_part = jnp.sum(normed_grad * unit_rows, 0)
    grad_gain = lax.psum(gain_part, ("ctx", "exp"))
    scaled_grad = norm_gain * normed_grad
    hidden_grad = inv_rms * (
        scaled_grad - unit_rows * jnp.mean(scaled_grad * unit_rows, -1, keepdims=True)
    )
    grad_resid = (grad_f + hidden_grad).astype(jnp.bfloat16)
    block_grad = lax.all_gather(grad_resid, "exp", axis=0, tiled=True)
    mixture_gradient = jnp.einsum(
        "td,hd->th", block_grad, proj_full, preferred_element_type=jnp.float32
    ).astype(jnp.bfloat16)
    proj_part = jnp.einsum("th,td->hd", attn_mix, block_grad, preferred_element_type=jnp.float32)
    grad_out_proj = lax.psum_scatter(
        proj_part.astype(jnp.bfloat16), "ctx", scatter_dimension=1, tiled=True
    )
    mixture_quad = mixture_gradient.reshape(seq_rows, kv_heads, group_width, HEAD_SIZE)
    delta_sum = jnp.sum(mixture_quad.astype(jnp.float32) * attention_quad.astype(jnp.float32), -1)
    back_count = (query_start + seq_rows + block_len - 1) // block_len

    def backward_turn(loop_turn, loop_carry):
        query_grad, pair_store = loop_carry
        row_begin = loop_turn * block_len
        key_rows = lax.dynamic_slice_in_dim(keys_all, row_begin, block_len, 0)
        val_rows = lax.dynamic_slice_in_dim(values_all, row_begin, block_len, 0)
        scores = (
            jnp.einsum("bngd,knd->bngk", queries, key_rows, preferred_element_type=jnp.float32)
            * score_scale
        )
        key_pos = row_begin + jnp.arange(block_len, dtype=jnp.int32)
        visible = key_pos[None, :] <= query_pos[:, None]
        prob_full = jnp.where(
            visible[:, None, None, :], jnp.exp(scores - log_sum_total[..., None]), 0.0
        )
        prob_grad = jnp.einsum(
            "bngd,knd->bngk", mixture_quad, val_rows, preferred_element_type=jnp.float32
        )
        score_grad = prob_full * (prob_grad - delta_sum[..., None])
        prob_half = prob_full.astype(jnp.bfloat16)
        score_half = score_grad.astype(jnp.bfloat16)
        query_grad = (
            query_grad
            + jnp.einsum("bngk,knd->bngd", score_half, key_rows, preferred_element_type=jnp.float32)
            * score_scale
        )
        key_grad = (
            jnp.einsum("bngk,bngd->knd", score_half, queries, preferred_element_type=jnp.float32)
            * score_scale
        )
        value_grad = jnp.einsum(
            "bngk,bngd->knd", prob_half, mixture_quad, preferred_element_type=jnp.float32
        )
        pair_store = lax.dynamic_update_slice_in_dim(
            pair_store, jnp.stack([key_grad, value_grad], 2), row_begin, 0
        )
        return (query_grad, pair_store)

    start_back = (
        jnp.zeros(state_shape + (HEAD_SIZE,), jnp.float32),
        jnp.zeros((seq_total, kv_heads, 2, HEAD_SIZE), jnp.float32),
    )
    query_grad, pair_store = lax.fori_loop(0, back_count, backward_turn, start_back)
    grad_query = query_grad.reshape(seq_rows, kv_heads * group_width * HEAD_SIZE).astype(
        jnp.bfloat16
    )
    pair_sum = lax.psum_scatter(
        pair_store.reshape(seq_total, kv_heads * 2 * HEAD_SIZE).astype(jnp.bfloat16),
        "ctx",
        scatter_dimension=0,
        tiled=True,
    ).astype(jnp.float32)
    pair_sum = pair_sum.reshape(seq_rows, kv_heads, 2, HEAD_SIZE)
    key_gradient = pair_sum[:, :, 0].reshape(seq_rows, kv_heads * HEAD_SIZE).astype(jnp.bfloat16)
    value_gradient = pair_sum[:, :, 1].reshape(seq_rows, kv_heads * HEAD_SIZE).astype(jnp.bfloat16)
    return (
        layer_out,
        grad_resid,
        grad_query,
        key_gradient,
        value_gradient,
        grad_out_proj,
        grad_gain,
        grad_w_gate,
        grad_w_up,
        grad_w_down,
    )


F32 = jnp.float32
BF16 = jnp.bfloat16
LOG2E = 1.4426950408889634
SETS = (0, 2, 1, 3)


def crossed(x, bits):
    return lax.ppermute(x, "ctx", [(i, i ^ bits) for i in range(4)])


def swapped(x, bits):
    return lax.ppermute(x, "exp", [(i, i ^ bits) for i in range(4)])


def after(x, *others):
    return lax.optimization_barrier((x, *others))[0]


def nt(a, b):
    return lax.dot_general(a, b, (((1,), (1,)), ((), ())), preferred_element_type=F32)


def tn(a, b):
    return lax.dot_general(a, b, (((0,), (0,)), ((), ())), preferred_element_type=F32)


def nn(a, b):
    return lax.dot_general(a, b, (((1,), (0,)), ((), ())), preferred_element_type=F32)


def run_kernel(body, name, place, args, outs, scratch=(), flops=0, limit=16):
    vmem = pl.BlockSpec(memory_space=pltpu.VMEM)
    shapes = [jax.ShapeDtypeStruct(shape, dtype) for shape, dtype in outs]
    moved = sum(x.size * x.dtype.itemsize for x in list(args) + shapes)
    return pl.pallas_call(
        body,
        in_specs=[pl.BlockSpec(memory_space=pltpu.SMEM)] + [vmem] * len(args),
        out_specs=[vmem] * len(outs),
        out_shape=shapes,
        scratch_shapes=[pltpu.VMEM(shape, dtype) for shape, dtype in scratch],
        compiler_params=pltpu.CompilerParams(vmem_limit_bytes=limit << 20),
        cost_estimate=pl.CostEstimate(flops=flops, bytes_accessed=moved, transcendentals=0),
        name=name,
    )(place, *args)


def visible_keys(rows, count, query_block, base):
    shape = (rows, count * rows)
    key_pos = lax.broadcasted_iota(jnp.int32, shape, 1)
    turn = sum([(key_pos >= i * rows).astype(jnp.int32) for i in range(1, count)])
    offset = key_pos - turn * rows
    diagonal = offset <= lax.broadcasted_iota(jnp.int32, shape, 0)
    block = turn ^ base
    return (block < query_block) | ((block == query_block) & diagonal)


def pack_rows(place, grad_out, routes, gate_weights, resid, cols):
    tok, width = grad_out.shape
    experts = 4 * (width // cols)

    def body(place_ref, grad_ref, route_ref, weight_ref, resid_ref, far_ref, near_ref, third_ref):
        lane = lax.broadcasted_iota(jnp.int32, (tok, 128), 1)
        weight = weight_ref[...]
        high = weight.astype(BF16).astype(F32)
        low = weight - high
        gates = jnp.zeros((tok, 128), F32)
        for k in range(routes.shape[1]):
            route = route_ref[:, k : k + 1]
            gates = gates + jnp.where(lane == route, high[:, k : k + 1], 0.0)
            gates = gates + jnp.where(lane == route + experts, low[:, k : k + 1], 0.0)

        def columns(turn):
            return resid_ref[:, pl.ds(pl.multiple_of((place_ref[0] ^ turn) * cols, cols), cols)]

        for ref, turn in ((far_ref, 2), (near_ref, 1)):
            ref[:, :width] = grad_ref[...]
            ref[:, width : width + 128] = gates.astype(BF16)
            ref[:, width + 128 :] = columns(turn)
        third_ref[...] = columns(3)

    message = ((tok, width + 128 + cols), BF16)
    return run_kernel(
        body,
        "pack_rows",
        place,
        [grad_out, routes, gate_weights, resid],
        [message, message, ((tok, cols), BF16)],
    )


def attend(place, parts, out_proj):
    n = len(parts)
    rows = parts[0].shape[0]
    width = out_proj.shape[0]
    tok = rows // 4
    cols = out_proj.shape[1]
    heads = width // HEAD_SIZE
    factor = HEAD_SIZE ** (-0.5) * LOG2E

    def body(place_ref, *refs):
        proj_ref, mix_ref, own_ref, keep_ref, send_ref, pairs_ref, everything, ps = refs[n:]
        c, e = place_ref[0], place_ref[1]
        for r in range(n):
            everything[pl.ds(pl.multiple_of((c ^ r) * rows, rows), rows), :] = refs[r][...]
            pairs_ref[r * rows : (r + 1) * rows, :] = refs[r][:, : 2 * HEAD_SIZE]
        keys, values = everything.at[:, :HEAD_SIZE], everything.at[:, HEAD_SIZE : 2 * HEAD_SIZE]
        below = lax.broadcasted_iota(jnp.int32, (rows, rows), 1) <= lax.broadcasted_iota(
            jnp.int32, (rows, rows), 0
        )
        for b in range(n):
            lo, hi = b * rows, (b + 1) * rows
            for first in range(0, heads, 8):
                queries = [
                    everything[lo:hi, (first + i + 2) * HEAD_SIZE : (first + i + 3) * HEAD_SIZE]
                    for i in range(8)
                ]
                scores = nt(jnp.concatenate(queries, 0), keys[:hi, :])
                last = jnp.where(jnp.concatenate([below] * 8, 0), scores[:, lo:], NEG)
                scores = jnp.concatenate([scores[:, :lo], last], 1) if b else last
                peak = jnp.max(scores, -1, keepdims=True)
                weights = jnp.exp2((scores - peak) * factor)
                total = jnp.sum(weights, -1, keepdims=True)
                mixed = nn(weights.astype(BF16), values[:hi, :]) * (1.0 / total)
                for i in range(8):
                    at = slice((first + i) * HEAD_SIZE, (first + i + 1) * HEAD_SIZE)
                    mix_ref[lo:hi, at] = mixed[i * rows : (i + 1) * rows].astype(BF16)
            ps[...] = nn(mix_ref[lo:hi, :], proj_ref[...]).astype(BF16)
            for turn in range(2):
                same, other = e ^ (2 * turn), e ^ (2 * turn + 1)
                keep_ref[turn, c ^ b] = ps[pl.ds(pl.multiple_of(same * tok, tok), tok), :]
                send_ref[turn, c ^ b] = ps[pl.ds(pl.multiple_of(other * tok, tok), tok), :]
        own_ref[...] = mix_ref[pl.ds(pl.multiple_of(c * rows, rows), rows), :]

    return run_kernel(
        body,
        "attend",
        place,
        [*parts, out_proj],
        [
            ((n * rows, width), BF16),
            ((rows, width), BF16),
            ((2, n, tok, cols), BF16),
            ((2, n, tok, cols), BF16),
            ((n * rows, 2 * HEAD_SIZE), BF16),
        ],
        [((n * rows, width + 2 * HEAD_SIZE), BF16), ((rows, cols), BF16)],
        flops=4 * n * rows * n * rows * width,
    )


def hidden_rows(place, keep, received, line, resid, near, far, third):
    cols = line.shape[2]
    last = near.shape[1] - cols

    def body(place_ref, keep_ref, received_ref, line_ref, resid_ref, near_ref, far_ref, third_ref, out_ref):
        total = keep_ref[0].astype(F32) + received_ref[0].astype(F32) + line_ref[...].astype(F32)
        own = resid_ref[:, pl.ds(pl.multiple_of(place_ref[0] * cols, cols), cols)]
        blocks = [own, near_ref[:, last:], far_ref[:, last:], third_ref[...]]
        for r, block in enumerate(blocks):
            out_ref[r] = (total[r] + block.astype(F32)).astype(BF16)

    return run_kernel(
        body,
        "hidden_rows",
        place,
        [keep, received, line, resid, near, far, third],
        [(line.shape, BF16)],
    )[0]


def grad_rows_of(place, grad_sets, w_down):
    lead, tok = grad_sets[0][0].shape[:2]
    n = lead + 1
    total = 4 * n * tok
    experts = 4 * n
    units, width = w_down.shape

    def body(place_ref, *refs):
        down_ref, rows_ref, gate_ref, act_ref = refs[8:]
        expert = place_ref[0] * 4 + place_ref[1]
        lane = lax.broadcasted_iota(jnp.int32, (tok, 128), 1)
        wanted = (lane == expert) | (lane == expert + experts)
        for s in range(4):
            for j in range(n):
                at = slice((s * n + j) * tok, (s * n + j + 1) * tok)
                block = refs[2 * s].at[j] if j < lead else refs[2 * s + 1]
                gate = jnp.where(wanted, block[:, width:].astype(F32), 0.0)
                gate = jnp.sum(gate, -1, keepdims=True)
                gate_ref[at, :] = gate
                rows_ref[at, :] = (block[:, :width].astype(F32) * gate).astype(BF16)
        act_ref[...] = nt(rows_ref[...], down_ref[...])

    return run_kernel(
        body,
        "grad_rows",
        place,
        [*sum(grad_sets, []), w_down],
        [((total, width), BF16), ((total, 1), F32), ((total, units), F32)],
        flops=2 * total * width * units,
        limit=24,
    )


def expert_rows(place, hidden_sets, act_grad, norm_gain, w_gate, w_up):
    n, tok, cols = hidden_sets[0][0].shape
    width, hidden_units = w_gate.shape
    group = n * tok
    total = 4 * group

    def body(place_ref, *refs):
        pieces = refs[: 4 * n]
        act_grad_ref, gain_ref, gate_ref, up_ref = refs[4 * n : 4 * n + 4]
        normed_ref, act_ref, gate_grad_ref, up_grad_ref, own_ref = refs[4 * n + 4 : 4 * n + 9]
        grads, sides, hid = refs[4 * n + 9 : 4 * n + 13], refs[4 * n + 13 : 4 * n + 15], refs[4 * n + 15]
        c = place_ref[0]
        for s in range(4):
            for d in range(n):
                at = pl.multiple_of((c ^ d) * cols, cols)
                for t in range(n):
                    row = s * group + (d ^ t) * tok
                    hid[row : row + tok, pl.ds(at, cols)] = pieces[s * n + d][t]
            rows = slice(s * group, (s + 1) * group)
            value = hid[rows, :].astype(F32)
            inv_rms = lax.rsqrt(jnp.mean(value * value, -1, keepdims=True) + EPS)
            normed_ref[rows, :] = (value * inv_rms * gain_ref[...]).astype(BF16)
        own_ref[...] = hid[:tok, :]
        pre_gate = nn(normed_ref[...], gate_ref[...])
        pre_up = nn(normed_ref[...], up_ref[...])
        sig = jax.nn.sigmoid(pre_gate)
        act_ref[...] = (pre_gate * sig * pre_up).astype(BF16)
        act_grad_value = act_grad_ref[...]
        up_grad_ref[...] = (act_grad_value * pre_gate * sig).astype(BF16)
        gate_grad_ref[...] = (
            act_grad_value * pre_up * sig * (1.0 + pre_gate * (1.0 - sig))
        ).astype(BF16)
        for j in range(n):
            at = slice(j * cols, (j + 1) * cols)
            part = nt(gate_grad_ref[...], gate_ref[at, :]) + nt(up_grad_ref[...], up_ref[at, :])
            for s in range(4):
                block = part[s * group : (s + 1) * group].astype(BF16).reshape(n, tok, cols)
                if j < n - 1:
                    grads[s][:, :, at] = block
                else:
                    sides[s // 2][:, s % 2] = block

    units = ((total, hidden_units), BF16)
    return run_kernel(
        body,
        "expert_rows",
        place,
        [*sum(hidden_sets, []), act_grad, norm_gain.reshape(1, width), w_gate, w_up],
        [((total, width), BF16), units, units, units, ((tok, width), BF16)]
        + [((n, tok, width - cols), BF16)] * 4
        + [((n, 2, tok, cols), BF16)] * 2,
        [((total, width), BF16)],
        flops=8 * total * width * hidden_units,
        limit=32,
    )


def weighted_rows(place, act_rows, gate, w_down, n):
    total = act_rows.shape[0]
    width = w_down.shape[1]
    group, cols = total // 4, width // n

    def body(place_ref, act_ref, gate_ref, down_ref, *outs):
        for j in range(n):
            at = slice(j * cols, (j + 1) * cols)
            part = nn(act_ref[...], down_ref[:, at]).astype(BF16).astype(F32) * gate_ref[...]
            for s in range(4):
                block = part[s * group : (s + 1) * group].astype(BF16)
                outs[s // 2][s % 2, :, :, at] = block.reshape(n, group // n, cols)

    return run_kernel(
        body,
        "weighted_rows",
        place,
        [act_rows, gate, w_down],
        [((2, n, group // n, width), BF16)] * 2,
        flops=2 * total * width * w_down.shape[0],
    )


def add(*xs):
    return sum([x.astype(F32) for x in xs[1:]], xs[0].astype(F32)).astype(BF16)


def sum_rows(parts, keep, send, beside, ready):
    side = swapped(send, 1)
    far = after(swapped(parts[3], 1), beside, side, ready)
    near = swapped(parts[2], 1)
    line = swapped(add(parts[1], far), 2)
    sides = [add(keep[j], side[j]) for j in range(4)]
    got = [crossed(sides[j], j) for j in range(1, 4)]
    total = add(sides[0], *got)
    sums = [after(add(parts[0][j], near[j], line[j]), total) for j in range(4)]
    wide = [sums[0]] + [crossed(sums[j], j) for j in range(1, 4)]
    return wide, [total[0], swapped(total[1], 2)]


def norm_backward(place, wide, narrow, hidden, grad_out, norm_gain, cols):
    n = len(wide) + len(narrow)
    tok, width = hidden.shape
    blocks = width // cols

    def body(place_ref, *refs):
        hidden_ref, grad_ref, gain_ref = refs[n : n + 3]
        out_ref, cuts, part_ref = refs[n + 3], refs[n + 4 : -1], refs[-1]
        c = place_ref[0]
        sums = [[r[...].astype(F32) for r in rs] for rs in (refs[: len(wide)], refs[len(wide) : n])]
        normed_grad = jnp.concatenate([sum(x[1:], x[0]) for x in sums], 1)
        value = hidden_ref[...].astype(F32)
        inv_rms = lax.rsqrt(jnp.mean(value * value, -1, keepdims=True) + EPS)
        unit_rows = value * inv_rms
        part = jnp.sum(normed_grad * unit_rows, 0, keepdims=True)
        high = part.astype(BF16)
        spare = jnp.zeros((14, width), BF16)
        part_ref[...] = jnp.concatenate([high, (part - high.astype(F32)).astype(BF16), spare], 0)
        scaled = gain_ref[...] * normed_grad
        mean = jnp.mean(scaled * unit_rows, -1, keepdims=True)
        grad = grad_ref[...].astype(F32) + inv_rms * (scaled - unit_rows * mean)
        out_ref[...] = grad.astype(BF16)
        for d in range(blocks):
            at = pl.ds(pl.multiple_of((c ^ d) * cols, cols), cols)
            to = slice(d % 2 * cols, (d % 2 + 1) * cols)
            cuts[d // 2][:tok, to] = out_ref[:, at]
            cuts[d // 2][tok:, to] = part_ref[:, at]

    return run_kernel(
        body,
        "norm_backward",
        place,
        [*wide, *narrow, hidden, grad_out, norm_gain.reshape(1, width)],
        [((tok, width), BF16)] + [((tok + 16, 2 * cols), BF16)] * (blocks // 2),
        [((16, width), BF16)],
    )


def layer_rows(place, summed, hidden):
    def body(place_ref, *refs):
        total = refs[-2][...].astype(F32)
        for r in refs[:-2]:
            total = total + r[...].astype(F32)
        refs[-1][...] = total.astype(BF16)

    return run_kernel(body, "layer_rows", place, [*summed, hidden], [(hidden.shape, BF16)])[0]


def mix_grad_parts(place, cut_sets, out_proj, proj_here, proj_there):
    count, cut, cols = cut_sets[0].shape
    tok, cols = cut - 16, cols // 2
    rows, width = 4 * tok, out_proj.shape[0]

    def body(place_ref, *refs):
        proj_ref, here_ref, there_ref, own_ref, far_ref, keep_ref, send_ref, gain_ref, grads, acc = refs[4:]
        e, g = place_ref[1], place_ref[2]
        gain = sum([refs[r][i, tok : tok + 2, :].astype(F32) for r in range(4) for i in range(count)])
        gain = jnp.sum(gain, 0, keepdims=True)
        high = gain.astype(BF16)
        low = (gain - high.astype(F32)).astype(BF16)
        half = cols // 2
        pieces = [x[:, i * half : (i + 1) * half] for x in (high, low) for i in range(4)]
        gain_ref[...] = jnp.concatenate([*pieces, jnp.zeros((8, half), BF16)], 0)
        for i in range(count):
            for r in range(4):
                at = pl.multiple_of(i * rows + (e ^ r) * tok, tok)
                grads[pl.ds(at, tok), :] = refs[r][i, :tok, :]
        for ref, at in ((keep_ref, slice(0, cols)), (send_ref, slice(cols, 2 * cols))):
            ref[...] = grads[:, at]
        half = width // 2
        for ref, index in ((here_ref, g), (there_ref, 1 - g)):
            at = pl.ds(pl.multiple_of(index * half, half), half)
            acc[:, at] = nt(grads[:, cols:], ref[...])
        for h in range(2):
            at = slice(h * half, (h + 1) * half)
            total = (acc[:, at] + nt(grads[:, :cols], proj_ref[at, :])).astype(BF16)
            own_ref[:, at] = total[:rows]
            far_ref[:, at] = total[rows:]

    return run_kernel(
        body,
        "mix_grad_parts",
        place,
        [*cut_sets, out_proj, proj_here, proj_there],
        [((rows, width), BF16)] * 2 + [((count * rows, cols), BF16)] * 2 + [((16, cols // 2), BF16)],
        [((count * rows, 2 * cols), BF16), ((count * rows, width), F32)],
        flops=4 * count * rows * cols * width,
    )


def attend_backward(place, grad_parts, query, pairs, mix, gain):
    g = len(grad_parts)
    rows, width = mix.shape
    n = pairs.shape[0] // rows
    heads = width // HEAD_SIZE
    scale = HEAD_SIZE ** (-0.5)

    def body(place_ref, *refs):
        g_refs, (query_ref, pairs_ref, mix_ref, gain_ref, dq_ref) = refs[:g], refs[g : g + 5]
        outs = refs[g + 5 : g + 5 + n]
        qs, ms, score_half, prob_half = refs[g + 5 + n :]
        ks, vs = pairs_ref.at[:, :HEAD_SIZE], pairs_ref.at[:, HEAD_SIZE:]
        c = place_ref[0]
        visible = visible_keys(rows, n, c, c)
        for head in range(heads):
            at = slice(head * HEAD_SIZE, (head + 1) * HEAD_SIZE)
            rs = slice(head * rows, (head + 1) * rows)
            grad = sum([x[:, at].astype(F32) for x in g_refs[1:]], g_refs[0][:, at].astype(F32))
            qs[rs, :] = query_ref[:, at]
            ms[rs, :] = grad.astype(BF16)
        for first in range(0, heads, 2):
            rs = slice(first * rows, (first + 2) * rows)
            scores = nt(qs[rs, :], ks[...]).reshape(2, rows, n * rows)
            scores = jnp.where(visible[None], scores, NEG).reshape(2 * rows, n * rows)
            peak = jnp.max(scores, -1, keepdims=True)
            weights = jnp.exp2((scores - peak) * (scale * LOG2E))
            prob = weights * (1.0 / jnp.sum(weights, -1, keepdims=True))
            mixes = [
                mix_ref[:, (first + i) * HEAD_SIZE : (first + i + 1) * HEAD_SIZE] for i in range(2)
            ]
            mixes = jnp.concatenate(mixes, 0).astype(F32)
            delta = jnp.sum(ms[rs, :].astype(F32) * mixes, -1, keepdims=True)
            score_half[rs, :] = (prob * (nt(ms[rs, :], vs[...]) - delta)).astype(BF16)
            prob_half[rs, :] = prob.astype(BF16)
        query_grad = nn(score_half[...], ks[...]) * scale
        for head in range(heads):
            at = slice(head * HEAD_SIZE, (head + 1) * HEAD_SIZE)
            dq_ref[:, at] = query_grad[head * rows : (head + 1) * rows].astype(BF16)
        key_sum = (tn(score_half[...], qs[...]) * scale).astype(BF16)
        value_sum = tn(prob_half[...], ms[...]).astype(BF16)
        for j in range(n):
            rs = slice(j * rows, (j + 1) * rows)
            outs[j][:rows, :HEAD_SIZE] = key_sum[rs]
            outs[j][:rows, HEAD_SIZE:] = value_sum[rs]
            outs[j][rows:, :] = gain_ref[...]

    stacked = ((heads * rows, HEAD_SIZE), BF16)
    halves = ((heads * rows, n * rows), BF16)
    return run_kernel(
        body,
        "attend_backward",
        place,
        [*grad_parts, query, pairs, mix, gain],
        [((rows, width), BF16)] + [((rows + 16, 2 * HEAD_SIZE), BF16)] * n,
        [stacked, stacked, halves, halves],
        flops=10 * rows * width * n * rows,
    )


def proj_grad(place, mix_all, keep, near):
    total, width = mix_all.shape
    rows, cols = total // 4, keep.shape[1]

    def body(place_ref, mix_ref, keep_ref, near_ref, out_ref, grads):
        c = place_ref[0]
        for d in range(4):
            ref = near_ref if d % 2 else keep_ref
            at = pl.multiple_of((c ^ d) * rows, rows)
            grads[pl.ds(at, rows), :] = ref[d // 2 * rows : (d // 2 + 1) * rows, :]
        out_ref[...] = tn(mix_ref[...], grads[...]).astype(BF16)

    return run_kernel(
        body,
        "proj_grad",
        place,
        [mix_all, keep, near],
        [((width, cols), BF16)],
        [((total, cols), BF16)],
        flops=2 * total * cols * width,
    )[0]


def pair_sums(place, parts):
    n = len(parts)
    rows = parts[0].shape[0] - 16
    half = parts[0].shape[1]

    def body(place_ref, *refs):
        key_ref, value_ref, gain_ref = refs[n:]
        c = place_ref[0]
        total = sum([r[:rows, :].astype(F32) for r in refs[1:n]], refs[0][:rows, :].astype(F32))
        key_ref[...] = total[:, :HEAD_SIZE].astype(BF16)
        value_ref[...] = total[:, HEAD_SIZE:].astype(BF16)
        gain_ref[...] = jnp.zeros(gain_ref.shape, F32)
        for j in range(n):
            tail = refs[j][rows : rows + 8, :].astype(F32)
            for i in range(4):
                at = pl.multiple_of(((c ^ j ^ (i // 2)) * 2 + i % 2) * half, half)
                gain_ref[:, pl.ds(at, half)] += tail[i : i + 1] + tail[i + 4 : i + 5]

    return run_kernel(
        body,
        "pair_sums",
        place,
        parts,
        [((rows, HEAD_SIZE), BF16), ((rows, HEAD_SIZE), BF16), ((1, 2 * n * half), F32)],
    )


def local_dense(
    resid,
    query,
    key,
    value,
    out_proj,
    norm_gain,
    w_gate,
    w_up,
    w_down,
    routes,
    gate_weights,
    grad_out,
):
    n = lax.axis_size("ctx")
    c, e, g = lax.axis_index("ctx"), lax.axis_index("exp"), lax.axis_index("groups")
    place = jnp.stack([c, e, g]).astype(jnp.int32)
    tok, width = resid.shape
    cols = out_proj.shape[1]
    scope = jax.named_scope

    def across(blocks):
        return [blocks[0]] + [crossed(blocks[r], r) for r in range(1, n)]

    with scope("gather_rows"):
        to_far, to_near, to_third = pack_rows(place, grad_out, routes, gate_weights, resid, cols)
    with scope("gather_heads"):
        heads = jnp.concatenate([key, value, query], 1)
        far, near = crossed(heads, 2), crossed(heads, 1)
        row_third = crossed(to_third, 3)
        parts = [heads, near, far, crossed(after(far, near, to_far, to_near, row_third), 1)]

    with scope("gather_rows"):
        to_far, to_near = lax.optimization_barrier((to_far, to_near, parts[3]))[:2]
        row_far, row_near = crossed(to_far, 2), crossed(to_near, 1)

    mix_all, mix, keep, send, pairs = attend(place, parts, out_proj)
    with scope("sum_heads"):
        received = swapped(send, 1)
        line = swapped(add(keep[1], received[1]), 2)
    hidden_block = hidden_rows(
        place, keep, received, line, resid, row_near, row_far, row_third
    )
    with scope("gather_rows"):
        size = width + 128
        rest = crossed(after(row_far[:, :size], line), 1)
        to_far, row_far, row_near = lax.optimization_barrier((to_far, row_far, row_near, hidden_block))[:3]
        grad_own = jnp.stack([to_far[:, :size], row_near[:, :size], row_far[:, :size]])
        grad_own, grad_line = [grad_own, rest], [swapped(grad_own, 2), swapped(rest, 2)]
        grad_sets = [grad_own, grad_line] + [
            [swapped(x, 1) for x in xs] for xs in (grad_own, grad_line)
        ]
    grad_rows, gate, act_grad = grad_rows_of(place, grad_sets, w_down[0])

    with scope("gather_hidden"):
        far, near = crossed(hidden_block, 2), crossed(hidden_block, 1)
        line = swapped(hidden_block, 2)
        hidden_own = [hidden_block, near, far, crossed(after(far, near), 1)]
        hidden_line = [line] + [swapped(after(x, line), 2) for x in hidden_own[1:3]]
        hidden_line.append(swapped(after(hidden_own[3], *hidden_line), 2))
    with scope("gather_proj"):
        half = out_proj.shape[0] // 2
        proj_half = lax.dynamic_slice_in_dim(out_proj, g * half, half, 0)
        proj_here = crossed(after(proj_half, hidden_own[3]), 1)
    with scope("gather_hidden"):
        hidden_line[-1], act_grad, proj_here = lax.optimization_barrier(
            (hidden_line[-1], act_grad, proj_here)
        )
        hidden_sets = [hidden_own, hidden_line] + [
            [swapped(x, 1) for x in xs] for xs in (hidden_own, hidden_line)
        ]

    with scope("gather_proj"):
        proj_there = lax.ppermute(proj_here, "groups", [(0, 1), (1, 0)])

    normed, act_rows, gate_grad, up_grad, hidden, *row_grads = expert_rows(
        place, hidden_sets, act_grad, norm_gain, w_gate[0], w_up[0]
    )
    out_keep, out_send = weighted_rows(place, act_rows, gate, w_down[0], n)
    with scope("sum_row_grads"):
        wide, narrow = sum_rows(row_grads[:4], *row_grads[4:], out_keep, proj_there)

    with scope("sum_outputs"):
        out_sent = swapped(out_send, 1)
        out_line = swapped(after(add(out_keep[1], out_sent[1]), wide[0]), 2)
    grad_w_down = tn(after(act_rows, wide[0]), grad_rows).astype(BF16)
    grad_resid, *cuts = norm_backward(
        place, wide, narrow, after(hidden, out_line, grad_w_down), grad_out, norm_gain, cols
    )

    with scope("gather_cuts"):
        cut_own = jnp.stack([cuts[0], crossed(cuts[1], 2)])
        cut_line = swapped(cut_own, 2)
        cut_sets = [cut_own, swapped(cut_own, 1), cut_line, swapped(cut_line, 1)]
    mix_own, mix_far, cut_keep, cut_send, gain_rows = mix_grad_parts(
        place, cut_sets, out_proj, proj_here, proj_there
    )
    with scope("sum_mix_grad"):
        mix_grads = [mix_own, crossed(mix_far, 2)]
    with scope("gather_cuts"):
        cut_near = crossed(cut_send, 1)

    with scope("sum_outputs"):
        out_sums = [add(out_keep[0][j], out_sent[0][j], out_line[j]) for j in range(n)]
        out_sums = [after(x, cut_own) for x in out_sums]
        second = add(out_sums[2], crossed(out_sums[3], 1))
        out_sums = [out_sums[0], crossed(out_sums[1], 1), crossed(second, 2)]
    normed, act_rows = lax.optimization_barrier((normed, act_rows, mix_own))[:2]
    grad_w_gate = tn(normed, gate_grad).astype(BF16)
    grad_w_up = tn(normed, up_grad).astype(BF16)
    grad_out_proj = proj_grad(place, mix_all, cut_keep, cut_near)
    mix_grads[0] = after(mix_own, grad_w_gate, grad_w_up, *out_sums[1:])

    grad_query, *pair_parts = attend_backward(place, mix_grads, query, pairs, mix, gain_rows)
    with scope("sum_pairs"):
        key_gradient, value_gradient, grad_gain = pair_sums(place, across(pair_parts))
    layer_out = layer_rows(place, out_sums, after(hidden, grad_query))

    return (
        layer_out,
        grad_resid,
        grad_query,
        key_gradient,
        value_gradient,
        grad_out_proj,
        grad_gain.reshape(width),
        grad_w_gate[None],
        grad_w_up[None],
        grad_w_down[None],
    )


def local(*args):
    key, w_gate, routes = args[2], args[6], args[9]
    ctx_count, exp_count = lax.axis_size("ctx"), lax.axis_size("exp")
    expert_total = w_gate.shape[0] * ctx_count * exp_count
    dense = (
        2 * routes.shape[1] >= expert_total
        and w_gate.shape[0] == 1
        and key.shape[1] == HEAD_SIZE
        and exp_count == 4
        and ctx_count == 4
        and lax.axis_size("groups") == 2
    )
    return (local_dense if dense else local_routed)(*args)


def solution(mesh):
    in_specs = (
        P(("groups", "ctx", "exp"), None),
        P(("groups", "ctx"), "exp"),
        P(("groups", "ctx"), "exp"),
        P(("groups", "ctx"), "exp"),
        P("exp", "ctx"),
        P(),
        P(("ctx", "exp"), None, None),
        P(("ctx", "exp"), None, None),
        P(("ctx", "exp"), None, None),
        P(("groups", "ctx", "exp"), None),
        P(("groups", "ctx", "exp"), None),
        P(("groups", "ctx", "exp"), None),
    )
    out_specs = (
        P(("groups", "ctx", "exp"), None),
        P(("groups", "ctx", "exp"), None),
        P(("groups", "ctx"), "exp"),
        P(("groups", "ctx"), "exp"),
        P(("groups", "ctx"), "exp"),
        P(("groups", "exp"), "ctx"),
        P("groups"),
        P(("groups", "ctx", "exp"), None, None),
        P(("groups", "ctx", "exp"), None, None),
        P(("groups", "ctx", "exp"), None, None),
    )
    return jax.shard_map(local, mesh=mesh, in_specs=in_specs, out_specs=out_specs, check_vma=False)
```
